32 devices in a mesh: groups: 2 (over x), tp: 16 (over z, y, core).
Axes of the slice: x: 2, y: 2, z: 4, core: 2. Of those that a mesh axis runs over, the one named last changes fastest.
Arguments:
- query_rows: bfloat16 [2048, 16384], P(('groups', 'tp')), parts along dimension 0, may hold values from -96 to 96
- key_rows: bfloat16 [2048, 1024], P(('groups', 'tp')), parts along dimension 0, may hold values from -4.5 to 4.5
- value_rows: bfloat16 [2048, 1024], P(('groups', 'tp')), parts along dimension 0, may hold values from -6 to 6
Outputs:
- attended: bfloat16 [2048, 16384], P(('groups', 'tp')), parts along dimension 0
The draws below stay inside these ranges and needn't reach their ends.
There are 2 independent parts, one for each index of `groups`. The reference program is written for one: setup_inputs(seed, part) draws one part's arguments, and reference() takes and returns one part's arrays. A program takes and returns all parts, laid end to end along the dimension named above; each array names one. Nothing has to cross between parts.
All inputs are finite; a program needn't handle non-finite values.
Results may differ from the reference program's by a relative error of at most 0.0044.
Values may be sent and summed in bfloat16 or wider, within the bound.
No kernel may reach another device: no remote copies, remote signals or barrier semaphores. Data moves between devices by JAX's collectives and lax.ppermute only.
A program may use at most 128 MiB of HBM per device.

```python
import jax
import jax.numpy as jnp
from jax import lax

HEADS = 128
KV_HEADS = 8
HEAD_DIM = 128
TOK_DEV = 64
SEQ = 1024


def shared_keys(key):
    return jnp.clip(jax.random.normal(key, (SEQ, KV_HEADS, HEAD_DIM), jnp.float32), -4.5, 4.5)


def draw_key_rows(key, part):
    base = shared_keys(key)
    return base.reshape(SEQ, KV_HEADS * HEAD_DIM).astype(jnp.bfloat16)


def draw_query_rows(key, part):
    key = jax.random.fold_in(key, 2)
    fresh = jnp.clip(jax.random.normal(key, (SEQ, HEADS, HEAD_DIM), jnp.float32), -6.0, 6.0)
    return fresh.reshape(SEQ, HEADS * HEAD_DIM).astype(jnp.bfloat16)


def shard_levels(own_key, shape, shards, least, high):
    loudness, own = 1.0, jax.random.fold_in(own_key, 6)
    for axis_at, parts in shards:
        draws = jnp.exp(jax.random.uniform(jax.random.fold_in(own, axis_at), (parts,), jnp.float32, least / len(shards), high / len(shards)))
        loudness = loudness * jnp.repeat(draws, shape[axis_at] // parts).reshape([-1 if axis == axis_at else 1 for axis in range(len(shape))])
    return loudness


def scatter_about(stream_key, extent, width, reach, pieces=(), kind=jnp.bfloat16):
    loudness = shard_levels(stream_key, extent, pieces, -0.22, 0.18) if pieces else 1.0
    entries = jax.random.normal(stream_key, extent, jnp.float32) * width * loudness
    return jnp.minimum(jnp.maximum(entries, -reach), reach).astype(kind)


def setup_inputs(seed: int = 0, part: int = 0) -> dict:
    splits = jax.random.split(jax.random.key(seed), 4)
    own_keys = jax.random.split(jax.random.fold_in(splits[3], part), 4)
    query_rows = draw_query_rows(jax.random.fold_in(jax.random.fold_in(splits[3], part), 71), part)
    key_rows = draw_key_rows(jax.random.fold_in(jax.random.fold_in(splits[3], part), 71), part)
    value_rows = scatter_about(own_keys[2], (SEQ, KV_HEADS * HEAD_DIM), 1.0, 6.0, ((0, 16),))
    return {"query_rows": query_rows, "key_rows": key_rows, "value_rows": value_rows}


masked_score = -1.0e30


def reference(query_rows, key_rows, value_rows):
    seq_len = query_rows.shape[0]
    group = HEADS // KV_HEADS
    scaling = HEAD_DIM ** -0.5
    block_len = TOK_DEV
    block_count = seq_len // block_len
    grouped = query_rows.reshape(seq_len, KV_HEADS, group, HEAD_DIM)
    key_heads = key_rows.reshape(seq_len, KV_HEADS, HEAD_DIM).astype(jnp.float32)
    value_heads = value_rows.reshape(seq_len, KV_HEADS, HEAD_DIM).astype(jnp.float32)
    key_pos = jnp.arange(seq_len, dtype=jnp.int32)

    def one_block(block_index):
        start = (block_index * block_len).astype(jnp.int32)
        block_q = lax.dynamic_slice_in_dim(grouped, start, block_len, 0).astype(jnp.float32)
        scores = jnp.einsum("tgqd,ngd->tgqn", block_q, key_heads, precision=lax.Precision.HIGHEST) * scaling
        query_pos = start + jnp.arange(block_len, dtype=jnp.int32)
        allowed = (key_pos[None, :] <= query_pos[:, None])[:, None, None, :]
        scores = jnp.where(allowed, scores, masked_score)
        row_peak = jnp.max(scores, axis=-1, keepdims=True)
        weights = jnp.where(allowed, jnp.exp(scores - row_peak), 0.0)
        denominator = jnp.sum(weights, axis=-1)
        rounded = lax.optimization_barrier(weights.astype(jnp.bfloat16)).astype(jnp.float32)
        numerator = jnp.einsum("tgqn,ngd->tgqd", rounded, value_heads, precision=lax.Precision.HIGHEST)
        return (numerator / denominator[..., None]).astype(jnp.bfloat16)

    blocks = lax.map(one_block, jnp.arange(block_count, dtype=jnp.int32))
    return blocks.reshape(seq_len, HEADS * HEAD_DIM)
```

```python
import functools
import math

import jax
import jax.numpy as jnp
from jax import lax
from jax.experimental import pallas as pl
from jax.experimental.pallas import tpu as pltpu
from jax.sharding import PartitionSpec as P

HEADS = 128
KV_HEADS = 8
GROUP = HEADS // KV_HEADS

masked_score = -1e30


def chip_grid(devices):
    if devices % 2:
        return devices, 1, 1
    chips = devices // 2
    if chips % 2 or chips > 8:
        return chips, 1, 2
    return chips // 2, 2, 2


def collect(own, grid):
    depth, width, cores = grid

    def index(z, y, c):
        return (z * width + y) * cores + c

    def move(block, pairs):
        return lax.ppermute(block, "tp", pairs)

    places = [(y, c) for y in range(width) for c in range(cores)]
    blocks = {(0, 0, 0): own}
    for dz in range(1, depth):
        blocks[dz, 0, 0] = move(
            blocks[dz - 1, 0, 0],
            [(index(z - 1, y, c), index(z, y, c)) for z in range(dz, depth) for y, c in places],
        )
    if width == 2:
        for dz in range(depth):
            blocks[dz, 1, 0] = move(
                blocks[dz, 0, 0],
                [
                    (index(z, y, c), index(z, 1 - y, c))
                    for z in range(dz, depth)
                    for y, c in places
                    if dz or y == 0
                ],
            )
    if cores == 2:
        for dz in range(depth):
            for dy in range(width):
                blocks[dz, dy, 1] = move(
                    blocks[dz, dy, 0],
                    [
                        (index(z, y, c), index(z, y, 1 - c))
                        for z in range(dz, depth)
                        for y, c in places
                        if dz or (dy and y == 1) or (not dy and c == 0)
                    ],
                )
    return blocks


def attend_kernel(keys, grid, order, chunk, *refs):
    depth, width, cores = grid
    count = len(order)
    query_ref = refs[0]
    block_refs = refs[1 : 1 + count]
    out_ref, held, sems, total, peak = refs[1 + count :]
    tok = query_ref.shape[0]
    dim = held.shape[1] // (2 * KV_HEADS)
    rows = GROUP * tok
    head = pl.program_id(0)
    me = lax.axis_index("tp")
    zz, yy, cc = me // (width * cores), (me // cores) % width, me % cores

    @pl.when(head == 0)
    def _():
        copies = []
        for place, (dz, dy, dc) in enumerate(order):
            source_z = jnp.where(zz >= dz, zz - dz, zz - dz + depth)
            source_y = jnp.where(yy >= dy, yy - dy, yy - dy + width)
            source_c = jnp.where(cc >= dc, cc - dc, cc - dc + cores)
            source = (source_z * width + source_y) * cores + source_c
            start = pl.multiple_of(source * tok, tok)
            copies.append(
                pltpu.make_async_copy(
                    block_refs[place], held.at[pl.ds(start, tok)], sems.at[place]
                )
            )
        for copy in copies:
            copy.start()
        for copy in copies:
            copy.wait()

    query = jnp.concatenate([query_ref[:, q * dim : (q + 1) * dim] for q in range(GROUP)], axis=0)
    factor = dim ** (-0.5) * math.log2(math.e)
    key_column = pl.ds(pl.multiple_of(head * dim, dim), dim)
    value_column = pl.ds(pl.multiple_of((KV_HEADS + head) * dim, dim), dim)
    ones = jnp.where(lax.broadcasted_iota(jnp.int32, (chunk, dim), 1) == 0, 1.0, 0.0).astype(
        jnp.bfloat16
    )
    parts = 4
    part_rows = rows // parts

    def absorb(start, first, allowed):
        span = pl.ds(pl.multiple_of(start, chunk), chunk)
        key_block = held[span, key_column]
        value_block = jnp.concatenate([held[span, value_column], ones], axis=1)
        for part in range(parts):
            here = slice(part * part_rows, (part + 1) * part_rows)
            scores = lax.dot_general(
                query[here],
                key_block,
                (((1,), (1,)), ((), ())),
                preferred_element_type=jnp.float32,
            )
            if allowed is not None:
                scores = jnp.where(allowed, scores, masked_score)
            top = jnp.max(scores, axis=1, keepdims=True)
            if not first:
                before = peak[here]
                top = jnp.maximum(before, top)
            weights = jnp.exp2((scores - top) * factor).astype(jnp.bfloat16)
            fresh = jnp.dot(weights, value_block, preferred_element_type=jnp.float32)
            if not first:
                fresh = total[here] * jnp.exp2((before - top) * factor) + fresh
            total[here] = fresh
            peak[here] = top

    first_pos = me * tok
    full = first_pos // chunk
    start = full * chunk
    row = lax.broadcasted_iota(jnp.int32, (part_rows, chunk), 0)
    column = lax.broadcasted_iota(jnp.int32, (part_rows, chunk), 1)
    allowed = column + start <= first_pos + row % tok
    absorb(start, True, allowed)

    @pl.loop(0, full)
    def _(block):
        absorb(block * chunk, False, None)

    for q in range(GROUP):
        here = slice(q * tok, (q + 1) * tok)
        out_ref[:, q * dim : (q + 1) * dim] = (
            total[here, :dim] / total[here, dim : dim + 1]
        ).astype(out_ref.dtype)


def attend(query_rows, blocks, grid):
    tok, width = query_rows.shape
    order = sorted(blocks)
    keys = tok * len(order)
    packed = blocks[order[0]].shape[1]
    dim = packed // (2 * KV_HEADS)
    chunk = math.gcd(keys, 512)
    columns = width // KV_HEADS
    return pl.pallas_call(
        functools.partial(attend_kernel, keys, grid, order, chunk),
        out_shape=jax.ShapeDtypeStruct(query_rows.shape, query_rows.dtype),
        grid=(KV_HEADS,),
        in_specs=[pl.BlockSpec((tok, columns), lambda head: (0, head))]
        + [pl.BlockSpec(memory_space=pl.ANY)] * len(order),
        out_specs=pl.BlockSpec((tok, columns), lambda head: (0, head)),
        scratch_shapes=[
            pltpu.VMEM((keys, packed), jnp.bfloat16),
            pltpu.SemaphoreType.DMA((len(order),)),
            pltpu.VMEM((GROUP * tok, 2 * dim), jnp.float32),
            pltpu.VMEM((GROUP * tok, 1), jnp.float32),
        ],
        compiler_params=pltpu.CompilerParams(vmem_limit_bytes=48 * 2**20),
        name="attend",
    )(query_rows, *[blocks[place] for place in order])


def solution(mesh):
    grid = chip_grid(mesh.shape["tp"])

    def body(query_rows, key_rows, value_rows):
        own = jnp.concatenate([key_rows, value_rows], axis=1)
        return attend(query_rows, collect(own, grid), grid)

    spec = P(("groups", "tp"), None)
    return jax.shard_map(
        body, mesh=mesh, in_specs=(spec, spec, spec), out_specs=spec, check_vma=False
    )
```

```python
import functools
import math

import jax
import jax.numpy as jnp
from jax import lax
from jax.experimental import pallas as pl
from jax.experimental.pallas import tpu as pltpu
from jax.sharding import PartitionSpec as P

HEADS = 128
KV_HEADS = 8
GROUP = HEADS // KV_HEADS
PARTS = 4

masked_score = -1e30


def chip_grid(devices):
    if devices % 2:
        return devices, 1, 1
    chips = devices // 2
    if chips % 2 or chips > 8:
        return chips, 1, 2
    return chips // 2, 2, 2


def place(grid):
    depth, width, cores = grid
    me = lax.axis_index("tp")
    return me // (width * cores), (me // cores) % width, me % cores


def stack(arrays, name, source=pl.ANY):
    rows, columns = arrays[0].shape

    def kernel(*refs):
        sems = refs[-1]
        out_ref = refs[-2]
        copies = [
            pltpu.make_async_copy(ref, out_ref.at[at], sems.at[at])
            for at, ref in enumerate(refs[:-2])
        ]
        for copy in copies:
            copy.start()
        for copy in copies:
            copy.wait()

    count = len(arrays)
    return pl.pallas_call(
        kernel,
        out_shape=jax.ShapeDtypeStruct((count, rows, columns), arrays[0].dtype),
        in_specs=[pl.BlockSpec(memory_space=source)] * count,
        out_specs=pl.BlockSpec(memory_space=pl.ANY),
        scratch_shapes=[pltpu.SemaphoreType.DMA((count,))],
        name=name,
    )(*arrays)


def z_move(own, grid, dz):
    depth, width, cores = grid
    side = width * cores
    pairs = [(at - dz * side, at) for at in range(dz * side, depth * side)]
    return lax.ppermute(own, "tp", pairs)


def y_swap(block, grid, dz):
    depth, width, cores = grid
    pairs = []
    for at in range(dz * width * cores, depth * width * cores):
        y = (at // cores) % width
        other = at + (1 - 2 * y) * cores
        if dz or other > at:
            pairs.append((at, other))
    return lax.ppermute(block, "tp", pairs)


def core_swap(blocks, grid):
    depth, width, cores = grid
    pairs = [(at, at ^ 1) for at in range(depth * width * cores)]
    return lax.ppermute(blocks, "tp", pairs)


def queries_of(query_ref, dim):
    return jnp.concatenate([query_ref[:, q * dim : (q + 1) * dim] for q in range(GROUP)], axis=0)


def keys_of(block, tok):
    count, _, _, dim = block.shape
    return block[:, 0].reshape(count * tok, dim), block[:, 1].reshape(count * tok, dim)


def with_ones(values):
    ones = jnp.where(lax.broadcasted_iota(jnp.int32, values.shape, 1) == 0, 1.0, 0.0)
    return jnp.concatenate([values, ones.astype(values.dtype)], axis=1)


def absorb(query, keys, values, bias, state, emit):
    rows, dim = query.shape
    factor = dim ** (-0.5) * math.log2(math.e)
    part_rows = rows // PARTS
    value_block = with_ones(values)
    lane = lax.broadcasted_iota(jnp.int32, (part_rows, 2 * dim), 1)
    for part in range(PARTS):
        here = slice(part * part_rows, (part + 1) * part_rows)
        scores = lax.dot_general(
            query[here], keys, (((1,), (1,)), ((), ())), preferred_element_type=jnp.float32
        )
        if bias is not None:
            repeats = part_rows // bias.shape[0]
            scores = (
                scores.reshape(repeats, bias.shape[0], scores.shape[1]) + bias[None]
            ).reshape(scores.shape)
        top = jnp.max(scores, axis=1, keepdims=True)
        if state is not None:
            before = state[here, dim + 1 : dim + 2]
            top = jnp.maximum(before, top)
        weights = jnp.exp2((scores - top) * factor).astype(jnp.bfloat16)
        fresh = jnp.dot(weights, value_block, preferred_element_type=jnp.float32)
        if state is not None:
            fresh = state[here, :] * jnp.exp2((before - top) * factor) + fresh
        emit(part, here, fresh, top, lane)


def first_kernel(grid, near, far, query_ref, near_ref, near_core_ref, far_ref, far_core_ref, state_ref, bias_ref):
    tok = query_ref.shape[0]
    dim = near_ref.shape[-1]
    zz, yy, cc = place(grid)
    width = grid[1]
    near_count = near_ref.shape[0]

    @pl.when(pl.program_id(0) == 0)
    def _():
        row = lax.broadcasted_iota(jnp.int32, bias_ref.shape, 0)
        column = lax.broadcasted_iota(jnp.int32, bias_ref.shape, 1)
        block, key = column // tok, column % tok
        other_y, other_c = block % width, block // near_count
        after_y = jnp.where(yy == 1, 0, tok)
        after_c = jnp.where(cc == 1, 0, tok)
        from_row = jnp.where(other_y == 1, after_y, jnp.where(other_c == 1, after_c, key))
        bias_ref[...] = jnp.where(from_row <= row, 0.0, masked_score)

    query = queries_of(query_ref, dim)

    def emit(part, here, fresh, top, lane):
        state_ref[here, :] = jnp.where(lane == dim + 1, top, fresh)

    near_keys, near_values = keys_of(
        jnp.concatenate([near_ref[...], near_core_ref[...]], axis=0), tok
    )

    if far:

        @pl.when(zz >= far)
        def _():
            far_keys, far_values = keys_of(
                jnp.concatenate([far_ref[...], far_core_ref[...]], axis=0), tok
            )
            bias = jnp.concatenate(
                [bias_ref[...], jnp.zeros((tok, far_keys.shape[0]), jnp.float32)], axis=1
            )
            absorb(
                query,
                jnp.concatenate([near_keys, far_keys], axis=0),
                jnp.concatenate([near_values, far_values], axis=0),
                bias,
                None,
                emit,
            )

    @pl.when(zz < far if far else zz >= 0)
    def _():
        absorb(query, near_keys, near_values, bias_ref[...], None, emit)


def later_kernel(grid, rows_below, last, query_ref, blocks_ref, state_ref, out_ref):
    tok = query_ref.shape[0]
    dim = blocks_ref.shape[-1]
    zz, _, _ = place(grid)
    query = queries_of(query_ref, dim)
    keys, values = keys_of(blocks_ref[...], tok)

    def emit(part, here, fresh, top, lane):
        if not last:
            out_ref[here, :] = jnp.where(lane == dim + 1, top, fresh)
            return
        done = (fresh[:, :dim] / fresh[:, dim : dim + 1]).astype(out_ref.dtype)
        heads = done.shape[0] // tok
        for head in range(heads):
            at = (part * heads + head) * dim
            out_ref[:, at : at + dim] = done[head * tok : (head + 1) * tok]

    state = state_ref
    all_there = zz >= max(rows_below)

    @pl.when(all_there)
    def _():
        absorb(query, keys, values, None, state, emit)

    @pl.when(jnp.logical_not(all_there))
    def _():
        block = lax.broadcasted_iota(jnp.int32, (tok, keys.shape[0]), 1) // tok
        bias = jnp.zeros(block.shape, jnp.float32)
        for at, below in enumerate(rows_below):
            bias = jnp.where(block == at, jnp.where(zz < below, masked_score, 0.0), bias)
        absorb(query, keys, values, bias, state, emit)


def solution(mesh):
    grid = chip_grid(mesh.shape["tp"])
    depth, width, cores = grid
    assert cores == 2 and depth > 2

    def body(query_rows, key_rows, value_rows):
        tok, columns = query_rows.shape
        dim = key_rows.shape[1] // KV_HEADS
        rows = GROUP * tok
        query_rows, key_rows, value_rows = (
            pltpu.with_memory_space_constraint(array, pltpu.HBM)
            for array in (query_rows, key_rows, value_rows)
        )
        own = stack([key_rows, value_rows], "pack", pltpu.HBM)

        def block_pair(block, dz):
            return [block, y_swap(block, grid, dz)] if width == 2 else [block]

        below = [depth - 1] + list(range(1, depth - 1))[::-1]
        moved = {dz: z_move(own, grid, dz) for dz in below}
        near = block_pair(own, 0)
        far = block_pair(moved[depth - 1], depth - 1)
        middle, rows_below = [], []
        for dz in below[1:]:
            pair = block_pair(moved[dz], dz)
            middle += pair
            rows_below += [dz] * len(pair)

        def pile(blocks, name):
            flat = [block.reshape(2 * tok, -1) for block in blocks]
            return stack(flat, name).reshape(len(blocks), 2, tok, -1)

        near, far, moved = lax.optimization_barrier((near, far, moved))
        early = pile(near + far, "early")
        early_core = core_swap(early, grid)
        query_spec = pl.BlockSpec((tok, columns // KV_HEADS), lambda head: (0, head))
        state_spec = pl.BlockSpec((None, rows, 2 * dim), lambda head: (head, 0, 0))
        state_shape = jax.ShapeDtypeStruct((KV_HEADS, rows, 2 * dim), jnp.float32)

        def blocks_spec(count, at):
            return pl.BlockSpec((count, 2, tok, dim), lambda head: (at, 0, 0, head))

        def cost(keys):
            return pl.CostEstimate(
                flops=4 * HEADS * tok * keys * dim,
                bytes_accessed=4 * HEADS * tok * dim,
                transcendentals=HEADS * tok * keys,
            )

        params = pltpu.CompilerParams(vmem_limit_bytes=32 * 2**20)
        count = len(near)
        state = pl.pallas_call(
            functools.partial(first_kernel, grid, 0, depth - 1),
            out_shape=state_shape,
            grid=(KV_HEADS,),
            in_specs=[
                query_spec,
                blocks_spec(count, 0),
                blocks_spec(count, 0),
                blocks_spec(count, 1),
                blocks_spec(count, 1),
            ],
            out_specs=state_spec,
            scratch_shapes=[pltpu.VMEM((tok, 2 * count * tok), jnp.float32)],
            compiler_params=params,
            cost_estimate=cost(4 * count * tok),
            name="attend_first",
        )(query_rows, early, early_core, early, early_core)
        middle, state = lax.optimization_barrier((middle, state))
        late = pile(middle, "late")
        late_core = core_swap(late, grid)
        for blocks, last in ((late, False), (late_core, True)):
            state = pl.pallas_call(
                functools.partial(later_kernel, grid, tuple(rows_below), last),
                out_shape=query_rows if last else state_shape,
                grid=(KV_HEADS,),
                in_specs=[query_spec, blocks_spec(len(middle), 0), state_spec],
                out_specs=query_spec if last else state_spec,
                compiler_params=params,
                cost_estimate=cost(len(middle) * tok),
                name="attend_last" if last else "attend_middle",
            )(query_rows, blocks, state)
        return state

    spec = P(("groups", "tp"), None)
    return jax.shard_map(
        body, mesh=mesh, in_specs=(spec, spec, spec), out_specs=spec, check_vma=False
    )
```

```python
import functools
import math

import jax
import jax.numpy as jnp
from jax import lax
from jax.experimental import pallas as pl
from jax.experimental.pallas import tpu as pltpu
from jax.sharding import PartitionSpec as P

HEADS = 128
KV_HEADS = 8
GROUP = HEADS // KV_HEADS
PARTS = 4

masked_score = -1e30


def chip_grid(devices):
    if devices % 2:
        return devices, 1, 1
    chips = devices // 2
    if chips % 2 or chips > 8:
        return chips, 1, 2
    return chips // 2, 2, 2


def place(grid):
    depth, width, cores = grid
    me = lax.axis_index("tp")
    return me // (width * cores), (me // cores) % width, me % cores


def stack(arrays, name):
    def kernel(*refs):
        for at, ref in enumerate(refs[:-1]):
            refs[-1][at] = ref[...]

    count = len(arrays)
    return pl.pallas_call(
        kernel,
        out_shape=jax.ShapeDtypeStruct((count, *arrays[0].shape), arrays[0].dtype),
        in_specs=[pl.BlockSpec(memory_space=pltpu.VMEM)] * count,
        out_specs=pl.BlockSpec(memory_space=pltpu.VMEM),
        compiler_params=pltpu.CompilerParams(vmem_limit_bytes=32 * 2**20),
        name=name,
    )(*arrays)


def z_forward(block, grid, dz):
    depth, width, cores = grid
    side = width * cores
    pairs = [(at - side, at) for at in range(dz * side, depth * side)]
    return lax.ppermute(block, "tp", pairs)


def y_swap(block, grid, dz):
    depth, width, cores = grid
    pairs = []
    for at in range(dz * width * cores, depth * width * cores):
        y = (at // cores) % width
        other = at + (1 - 2 * y) * cores
        if dz or other > at:
            pairs.append((at, other))
    return lax.ppermute(block, "tp", pairs)


def core_swap(blocks, grid, dz):
    depth, width, cores = grid
    pairs = [(at, at ^ 1) for at in range(dz * width * cores, depth * width * cores)]
    return lax.ppermute(blocks, "tp", pairs)


def keys_of(blocks):
    count, _, tok, dim = blocks.shape
    return blocks[:, 0].reshape(count * tok, dim), blocks[:, 1].reshape(count * tok, dim)


def attend_kernel(grid, groups, query_ref, *refs):
    depth, width, cores = grid
    out_ref, bias_ref = refs[-2:]
    blocks_refs = refs[:-2]
    tok = query_ref.shape[0]
    dim = blocks_refs[0].shape[-1]
    rows = GROUP * tok
    factor = dim ** (-0.5) * math.log2(math.e)
    zz, yy, cc = place(grid)

    pieces, origin = [], []
    for (below, own_ref, core_ref) in zip(groups, blocks_refs[::2], blocks_refs[1::2]):
        for dc, ref in ((0, own_ref), (1, core_ref)):
            for at, dz in enumerate(below):
                pieces.append((dz, dc, below[:at].count(dz), ref, at))
    pieces.sort(key=lambda piece: piece[:3])
    near = width * cores * tok

    @pl.when(pl.program_id(0) == 0)
    def _():
        row = lax.broadcasted_iota(jnp.int32, (tok, tok), 0)
        key = lax.broadcasted_iota(jnp.int32, (tok, tok), 1)
        for at, (dz, dc, dy, _, _) in enumerate(pieces):
            if dz:
                limit = jnp.where(zz >= dz, 0, tok) + 0 * key
            elif dy:
                limit = jnp.where(yy == 1, 0, tok) + 0 * key
            elif dc:
                limit = jnp.where(cc == 1, 0, tok) + 0 * key
            else:
                limit = key
            bias_ref[:, at * tok : (at + 1) * tok] = jnp.where(limit <= row, 0.0, masked_score)

    def attend(bias):
        query = jnp.concatenate(
            [query_ref[:, q * dim : (q + 1) * dim] for q in range(GROUP)], axis=0
        )
        keys = jnp.concatenate([ref[at, 0] for _, _, _, ref, at in pieces], axis=0)
        values = jnp.concatenate([ref[at, 1] for _, _, _, ref, at in pieces], axis=0)
        ones = jnp.where(lax.broadcasted_iota(jnp.int32, values.shape, 1) == 0, 1.0, 0.0)
        values = jnp.concatenate([values, ones.astype(values.dtype)], axis=1)
        part_rows = rows // PARTS
        heads = part_rows // tok
        for part in range(PARTS):
            scores = lax.dot_general(
                query[part * part_rows : (part + 1) * part_rows],
                keys,
                (((1,), (1,)), ((), ())),
                preferred_element_type=jnp.float32,
            )
            span = bias.shape[1]
            first = scores[:, :span].reshape(heads, tok, span) + bias[None]
            first = first.reshape(part_rows, span)
            if span < scores.shape[1]:
                first = jnp.concatenate([first, scores[:, span:]], axis=1)
            scores = first
            top = jnp.max(scores, axis=1, keepdims=True)
            weights = jnp.exp2((scores - top) * factor).astype(jnp.bfloat16)
            sums = jnp.dot(weights, values, preferred_element_type=jnp.float32)
            done = (sums[:, :dim] / sums[:, dim : dim + 1]).astype(out_ref.dtype)
            for head in range(heads):
                at = (part * heads + head) * dim
                out_ref[:, at : at + dim] = done[head * tok : (head + 1) * tok]

    @pl.when(zz == depth - 1)
    def _():
        attend(bias_ref[:, :near])

    @pl.when(zz < depth - 1)
    def _():
        attend(bias_ref[...])


def solution(mesh):
    grid = chip_grid(mesh.shape["tp"])
    depth, width, cores = grid
    assert cores == 2 and depth > 2

    def body(query_rows, key_rows, value_rows):
        tok, columns = query_rows.shape
        dim = key_rows.shape[1] // KV_HEADS
        query_rows, key_rows, value_rows = (
            pltpu.with_memory_space_constraint(array, pltpu.HBM)
            for array in (query_rows, key_rows, value_rows)
        )
        block = stack([key_rows, value_rows], "pack")

        def with_swap(block, dz):
            return [block, y_swap(block, grid, dz)] if width == 2 else [block]

        rows_of = []
        for dz in range(depth):
            rows_of.append(with_swap(block, dz))
            if dz + 1 < depth:
                block = z_forward(block, grid, dz + 1)
                block, rows_of[dz] = lax.optimization_barrier((block, rows_of[dz]))

        spans = [range(0, 2), range(2, depth - 1), range(depth - 1, depth)]
        groups, operands = [], []
        for span in spans:
            blocks = [block for dz in span for block in rows_of[dz]]
            if not blocks:
                continue
            groups.append([dz for dz in span for _ in rows_of[dz]])
            merged = stack(blocks, "merge")
            operands += [merged, core_swap(merged, grid, span[0])]

        query_spec = pl.BlockSpec((tok, columns // KV_HEADS), lambda head: (0, head))
        keys = tok * depth * width * cores
        return pl.pallas_call(
            functools.partial(attend_kernel, grid, groups),
            out_shape=query_rows,
            grid=(KV_HEADS,),
            in_specs=[query_spec]
            + [
                pl.BlockSpec((operand.shape[0], 2, tok, dim), lambda head: (0, 0, 0, head))
                for operand in operands
            ],
            out_specs=query_spec,
            scratch_shapes=[pltpu.VMEM((tok, keys), jnp.float32)],
            compiler_params=pltpu.CompilerParams(vmem_limit_bytes=32 * 2**20),
            cost_estimate=pl.CostEstimate(
                flops=4 * HEADS * tok * keys * dim,
                bytes_accessed=4 * HEADS * tok * dim,
                transcendentals=HEADS * tok * keys,
            ),
            name="attend",
        )(query_rows, *operands)

    spec = P(("groups", "tp"), None)
    return jax.shard_map(
        body, mesh=mesh, in_specs=(spec, spec, spec), out_specs=spec, check_vma=False
    )
```

```python
import functools
import math

import jax
import jax.numpy as jnp
from jax import lax
from jax.experimental import pallas as pl
from jax.experimental.pallas import tpu as pltpu
from jax.sharding import PartitionSpec as P

HEADS = 128
KV_HEADS = 8
GROUP = HEADS // KV_HEADS
PARTS = 4
CHUNKS = 2

masked_score = -1e30


def chip_grid(devices):
    if devices % 2:
        return devices, 1, 1
    chips = devices // 2
    if chips % 2 or chips > 8:
        return chips, 1, 2
    return chips // 2, 2, 2


def place(grid):
    depth, width, cores = grid
    me = lax.axis_index("tp")
    return me // (width * cores), (me // cores) % width, me % cores


def stack(arrays, name):
    def kernel(*refs):
        for at, ref in enumerate(refs[:-1]):
            refs[-1][at] = ref[...]

    count = len(arrays)
    return pl.pallas_call(
        kernel,
        out_shape=jax.ShapeDtypeStruct((count, *arrays[0].shape), arrays[0].dtype),
        in_specs=[pl.BlockSpec(memory_space=pltpu.VMEM)] * count,
        out_specs=pl.BlockSpec(memory_space=pltpu.VMEM),
        compiler_params=pltpu.CompilerParams(vmem_limit_bytes=32 * 2**20),
        name=name,
    )(*arrays)


def pack(key_rows, value_rows, chunks):
    tok, columns = key_rows.shape
    columns //= chunks

    def kernel(key_ref, value_ref, *out_refs):
        for chunk, out_ref in enumerate(out_refs):
            span = slice(chunk * columns, (chunk + 1) * columns)
            out_ref[0] = key_ref[:, span]
            out_ref[1] = value_ref[:, span]

    return pl.pallas_call(
        kernel,
        out_shape=[jax.ShapeDtypeStruct((2, tok, columns), key_rows.dtype)] * chunks,
        in_specs=[pl.BlockSpec(memory_space=pltpu.VMEM)] * 2,
        out_specs=[pl.BlockSpec(memory_space=pltpu.VMEM)] * chunks,
        name="pack",
    )(key_rows, value_rows)


def z_forward(block, grid):
    depth, width, cores = grid
    count = depth * width * cores
    return lax.ppermute(
        block, "tp", [(at, (at + width * cores) % count) for at in range(count)]
    )


def y_swap(block, grid):
    depth, width, cores = grid
    return lax.ppermute(
        block, "tp", [(at, at ^ cores) for at in range(depth * width * cores)]
    )


def core_swap(blocks, grid):
    depth, width, cores = grid
    return lax.ppermute(blocks, "tp", [(at, at ^ 1) for at in range(depth * width * cores)])


def keys_of(blocks):
    count, _, tok, dim = blocks.shape
    return blocks[:, 0].reshape(count * tok, dim), blocks[:, 1].reshape(count * tok, dim)


def attend_kernel(grid, groups, query_ref, *refs):
    depth, width, cores = grid
    out_ref, bias_ref = refs[-2:]
    blocks_refs = refs[: 2 * len(groups)]
    tok = query_ref.shape[0]
    dim = blocks_refs[0].shape[-1]
    rows = GROUP * tok
    factor = dim ** (-0.5) * math.log2(math.e)
    zz, yy, cc = place(grid)

    pieces, origin = [], []
    for (below, own_ref, core_ref) in zip(groups, blocks_refs[::2], blocks_refs[1::2]):
        for dc, ref in ((0, own_ref), (1, core_ref)):
            for at, dz in enumerate(below):
                pieces.append((dz, dc, below[:at].count(dz), ref, at))
    pieces.sort(key=lambda piece: piece[:3])
    near = width * cores * tok

    @pl.when(pl.program_id(0) == 0)
    def _():
        row = lax.broadcasted_iota(jnp.int32, (tok, tok), 0)
        key = lax.broadcasted_iota(jnp.int32, (tok, tok), 1)
        for at, (dz, dc, dy, _, _) in enumerate(pieces):
            if dz:
                limit = jnp.where(zz >= dz, 0, tok) + 0 * key
            elif dy:
                limit = jnp.where(yy == 1, 0, tok) + 0 * key
            elif dc:
                limit = jnp.where(cc == 1, 0, tok) + 0 * key
            else:
                limit = key
            bias_ref[:, at * tok : (at + 1) * tok] = jnp.where(limit <= row, 0.0, masked_score)

    def attend(bias):
        query = jnp.concatenate(
            [query_ref[:, q * dim : (q + 1) * dim] for q in range(GROUP)], axis=0
        )
        keys = jnp.concatenate([ref[at, 0] for _, _, _, ref, at in pieces], axis=0)
        values = jnp.concatenate([ref[at, 1] for _, _, _, ref, at in pieces], axis=0)
        ones = jnp.where(lax.broadcasted_iota(jnp.int32, values.shape, 1) == 0, 1.0, 0.0)
        values = jnp.concatenate([values, ones.astype(values.dtype)], axis=1)
        part_rows = rows // PARTS
        heads = part_rows // tok
        span = bias.shape[1]

        def scores_of(part):
            return lax.dot_general(
                query[part * part_rows : (part + 1) * part_rows],
                keys,
                (((1,), (1,)), ((), ())),
                preferred_element_type=jnp.float32,
            )

        following = scores_of(0)
        for part in range(PARTS):
            scores = following
            if part + 1 < PARTS:
                following = scores_of(part + 1)
            first = scores[:, :span].reshape(heads, tok, span) + bias[None]
            first = first.reshape(part_rows, span)
            if span < scores.shape[1]:
                first = jnp.concatenate([first, scores[:, span:]], axis=1)
            scores = first
            top = jnp.max(scores, axis=1, keepdims=True)
            weights = jnp.exp2((scores - top) * factor).astype(jnp.bfloat16)
            sums = jnp.dot(weights, values, preferred_element_type=jnp.float32)
            done = (sums[:, :dim] / sums[:, dim : dim + 1]).astype(out_ref.dtype)
            for head in range(heads):
                at = (part * heads + head) * dim
                out_ref[:, at : at + dim] = done[head * tok : (head + 1) * tok]

    @pl.when(zz == depth - 1)
    def _():
        attend(bias_ref[:, :near])

    @pl.when(zz < depth - 1)
    def _():
        attend(bias_ref[...])


def solution(mesh):
    grid = chip_grid(mesh.shape["tp"])
    depth, width, cores = grid
    assert cores == 2 and depth > 2

    def body(query_rows, key_rows, value_rows):
        tok, columns = query_rows.shape
        dim = key_rows.shape[1] // KV_HEADS
        query_rows, key_rows, value_rows = (
            pltpu.with_memory_space_constraint(array, pltpu.HBM)
            for array in (query_rows, key_rows, value_rows)
        )
        blocks = list(pack(key_rows, value_rows, CHUNKS))
        rows_of = [[] for _ in range(CHUNKS)]
        for dz in range(depth):
            for chunk in range(CHUNKS):
                block = blocks[chunk]
                row = [block, y_swap(block, grid)] if width == 2 else [block]
                if dz + 1 < depth:
                    following = z_forward(block, grid)
                    blocks[chunk], row = lax.optimization_barrier((following, row))
                rows_of[chunk].append(row)

        spans = [range(0, 2), range(2, depth - 1), range(depth - 1, depth)]
        spans = [span for span in spans if len(span)]
        groups = [[dz for dz in span for _ in range(width)] for span in spans]
        keys = tok * depth * width * cores
        heads = KV_HEADS // CHUNKS
        result = None
        for chunk in range(CHUNKS):
            operands = []
            for span in spans:
                merged = stack([block for dz in span for block in rows_of[chunk][dz]], "merge")
                operands += [merged, core_swap(merged, grid)]
            query_spec = pl.BlockSpec(
                (tok, columns // KV_HEADS), lambda head, chunk=chunk: (0, chunk * heads + head)
            )
            result = pl.pallas_call(
                functools.partial(attend_kernel, grid, groups),
                out_shape=query_rows,
                grid=(heads,),
                in_specs=[query_spec]
                + [
                    pl.BlockSpec((operand.shape[0], 2, tok, dim), lambda head: (0, 0, 0, head))
                    for operand in operands
                ]
                + [pl.BlockSpec(memory_space=pl.ANY)] * (chunk > 0),
                out_specs=query_spec,
                scratch_shapes=[pltpu.VMEM((tok, keys), jnp.float32)],
                input_output_aliases={1 + len(operands): 0} if chunk else {},
                compiler_params=pltpu.CompilerParams(vmem_limit_bytes=32 * 2**20),
                cost_estimate=pl.CostEstimate(
                    flops=4 * HEADS * tok * keys * dim // CHUNKS,
                    bytes_accessed=4 * HEADS * tok * dim // CHUNKS,
                    transcendentals=HEADS * tok * keys // CHUNKS,
                ),
                name="attend",
            )(query_rows, *operands, *([result] if chunk else []))
        return result

    spec = P(("groups", "tp"), None)
    return jax.shard_map(
        body, mesh=mesh, in_specs=(spec, spec, spec), out_specs=spec, check_vma=False
    )
```

```python
import functools
import math

import jax
import jax.numpy as jnp
from jax import lax
from jax.experimental import pallas as pl
from jax.experimental.pallas import tpu as pltpu
from jax.sharding import PartitionSpec as P

HEADS = 128
KV_HEADS = 8
GROUP = HEADS // KV_HEADS
PARTS = 4
STEP_HEADS = 2

masked_score = -1e30


def chip_grid(devices):
    if devices % 2:
        return devices, 1, 1
    chips = devices // 2
    if chips % 2 or chips > 8:
        return chips, 1, 2
    return chips // 2, 2, 2


def place(grid):
    depth, width, cores = grid
    me = lax.axis_index("tp")
    return me // (width * cores), (me // cores) % width, me % cores


def stack(arrays, name):
    def kernel(*refs):
        for at, ref in enumerate(refs[:-1]):
            refs[-1][at] = ref[...]

    count = len(arrays)
    return pl.pallas_call(
        kernel,
        out_shape=jax.ShapeDtypeStruct((count, *arrays[0].shape), arrays[0].dtype),
        in_specs=[pl.BlockSpec(memory_space=pltpu.VMEM)] * count,
        out_specs=pl.BlockSpec(memory_space=pltpu.VMEM),
        compiler_params=pltpu.CompilerParams(vmem_limit_bytes=32 * 2**20),
        name=name,
    )(*arrays)


def z_forward(block, grid):
    depth, width, cores = grid
    count = depth * width * cores
    return lax.ppermute(
        block, "tp", [(at, (at + width * cores) % count) for at in range(count)]
    )


def y_swap(block, grid):
    depth, width, cores = grid
    return lax.ppermute(
        block, "tp", [(at, at ^ cores) for at in range(depth * width * cores)]
    )


def core_swap(blocks, grid):
    depth, width, cores = grid
    return lax.ppermute(blocks, "tp", [(at, at ^ 1) for at in range(depth * width * cores)])


def reciprocal(x):
    guess = pl.reciprocal(x, approx=True)
    return guess * (2.0 - x * guess)


def attend_kernel(grid, groups, kept, last, query_ref, *refs):
    depth, width, cores = grid
    blocks_refs, refs = refs[: 2 * len(groups)], refs[2 * len(groups) :]
    kept_refs, refs = refs[: 2 * kept], refs[2 * kept :]
    out_refs, scratch = refs[: 2 - last], refs[2 - last :]
    tok = query_ref.shape[0]
    dim = blocks_refs[0].shape[-1] // STEP_HEADS
    rows = GROUP * tok
    part_rows = rows // PARTS
    heads = part_rows // tok
    factor = dim ** (-0.5) * math.log2(math.e)
    zz, yy, cc = place(grid)

    pieces = []
    for below, own_ref, core_ref in zip(groups, blocks_refs[::2], blocks_refs[1::2]):
        for dc, ref in ((0, own_ref), (1, core_ref)):
            for at, dz in enumerate(below):
                pieces.append((dz, dc, below[:at].count(dz), ref, at))
    pieces.sort(key=lambda piece: piece[:3])
    lowest, highest = pieces[0][0], pieces[-1][0]

    if scratch:
        bias_ref = scratch[0]

        @pl.when(pl.program_id(0) == 0)
        def _():
            row = lax.broadcasted_iota(jnp.int32, (tok, tok), 0)
            key = lax.broadcasted_iota(jnp.int32, (tok, tok), 1)
            for at, (dz, dc, dy, _, _) in enumerate(pieces):
                if dz:
                    limit = jnp.where(zz >= dz, 0, tok) + 0 * key
                elif dy:
                    limit = jnp.where(yy == 1, 0, tok) + 0 * key
                elif dc:
                    limit = jnp.where(cc == 1, 0, tok) + 0 * key
                else:
                    limit = key
                bias_ref[:, at * tok : (at + 1) * tok] = jnp.where(
                    limit <= row, 0.0, masked_score
                )

    def emit(head, part, result, level):
        here = slice(part * part_rows, (part + 1) * part_rows)
        if not last:
            out_refs[0][head, here, :] = result
            out_refs[1][head, here, :] = level()
            return
        result = result.astype(out_refs[0].dtype)
        for index in range(heads):
            at = ((head * PARTS + part) * heads + index) * dim
            out_refs[0][:, at : at + dim] = result[index * tok : (index + 1) * tok]

    def attend(used, span):
        for head in range(STEP_HEADS):
            column = slice(head * dim, (head + 1) * dim)
            keys = jnp.concatenate([ref[at, 0, :, column] for _, _, _, ref, at in used], axis=0)
            values = jnp.concatenate([ref[at, 1, :, column] for _, _, _, ref, at in used], axis=0)
            values = jnp.concatenate([values, jnp.ones_like(values)], axis=1)
            first_head = head * GROUP
            for part in range(PARTS):
                here = slice(part * part_rows, (part + 1) * part_rows)
                query = jnp.concatenate(
                    [
                        query_ref[:, at * dim : (at + 1) * dim]
                        for at in range(first_head + part * heads, first_head + (part + 1) * heads)
                    ],
                    axis=0,
                )
                scores = lax.dot_general(
                    query, keys, (((1,), (1,)), ((), ())), preferred_element_type=jnp.float32
                )
                if span:
                    first = scores[:, :span].reshape(heads, tok, span) + bias_ref[:, :span][None]
                    first = first.reshape(part_rows, span)
                    if span < scores.shape[1]:
                        first = jnp.concatenate([first, scores[:, span:]], axis=1)
                    scores = first
                peak = jnp.max(scores, axis=1, keepdims=True) * factor
                if kept:
                    before = kept_refs[1][head, here, :]
                    peak = jnp.maximum(jnp.broadcast_to(peak, before.shape), before)
                    shifted = jnp.concatenate(
                        [
                            scores[:, at : at + dim] * factor - peak
                            for at in range(0, scores.shape[1], dim)
                        ],
                        axis=1,
                    )
                else:
                    shifted = scores * factor - peak
                weights = jnp.exp2(shifted).astype(jnp.bfloat16)
                sums = jnp.dot(weights, values, preferred_element_type=jnp.float32)
                numerator, denominator = sums[:, :dim], sums[:, dim:]
                if kept:
                    carry = jnp.exp2(before - peak)
                    numerator = numerator + carry * kept_refs[0][head, here, :]
                    denominator = denominator + carry
                emit(
                    head,
                    part,
                    numerator * reciprocal(denominator),
                    lambda: peak + jnp.log2(denominator),
                )

    def hand_on():
        for head in range(STEP_HEADS):
            for part in range(PARTS):
                here = slice(part * part_rows, (part + 1) * part_rows)
                emit(head, part, kept_refs[0][head, here, :], lambda: kept_refs[1][head, here, :])

    near = width * cores * tok if lowest == 0 else 0
    levels = sorted(set(range(lowest, highest + 1)))
    if len(levels) > 4:
        levels = sorted({lowest + (len(levels) - 1) * part // 3 for part in range(4)})
    below = lowest - 1
    if kept and lowest > 0:

        @pl.when(zz < lowest)
        def _():
            hand_on()

    for level in levels:
        used = [piece for piece in pieces if piece[0] <= level]
        alone = level == below + 1
        span = near if alone else len(used) * tok
        reached = jnp.logical_and(zz > below, zz <= level)
        if level == levels[-1]:
            reached = zz > below

        @pl.when(reached)
        def _(used=used, span=span):
            attend(used, span)

        below = level


def solution(mesh):
    grid = chip_grid(mesh.shape["tp"])
    depth, width, cores = grid
    assert cores == 2 and depth > 2

    def body(query_rows, key_rows, value_rows):
        tok, columns = query_rows.shape
        dim = key_rows.shape[1] // KV_HEADS
        rows = GROUP * tok
        query_rows, key_rows, value_rows = (
            pltpu.with_memory_space_constraint(array, pltpu.HBM)
            for array in (query_rows, key_rows, value_rows)
        )
        block = stack([key_rows, value_rows], "pack")
        rows_of = []
        for dz in range(depth):
            row = [block, y_swap(block, grid)] if width == 2 else [block]
            if dz + 1 < depth:
                following = z_forward(block, grid)
                block, row = lax.optimization_barrier((following, row))
            rows_of.append(row)

        query_spec = pl.BlockSpec(
            (tok, STEP_HEADS * columns // KV_HEADS), lambda step: (0, step)
        )
        state_spec = pl.BlockSpec((STEP_HEADS, rows, dim), lambda step: (step, 0, 0))
        state_shape = pltpu.HBM((KV_HEADS, rows, dim), jnp.float32)

        def merge(span):
            merged = stack([block for dz in span for block in rows_of[dz]], "merge")
            return [merged, core_swap(merged, grid)]

        def phase(spans, operands, state, last):
            groups = [[dz for dz in span for _ in range(width)] for span in spans]
            count = sum(2 * len(group) for group in groups)
            keys = tok * count
            masked = spans[0][0] == 0 or spans[-1][-1] - spans[0][0] > 3
            return pl.pallas_call(
                functools.partial(attend_kernel, grid, groups, bool(state), last),
                out_shape=query_rows if last else [state_shape] * 2,
                grid=(KV_HEADS // STEP_HEADS,),
                in_specs=[query_spec]
                + [
                    pl.BlockSpec(
                        (operand.shape[0], 2, tok, STEP_HEADS * dim), lambda step: (0, 0, 0, step)
                    )
                    for operand in operands
                ]
                + [state_spec] * len(state),
                out_specs=query_spec if last else [state_spec] * 2,
                scratch_shapes=[pltpu.VMEM((tok, keys), jnp.float32)] if masked else [],
                compiler_params=pltpu.CompilerParams(vmem_limit_bytes=40 * 2**20),
                cost_estimate=pl.CostEstimate(
                    flops=4 * HEADS * tok * keys * dim,
                    bytes_accessed=4 * HEADS * tok * dim,
                    transcendentals=HEADS * tok * keys,
                ),
                name="attend_last" if last else "attend_first",
            )(query_rows, *operands, *state)

        early = [range(0, 2)]
        late = [range(2, depth - 1), range(depth - 1, depth)]
        late = [span for span in late if len(span)]
        operands = merge(early[0])
        operands, rows_of[-1][0] = lax.optimization_barrier((operands, rows_of[-1][0]))
        state = phase(early, operands, [], False)
        rows_of[-1], state = lax.optimization_barrier((rows_of[-1], state))
        state = [pltpu.with_memory_space_constraint(array, pltpu.HBM) for array in state]
        operands = [operand for span in late for operand in merge(span)]
        return phase(late, operands, list(state), True)

    spec = P(("groups", "tp"), None)
    return jax.shard_map(
        body, mesh=mesh, in_specs=(spec, spec, spec), out_specs=spec, check_vma=False
    )
```

```python
import functools
import math

import jax
import jax.numpy as jnp
from jax import lax
from jax.experimental import pallas as pl
from jax.experimental.pallas import tpu as pltpu
from jax.sharding import PartitionSpec as P

HEADS = 128
KV_HEADS = 8
GROUP = HEADS // KV_HEADS
PARTS = 4
STEP_HEADS = 2

masked_score = -1e30


def chip_grid(devices):
    if devices % 2:
        return devices, 1, 1
    chips = devices // 2
    if chips % 2 or chips > 8:
        return chips, 1, 2
    return chips // 2, 2, 2


def place(grid):
    depth, width, cores = grid
    me = lax.axis_index("tp")
    return me // (width * cores), (me // cores) % width, me % cores


def stack(arrays, name):
    def kernel(*refs):
        for at, ref in enumerate(refs[:-1]):
            refs[-1][at] = ref[...]

    count = len(arrays)
    return pl.pallas_call(
        kernel,
        out_shape=jax.ShapeDtypeStruct((count, *arrays[0].shape), arrays[0].dtype),
        in_specs=[pl.BlockSpec(memory_space=pltpu.VMEM)] * count,
        out_specs=pl.BlockSpec(memory_space=pltpu.VMEM),
        compiler_params=pltpu.CompilerParams(vmem_limit_bytes=32 * 2**20),
        name=name,
    )(*arrays)


def fetch(array):
    def kernel(array_ref, out_ref):
        out_ref[...] = array_ref[...]

    return pl.pallas_call(
        kernel,
        out_shape=jax.ShapeDtypeStruct(array.shape, array.dtype),
        in_specs=[pl.BlockSpec(memory_space=pltpu.VMEM)],
        out_specs=pl.BlockSpec(memory_space=pltpu.VMEM),
        name="fetch",
    )(array)


def z_forward(block, grid):
    depth, width, cores = grid
    count = depth * width * cores
    return lax.ppermute(
        block, "tp", [(at, (at + width * cores) % count) for at in range(count)]
    )


def y_swap(block, grid):
    depth, width, cores = grid
    return lax.ppermute(
        block, "tp", [(at, at ^ cores) for at in range(depth * width * cores)]
    )


def core_swap(blocks, grid):
    depth, width, cores = grid
    return lax.ppermute(blocks, "tp", [(at, at ^ 1) for at in range(depth * width * cores)])


def reciprocal(x):
    guess = pl.reciprocal(x, approx=True)
    return guess * (2.0 - x * guess)


def attend_kernel(grid, groups, kept, last, query_ref, *refs):
    depth, width, cores = grid
    blocks_refs, refs = refs[: 2 * len(groups)], refs[2 * len(groups) :]
    kept_refs, refs = refs[: 2 * kept], refs[2 * kept :]
    out_refs, scratch = list(refs[: 2 - last]), list(refs[2 - last :])
    if last:
        result_ref = out_refs[0]
        out_refs[0], sems = scratch.pop(0), scratch.pop(0)
    tok = query_ref.shape[0]
    dim = blocks_refs[0].shape[-1] // KV_HEADS
    rows = GROUP * tok
    part_rows = rows // PARTS
    heads = part_rows // tok
    factor = dim ** (-0.5) * math.log2(math.e)
    zz, yy, cc = place(grid)

    pieces = []
    for below, own_ref, core_ref in zip(groups, blocks_refs[::2], blocks_refs[1::2]):
        for dc, ref in ((0, own_ref), (1, core_ref)):
            for at, dz in enumerate(below):
                pieces.append((dz, dc, below[:at].count(dz), ref, at))
    pieces.sort(key=lambda piece: piece[:3])
    lowest, highest = pieces[0][0], pieces[-1][0]

    if scratch:
        bias_ref = scratch[0]

        row = lax.broadcasted_iota(jnp.int32, (tok, tok), 0)
        key = lax.broadcasted_iota(jnp.int32, (tok, tok), 1)
        for at, (dz, dc, dy, _, _) in enumerate(pieces):
            if dz:
                limit = jnp.where(zz >= dz, 0, tok) + 0 * key
            elif dy:
                limit = jnp.where(yy == 1, 0, tok) + 0 * key
            elif dc:
                limit = jnp.where(cc == 1, 0, tok) + 0 * key
            else:
                limit = key
            bias_ref[:, at * tok : (at + 1) * tok] = jnp.where(limit <= row, 0.0, masked_score)

    def column(index):
        return pl.ds(pl.multiple_of(index * dim, dim), dim)

    def emit(head, part, result, level):
        here = slice(part * part_rows, (part + 1) * part_rows)
        if not last:
            out_refs[0][head, here, :] = result
            out_refs[1][head, here, :] = level()
            return
        result = result.astype(out_refs[0].dtype)
        for index in range(heads):
            out_refs[0][:, column((head * PARTS + part) * heads + index)] = result[
                index * tok : (index + 1) * tok
            ]

    def attend(used, span):
        def one(head):
            span_of = column(head)
            keys = jnp.concatenate([ref[at, 0, :, span_of] for _, _, _, ref, at in used], axis=0)
            values = jnp.concatenate([ref[at, 1, :, span_of] for _, _, _, ref, at in used], axis=0)
            values = jnp.concatenate([values, jnp.ones_like(values)], axis=1)
            first_head = head * GROUP
            for part in range(PARTS):
                here = slice(part * part_rows, (part + 1) * part_rows)
                query = jnp.concatenate(
                    [
                        query_ref[:, column(first_head + index)]
                        for index in range(part * heads, (part + 1) * heads)
                    ],
                    axis=0,
                )
                scores = lax.dot_general(
                    query, keys, (((1,), (1,)), ((), ())), preferred_element_type=jnp.float32
                )
                if span:
                    first = scores[:, :span].reshape(heads, tok, span) + bias_ref[:, :span][None]
                    first = first.reshape(part_rows, span)
                    if span < scores.shape[1]:
                        first = jnp.concatenate([first, scores[:, span:]], axis=1)
                    scores = first
                peak = jnp.max(scores, axis=1, keepdims=True) * factor
                if kept:
                    before = kept_refs[1][head, here, :]
                    peak = jnp.maximum(jnp.broadcast_to(peak, before.shape), before)
                    shifted = jnp.concatenate(
                        [
                            scores[:, at : at + dim] * factor - peak
                            for at in range(0, scores.shape[1], dim)
                        ],
                        axis=1,
                    )
                else:
                    shifted = scores * factor - peak
                weights = jnp.exp2(shifted).astype(jnp.bfloat16)
                sums = jnp.dot(weights, values, preferred_element_type=jnp.float32)
                numerator, denominator = sums[:, :dim], sums[:, dim:]
                if kept:
                    carry = jnp.exp2(before - peak)
                    numerator = numerator + carry * kept_refs[0][head, here, :]
                    denominator = denominator + carry
                emit(
                    head,
                    part,
                    numerator * reciprocal(denominator),
                    lambda: peak + jnp.log2(denominator),
                )

        all_heads(one)

    def hand_on():
        def one(head):
            for part in range(PARTS):
                here = slice(part * part_rows, (part + 1) * part_rows)
                emit(head, part, kept_refs[0][head, here, :], lambda: kept_refs[1][head, here, :])

        all_heads(one)

    def out_copy(step):
        span = STEP_HEADS * GROUP * dim
        here = pl.ds(pl.multiple_of(step * span, span), span)
        return pltpu.make_async_copy(out_refs[0].at[:, here], result_ref.at[:, here], sems.at[step])

    def all_heads(one):
        @pl.loop(0, KV_HEADS // STEP_HEADS)
        def _(step):
            for index in range(STEP_HEADS):
                one(step * STEP_HEADS + index)
            if last:
                out_copy(step).start()

    near = width * cores * tok if lowest == 0 else 0
    levels = sorted(set(range(lowest, highest + 1)))
    if len(levels) > 4:
        levels = sorted({lowest + (len(levels) - 1) * part // 3 for part in range(4)})
    below = lowest - 1
    if kept and lowest > 0:

        @pl.when(zz < lowest)
        def _():
            hand_on()

    for level in levels:
        used = [piece for piece in pieces if piece[0] <= level]
        alone = level == below + 1
        span = near if alone else len(used) * tok
        reached = jnp.logical_and(zz > below, zz <= level)
        if level == levels[-1]:
            reached = zz > below

        @pl.when(reached)
        def _(used=used, span=span):
            attend(used, span)

        below = level

    if last:

        @pl.loop(0, KV_HEADS // STEP_HEADS)
        def _(step):
            out_copy(step).wait()


def solution(mesh):
    grid = chip_grid(mesh.shape["tp"])
    depth, width, cores = grid
    assert cores == 2 and depth > 2

    def body(query_rows, key_rows, value_rows):
        tok, columns = query_rows.shape
        dim = key_rows.shape[1] // KV_HEADS
        rows = GROUP * tok
        query_rows, key_rows, value_rows = (
            pltpu.with_memory_space_constraint(array, pltpu.HBM)
            for array in (query_rows, key_rows, value_rows)
        )
        block = stack([key_rows, value_rows], "pack")
        queries = fetch(query_rows)
        rows_of = []
        for dz in range(depth):
            row = [block, y_swap(block, grid)] if width == 2 else [block]
            if dz + 1 < depth:
                following = z_forward(block, grid)
                block, row, queries = lax.optimization_barrier((following, row, queries))
            rows_of.append(row)

        whole = pl.BlockSpec(memory_space=pltpu.VMEM)
        state_shape = jax.ShapeDtypeStruct((KV_HEADS, rows, dim), jnp.float32)
        steps = KV_HEADS // STEP_HEADS
        def merge(span):
            merged = stack([block for dz in span for block in rows_of[dz]], "merge")
            return [merged, core_swap(merged, grid)]

        def phase(spans, operands, state, last):
            groups = [[dz for dz in span for _ in range(width)] for span in spans]
            count = sum(2 * len(group) for group in groups)
            keys = tok * count
            masked = spans[0][0] == 0 or spans[-1][-1] - spans[0][0] > 3
            scratch = []
            if last:
                scratch += [pltpu.VMEM((tok, columns), query_rows.dtype)]
                scratch += [pltpu.SemaphoreType.DMA((steps,))]
            if masked:
                scratch += [pltpu.VMEM((tok, keys), jnp.float32)]
            return pl.pallas_call(
                functools.partial(attend_kernel, grid, groups, bool(state), last),
                out_shape=query_rows if last else [state_shape] * 2,
                in_specs=[whole] * (1 + len(operands) + len(state)),
                out_specs=pl.BlockSpec(memory_space=pltpu.HBM) if last else [whole] * 2,
                scratch_shapes=scratch,
                compiler_params=pltpu.CompilerParams(vmem_limit_bytes=24 * 2**20),
                cost_estimate=pl.CostEstimate(
                    flops=4 * HEADS * tok * keys * dim,
                    bytes_accessed=4 * HEADS * tok * dim,
                    transcendentals=HEADS * tok * keys,
                ),
                name="attend_last" if last else "attend_first",
            )(queries, *operands, *state)

        early = [range(0, 2)]
        late = [range(2, depth - 1), range(depth - 1, depth)]
        late = [span for span in late if len(span)]
        operands = merge(early[0])
        operands, rows_of[-1][0] = lax.optimization_barrier((operands, rows_of[-1][0]))
        state = phase(early, operands, [], False)
        rows_of[-1], state = lax.optimization_barrier((rows_of[-1], state))
        operands = [operand for span in late for operand in merge(span)]
        return phase(late, operands, list(state), True)

    spec = P(("groups", "tp"), None)
    return jax.shard_map(
        body, mesh=mesh, in_specs=(spec, spec, spec), out_specs=spec, check_vma=False
    )
```

```python
import functools
import math

import jax
import jax.numpy as jnp
from jax import lax
from jax.experimental import pallas as pl
from jax.experimental.pallas import tpu as pltpu
from jax.sharding import PartitionSpec as P

HEADS = 128
KV_HEADS = 8
GROUP = HEADS // KV_HEADS
PARTS = 4
STEP_HEADS = 2

masked_score = -1e30


def chip_grid(devices):
    if devices % 2:
        return devices, 1, 1
    chips = devices // 2
    if chips % 2 or chips > 8:
        return chips, 1, 2
    return chips // 2, 2, 2


def place(grid):
    depth, width, cores = grid
    me = lax.axis_index("tp")
    return me // (width * cores), (me // cores) % width, me % cores


def stack(arrays, name):
    def kernel(*refs):
        for at, ref in enumerate(refs[:-1]):
            refs[-1][at] = ref[...]

    count = len(arrays)
    return pl.pallas_call(
        kernel,
        out_shape=jax.ShapeDtypeStruct((count, *arrays[0].shape), arrays[0].dtype),
        in_specs=[pl.BlockSpec(memory_space=pltpu.VMEM)] * count,
        out_specs=pl.BlockSpec(memory_space=pltpu.VMEM),
        compiler_params=pltpu.CompilerParams(vmem_limit_bytes=32 * 2**20),
        name=name,
    )(*arrays)


def z_forward(block, grid):
    depth, width, cores = grid
    count = depth * width * cores
    return lax.ppermute(
        block, "tp", [(at, (at + width * cores) % count) for at in range(count)]
    )


def y_swap(block, grid):
    depth, width, cores = grid
    return lax.ppermute(
        block, "tp", [(at, at ^ cores) for at in range(depth * width * cores)]
    )


def core_swap(blocks, grid):
    depth, width, cores = grid
    return lax.ppermute(blocks, "tp", [(at, at ^ 1) for at in range(depth * width * cores)])


def reciprocal(x):
    guess = pl.reciprocal(x, approx=True)
    return guess * (2.0 - x * guess)


def attend_kernel(grid, groups, kept, last, query_ref, *refs):
    depth, width, cores = grid
    blocks_refs, refs = refs[: 2 * len(groups)], refs[2 * len(groups) :]
    kept_refs, refs = refs[: 2 * kept], refs[2 * kept :]
    out_refs, scratch = list(refs[: 2 - last]), list(refs[2 - last :])
    if not kept:
        source_ref, query_ref, query_sems = query_ref, scratch.pop(0), scratch.pop(0)
    if last:
        result_ref = out_refs[0]
        out_refs[0], sems = scratch.pop(0), scratch.pop(0)
    tok = query_ref.shape[0]
    dim = blocks_refs[0].shape[-1] // KV_HEADS
    rows = GROUP * tok
    part_rows = rows // PARTS
    heads = part_rows // tok
    factor = dim ** (-0.5) * math.log2(math.e)
    zz, yy, cc = place(grid)

    pieces = []
    for below, own_ref, core_ref in zip(groups, blocks_refs[::2], blocks_refs[1::2]):
        for dc, ref in ((0, own_ref), (1, core_ref)):
            for at, dz in enumerate(below):
                pieces.append((dz, dc, below[:at].count(dz), ref, at))
    pieces.sort(key=lambda piece: piece[:3])
    lowest, highest = pieces[0][0], pieces[-1][0]

    if scratch:
        bias_ref = scratch[0]

        row = lax.broadcasted_iota(jnp.int32, (tok, tok), 0)
        key = lax.broadcasted_iota(jnp.int32, (tok, tok), 1)
        for at, (dz, dc, dy, _, _) in enumerate(pieces):
            if dz:
                limit = jnp.where(zz >= dz, 0, tok) + 0 * key
            elif dy:
                limit = jnp.where(yy == 1, 0, tok) + 0 * key
            elif dc:
                limit = jnp.where(cc == 1, 0, tok) + 0 * key
            else:
                limit = key
            bias_ref[:, at * tok : (at + 1) * tok] = jnp.where(limit <= row, 0.0, masked_score)

    def column(index):
        return pl.ds(pl.multiple_of(index * dim, dim), dim)

    def emit(head, part, sums, peak):
        here = slice(part * part_rows, (part + 1) * part_rows)
        if not last:
            out_refs[0][head, here, :] = sums
            out_refs[1][head, here, :] = jnp.broadcast_to(peak, (part_rows, dim))
            return
        result = (sums[:, :dim] * reciprocal(sums[:, dim:])).astype(out_refs[0].dtype)
        for index in range(heads):
            out_refs[0][:, column((head * PARTS + part) * heads + index)] = result[
                index * tok : (index + 1) * tok
            ]

    def attend(used, span):
        def one(head):
            span_of = column(head)
            keys = jnp.concatenate([ref[at, 0, :, span_of] for _, _, _, ref, at in used], axis=0)
            values = jnp.concatenate([ref[at, 1, :, span_of] for _, _, _, ref, at in used], axis=0)
            values = jnp.concatenate([values, jnp.ones_like(values)], axis=1)
            first_head = head * GROUP
            for part in range(PARTS):
                here = slice(part * part_rows, (part + 1) * part_rows)
                query = jnp.concatenate(
                    [
                        query_ref[:, column(first_head + index)]
                        for index in range(part * heads, (part + 1) * heads)
                    ],
                    axis=0,
                )
                scores = lax.dot_general(
                    query, keys, (((1,), (1,)), ((), ())), preferred_element_type=jnp.float32
                )
                if span:
                    first = scores[:, :span].reshape(heads, tok, span) + bias_ref[:, :span][None]
                    first = first.reshape(part_rows, span)
                    if span < scores.shape[1]:
                        first = jnp.concatenate([first, scores[:, span:]], axis=1)
                    scores = first
                peak = jnp.max(scores, axis=1, keepdims=True) * factor
                if kept:
                    before = kept_refs[1][head, here, :]
                    peak = jnp.maximum(jnp.broadcast_to(peak, before.shape), before)
                    shifted = jnp.concatenate(
                        [
                            scores[:, at : at + dim] * factor - peak
                            for at in range(0, scores.shape[1], dim)
                        ],
                        axis=1,
                    )
                else:
                    shifted = scores * factor - peak
                weights = jnp.exp2(shifted).astype(jnp.bfloat16)
                sums = jnp.dot(weights, values, preferred_element_type=jnp.float32)
                if kept:
                    carry = jnp.exp2(before - peak)
                    carry = jnp.concatenate([carry, carry], axis=1)
                    sums = sums + carry * kept_refs[0][head, here, :]
                emit(head, part, sums, peak)

        all_heads(one)

    def hand_on():
        def one(head):
            for part in range(PARTS):
                here = slice(part * part_rows, (part + 1) * part_rows)
                emit(head, part, kept_refs[0][head, here, :], kept_refs[1][head, here, :])

        all_heads(one)

    def out_copy(step):
        span = STEP_HEADS * GROUP * dim
        here = pl.ds(pl.multiple_of(step * span, span), span)
        return pltpu.make_async_copy(out_refs[0].at[:, here], result_ref.at[:, here], sems.at[step])

    def query_copy(step):
        span = STEP_HEADS * GROUP * dim
        here = pl.ds(pl.multiple_of(step * span, span), span)
        return pltpu.make_async_copy(
            source_ref.at[:, here], query_ref.at[:, here], query_sems.at[step]
        )

    if not kept:

        @pl.loop(0, KV_HEADS // STEP_HEADS)
        def _(step):
            query_copy(step).start()

    def all_heads(one):
        @pl.loop(0, KV_HEADS // STEP_HEADS)
        def _(step):
            if not kept:
                query_copy(step).wait()
            for index in range(STEP_HEADS):
                one(step * STEP_HEADS + index)
            if last:
                out_copy(step).start()

    near = width * cores * tok if lowest == 0 else 0
    levels = sorted(set(range(lowest, highest + 1)))
    if len(levels) > 4:
        levels = sorted({lowest + (len(levels) - 1) * part // 3 for part in range(4)})
    below = lowest - 1
    if kept and lowest > 0:

        @pl.when(zz < lowest)
        def _():
            hand_on()

    for level in levels:
        used = [piece for piece in pieces if piece[0] <= level]
        alone = level == below + 1
        span = near if alone else len(used) * tok
        reached = jnp.logical_and(zz > below, zz <= level)
        if level == levels[-1]:
            reached = zz > below

        @pl.when(reached)
        def _(used=used, span=span):
            attend(used, span)

        below = level

    if last:

        @pl.loop(0, KV_HEADS // STEP_HEADS)
        def _(step):
            out_copy(step).wait()


def solution(mesh):
    grid = chip_grid(mesh.shape["tp"])
    depth, width, cores = grid
    assert cores == 2 and depth > 2

    def body(query_rows, key_rows, value_rows):
        tok, columns = query_rows.shape
        dim = key_rows.shape[1] // KV_HEADS
        rows = GROUP * tok
        pinned, key_rows, value_rows = (
            pltpu.with_memory_space_constraint(array, pltpu.HBM)
            for array in (query_rows, key_rows, value_rows)
        )
        whole = pl.BlockSpec(memory_space=pltpu.VMEM)
        state_shapes = [
            jax.ShapeDtypeStruct((KV_HEADS, rows, size), jnp.float32) for size in (2 * dim, dim)
        ]
        steps = KV_HEADS // STEP_HEADS

        def phase(span, state):
            last = span[-1] == depth - 1
            merged = stack([block for dz in span for block in rows_of[dz]], "merge")
            operands = [merged, core_swap(merged, grid)]
            groups = [[dz for dz in span for _ in range(width)]]
            keys = tok * 2 * len(groups[0])
            scratch = []
            if not state:
                scratch += [pltpu.VMEM((tok, columns), query_rows.dtype)]
                scratch += [pltpu.SemaphoreType.DMA((steps,))]
            if last:
                scratch += [pltpu.VMEM((tok, columns), query_rows.dtype)]
                scratch += [pltpu.SemaphoreType.DMA((steps,))]
            if span[0] == 0 or len(span) > 4:
                scratch += [pltpu.VMEM((tok, keys), jnp.float32)]
            return pl.pallas_call(
                functools.partial(attend_kernel, grid, groups, bool(state), last),
                out_shape=query_rows if last else state_shapes,
                in_specs=[whole if state else pl.BlockSpec(memory_space=pltpu.HBM)]
                + [whole] * (len(operands) + len(state)),
                out_specs=pl.BlockSpec(memory_space=pltpu.HBM) if last else [whole] * 2,
                scratch_shapes=scratch,
                input_output_aliases={} if last or not state else {3: 0, 4: 1},
                compiler_params=pltpu.CompilerParams(vmem_limit_bytes=16 * 2**20),
                cost_estimate=pl.CostEstimate(
                    flops=4 * HEADS * tok * keys * dim,
                    bytes_accessed=4 * HEADS * tok * dim,
                    transcendentals=HEADS * tok * keys,
                ),
                name=f"attend_{span[0]}",
            )(query_rows if state else pinned, *operands, *state)

        spans = [range(0, 1), range(1, 2)]
        spans += [range(at, min(at + 4, depth - 1)) for at in range(2, depth - 1, 4)]
        spans += [range(depth - 1, depth)]
        block = stack([key_rows, value_rows], "pack")
        rows_of, state = [], []
        for dz in range(depth):
            rows_of.append([block, y_swap(block, grid)] if width == 2 else [block])
            if dz + 1 == depth:
                break
            block = z_forward(block, grid)
            at = dz - 1
            if dz and spans[0][-1] <= at:
                span = spans.pop(0)
                state = phase(span, state)
            if dz:
                block, state, rows_of[dz] = lax.optimization_barrier((block, state, rows_of[dz]))
            else:
                block, rows_of[0] = lax.optimization_barrier((block, rows_of[0]))
        while spans:
            if len(spans) == 1:
                rows_of[-1], state = lax.optimization_barrier((rows_of[-1], state))
            state = phase(spans.pop(0), state)
        return state

    spec = P(("groups", "tp"), None)
    return jax.shard_map(
        body, mesh=mesh, in_specs=(spec, spec, spec), out_specs=spec, check_vma=False
    )
```

```python
import functools
import math

import jax
import jax.numpy as jnp
from jax import lax
from jax.experimental import pallas as pl
from jax.experimental.pallas import tpu as pltpu
from jax.sharding import PartitionSpec as P

HEADS = 128
KV_HEADS = 8
GROUP = HEADS // KV_HEADS
PARTS = 4
STEP_HEADS = 2

masked_score = -1e30


def chip_grid(devices):
    if devices % 2:
        return devices, 1, 1
    chips = devices // 2
    if chips % 2 or chips > 8:
        return chips, 1, 2
    return chips // 2, 2, 2


def place(grid):
    depth, width, cores = grid
    me = lax.axis_index("tp")
    return me // (width * cores), (me // cores) % width, me % cores


def stack(arrays, name):
    def kernel(*refs):
        for at, ref in enumerate(refs[:-1]):
            refs[-1][at] = ref[...]

    count = len(arrays)
    return pl.pallas_call(
        kernel,
        out_shape=jax.ShapeDtypeStruct((count, *arrays[0].shape), arrays[0].dtype),
        in_specs=[pl.BlockSpec(memory_space=pltpu.VMEM)] * count,
        out_specs=pl.BlockSpec(memory_space=pltpu.VMEM),
        compiler_params=pltpu.CompilerParams(vmem_limit_bytes=32 * 2**20),
        name=name,
    )(*arrays)


def z_forward(block, grid):
    depth, width, cores = grid
    count = depth * width * cores
    return lax.ppermute(
        block, "tp", [(at, (at + width * cores) % count) for at in range(count)]
    )


def y_swap(block, grid):
    depth, width, cores = grid
    return lax.ppermute(
        block, "tp", [(at, at ^ cores) for at in range(depth * width * cores)]
    )


def step(block, grid):
    depth, width, cores = grid
    count = depth * width * cores
    halves = [
        lax.ppermute(
            block,
            "tp",
            [
                (at, (at + width * cores) % count if at % cores == along_z else at ^ cores)
                for at in range(count)
            ],
        )
        for along_z in range(cores)
    ]

    def kernel(first_ref, second_ref, z_ref, y_ref):
        _, _, cc = place(grid)

        @pl.when(cc == 0)
        def _():
            z_ref[...] = first_ref[...]
            y_ref[...] = second_ref[...]

        @pl.when(cc != 0)
        def _():
            z_ref[...] = second_ref[...]
            y_ref[...] = first_ref[...]

    return halves, lambda halves: pl.pallas_call(
        kernel,
        out_shape=[jax.ShapeDtypeStruct(block.shape, block.dtype)] * 2,
        in_specs=[pl.BlockSpec(memory_space=pltpu.VMEM)] * 2,
        out_specs=[pl.BlockSpec(memory_space=pltpu.VMEM)] * 2,
        name="sort",
    )(*halves)


def core_swap(blocks, grid):
    depth, width, cores = grid
    return lax.ppermute(blocks, "tp", [(at, at ^ 1) for at in range(depth * width * cores)])


def reciprocal(x):
    guess = pl.reciprocal(x, approx=True)
    return guess * (2.0 - x * guess)


def attend_kernel(grid, entries, kept, last, query_ref, *refs):
    depth, width, cores = grid
    blocks_refs, refs = refs[:2], refs[2:]
    kept_refs, refs = refs[: 2 * kept], refs[2 * kept :]
    out_refs, scratch = list(refs[: 2 - last]), list(refs[2 - last :])
    if not kept:
        source_ref, query_ref, query_sems = query_ref, scratch.pop(0), scratch.pop(0)
    if last:
        result_ref = out_refs[0]
        out_refs[0], sems = scratch.pop(0), scratch.pop(0)
    tok = query_ref.shape[0]
    dim = blocks_refs[0].shape[-1] // KV_HEADS
    rows = GROUP * tok
    part_rows = rows // PARTS
    heads = part_rows // tok
    factor = dim ** (-0.5) * math.log2(math.e)
    zz, yy, cc = place(grid)

    pieces = []
    for dc, ref in enumerate(blocks_refs):
        for at, (dz, dy) in enumerate(entries):
            pieces.append((dz, dc, dy, ref, at))
    pieces.sort(key=lambda piece: piece[:3])
    lowest, highest = pieces[0][0], pieces[-1][0]

    if scratch:
        bias_ref = scratch[0]

        row = lax.broadcasted_iota(jnp.int32, (tok, tok), 0)
        key = lax.broadcasted_iota(jnp.int32, (tok, tok), 1)
        for at, (dz, dc, dy, _, _) in enumerate(pieces):
            if dz:
                limit = jnp.where(zz >= dz, 0, tok) + 0 * key
            elif dy:
                limit = jnp.where(yy == 1, 0, tok) + 0 * key
            elif dc:
                limit = jnp.where(cc == 1, 0, tok) + 0 * key
            else:
                limit = key
            bias_ref[:, at * tok : (at + 1) * tok] = jnp.where(limit <= row, 0.0, masked_score)

    def column(index):
        return pl.ds(pl.multiple_of(index * dim, dim), dim)

    def emit(head, part, sums, peak):
        here = slice(part * part_rows, (part + 1) * part_rows)
        if not last:
            out_refs[0][head, here, :] = sums
            out_refs[1][head, here, :] = jnp.broadcast_to(peak, (part_rows, dim))
            return
        result = (sums[:, :dim] * reciprocal(sums[:, dim:])).astype(out_refs[0].dtype)
        for index in range(heads):
            out_refs[0][:, column((head * PARTS + part) * heads + index)] = result[
                index * tok : (index + 1) * tok
            ]

    def attend(used, span):
        def one(head):
            span_of = column(head)
            keys = jnp.concatenate([ref[at, 0, :, span_of] for _, _, _, ref, at in used], axis=0)
            values = jnp.concatenate([ref[at, 1, :, span_of] for _, _, _, ref, at in used], axis=0)
            values = jnp.concatenate([values, jnp.ones_like(values)], axis=1)
            first_head = head * GROUP
            for part in range(PARTS):
                here = slice(part * part_rows, (part + 1) * part_rows)
                query = jnp.concatenate(
                    [
                        query_ref[:, column(first_head + index)]
                        for index in range(part * heads, (part + 1) * heads)
                    ],
                    axis=0,
                )
                scores = lax.dot_general(
                    query, keys, (((1,), (1,)), ((), ())), preferred_element_type=jnp.float32
                )
                if span:
                    first = scores[:, :span].reshape(heads, tok, span) + bias_ref[:, :span][None]
                    first = first.reshape(part_rows, span)
                    if span < scores.shape[1]:
                        first = jnp.concatenate([first, scores[:, span:]], axis=1)
                    scores = first
                peak = jnp.max(scores, axis=1, keepdims=True) * factor
                if kept:
                    before = kept_refs[1][head, here, :]
                    peak = jnp.maximum(jnp.broadcast_to(peak, before.shape), before)
                    shifted = jnp.concatenate(
                        [
                            scores[:, at : at + dim] * factor - peak
                            for at in range(0, scores.shape[1], dim)
                        ],
                        axis=1,
                    )
                else:
                    shifted = scores * factor - peak
                weights = jnp.exp2(shifted).astype(jnp.bfloat16)
                sums = jnp.dot(weights, values, preferred_element_type=jnp.float32)
                if kept:
                    carry = jnp.exp2(before - peak)
                    carry = jnp.concatenate([carry, carry], axis=1)
                    sums = sums + carry * kept_refs[0][head, here, :]
                emit(head, part, sums, peak)

        all_heads(one)

    def hand_on():
        def one(head):
            for part in range(PARTS):
                here = slice(part * part_rows, (part + 1) * part_rows)
                emit(head, part, kept_refs[0][head, here, :], kept_refs[1][head, here, :])

        all_heads(one)

    def out_copy(step):
        span = STEP_HEADS * GROUP * dim
        here = pl.ds(pl.multiple_of(step * span, span), span)
        return pltpu.make_async_copy(out_refs[0].at[:, here], result_ref.at[:, here], sems.at[step])

    def query_copy(step):
        span = STEP_HEADS * GROUP * dim
        here = pl.ds(pl.multiple_of(step * span, span), span)
        return pltpu.make_async_copy(
            source_ref.at[:, here], query_ref.at[:, here], query_sems.at[step]
        )

    if not kept:

        @pl.loop(0, KV_HEADS // STEP_HEADS)
        def _(step):
            query_copy(step).start()

    def all_heads(one):
        @pl.loop(0, KV_HEADS // STEP_HEADS)
        def _(step):
            if not kept:
                query_copy(step).wait()
            for index in range(STEP_HEADS):
                one(step * STEP_HEADS + index)
            if last:
                out_copy(step).start()

    near = width * cores * tok if lowest == 0 else 0
    levels = sorted(set(range(lowest, highest + 1)))
    if len(levels) > 4:
        levels = sorted({lowest + (len(levels) - 1) * part // 3 for part in range(4)})
    below = lowest - 1
    if kept and lowest > 0:

        @pl.when(zz < lowest)
        def _():
            hand_on()

    for level in levels:
        used = [piece for piece in pieces if piece[0] <= level]
        alone = level == below + 1
        span = near if alone else len(used) * tok
        reached = jnp.logical_and(zz > below, zz <= level)
        if level == levels[-1]:
            reached = zz > below

        @pl.when(reached)
        def _(used=used, span=span):
            attend(used, span)

        below = level

    if last:

        @pl.loop(0, KV_HEADS // STEP_HEADS)
        def _(step):
            out_copy(step).wait()


def solution(mesh):
    grid = chip_grid(mesh.shape["tp"])
    depth, width, cores = grid
    assert cores == 2 and depth > 2

    def body(query_rows, key_rows, value_rows):
        tok, columns = query_rows.shape
        dim = key_rows.shape[1] // KV_HEADS
        rows = GROUP * tok
        pinned, key_rows, value_rows = (
            pltpu.with_memory_space_constraint(array, pltpu.HBM)
            for array in (query_rows, key_rows, value_rows)
        )
        whole = pl.BlockSpec(memory_space=pltpu.VMEM)
        state_shapes = [
            jax.ShapeDtypeStruct((KV_HEADS, rows, size), jnp.float32) for size in (2 * dim, dim)
        ]
        steps = KV_HEADS // STEP_HEADS

        def phase(entries, blocks, state, last=False):
            merged = stack([blocks[entry] for entry in entries], "merge")
            operands = [merged, core_swap(merged, grid)]
            keys = tok * 2 * len(entries)
            rows_below = entries[-1][0] - entries[0][0]
            scratch = []
            if not state:
                scratch += [pltpu.VMEM((tok, columns), query_rows.dtype)]
                scratch += [pltpu.SemaphoreType.DMA((steps,))]
            if last:
                scratch += [pltpu.VMEM((tok, columns), query_rows.dtype)]
                scratch += [pltpu.SemaphoreType.DMA((steps,))]
            if entries[0][0] == 0 or rows_below > 3:
                scratch += [pltpu.VMEM((tok, keys), jnp.float32)]
            return pl.pallas_call(
                functools.partial(attend_kernel, grid, entries, bool(state), last),
                out_shape=query_rows if last else state_shapes,
                in_specs=[whole if state else pl.BlockSpec(memory_space=pltpu.HBM)]
                + [whole] * (len(operands) + len(state)),
                out_specs=pl.BlockSpec(memory_space=pltpu.HBM) if last else [whole] * 2,
                scratch_shapes=scratch,
                input_output_aliases={} if last or not state else {3: 0, 4: 1},
                compiler_params=pltpu.CompilerParams(vmem_limit_bytes=16 * 2**20),
                cost_estimate=pl.CostEstimate(
                    flops=4 * HEADS * tok * keys * dim,
                    bytes_accessed=4 * HEADS * tok * dim,
                    transcendentals=HEADS * tok * keys,
                ),
                name="attend_last" if last else f"attend_{entries[0][0]}",
            )(query_rows if state else pinned, *operands, *state)

        batches = [[(dz, dy) for dy in range(width)] for dz in range(depth - 1)]
        while len(batches) > 3 + depth // 4:
            batches[-2:] = [batches[-2] + batches[-1]]
        final = (depth - 1, width - 1)
        if width == 2:
            batches[-1].append((depth - 1, 0))
        blocks = {(0, 0): stack([key_rows, value_rows], "pack")}
        state = []
        for dz in range(depth - 1):
            if width == 2:
                halves, sort = step(blocks[dz, 0], grid)
                halves, state = lax.optimization_barrier((halves, state))
                blocks[dz + 1, 0], blocks[dz, 1] = sort(halves)
            else:
                blocks[dz + 1, 0], state = lax.optimization_barrier(
                    (z_forward(blocks[dz, 0], grid), state)
                )
            if batches and all(entry in blocks for entry in batches[0]):
                state = phase(batches.pop(0), blocks, state)
        if width == 2:
            blocks[final] = y_swap(blocks[depth - 1, 0], grid)
        blocks[final], state = lax.optimization_barrier((blocks[final], state))
        return phase([final], blocks, state, last=True)

    spec = P(("groups", "tp"), None)
    return jax.shard_map(
        body, mesh=mesh, in_specs=(spec, spec, spec), out_specs=spec, check_vma=False
    )
```

```python
import functools
import math

import jax
import jax.numpy as jnp
from jax import lax
from jax.experimental import pallas as pl
from jax.experimental.pallas import tpu as pltpu
from jax.sharding import PartitionSpec as P

HEADS = 128
KV_HEADS = 8
GROUP = HEADS // KV_HEADS
PARTS = 4
STEP_HEADS = 2

masked_score = -1e30


def chip_grid(devices):
    if devices % 2:
        return devices, 1, 1
    chips = devices // 2
    if chips % 2 or chips > 8:
        return chips, 1, 2
    return chips // 2, 2, 2


def place(grid):
    depth, width, cores = grid
    me = lax.axis_index("tp")
    return me // (width * cores), (me // cores) % width, me % cores


def stack(arrays, name):
    def kernel(*refs):
        for at, ref in enumerate(refs[:-1]):
            refs[-1][at] = ref[...]

    count = len(arrays)
    return pl.pallas_call(
        kernel,
        out_shape=jax.ShapeDtypeStruct((count, *arrays[0].shape), arrays[0].dtype),
        in_specs=[pl.BlockSpec(memory_space=pltpu.VMEM)] * count,
        out_specs=pl.BlockSpec(memory_space=pltpu.VMEM),
        compiler_params=pltpu.CompilerParams(vmem_limit_bytes=4 * 2**20),
        name=name,
    )(*arrays)


def z_forward(block, grid):
    depth, width, cores = grid
    count = depth * width * cores
    return lax.ppermute(
        block, "tp", [(at, (at + width * cores) % count) for at in range(count)]
    )


def y_swap(block, grid):
    depth, width, cores = grid
    return lax.ppermute(
        block, "tp", [(at, at ^ cores) for at in range(depth * width * cores)]
    )


def core_swap(blocks, grid):
    depth, width, cores = grid
    return lax.ppermute(blocks, "tp", [(at, at ^ 1) for at in range(depth * width * cores)])


def reciprocal(x):
    guess = pl.reciprocal(x, approx=True)
    return guess * (2.0 - x * guess)


def attend_kernel(grid, entries, kept, last, query_ref, *refs):
    depth, width, cores = grid
    count = len(entries)
    own_refs, core_refs, refs = refs[:count], refs[count : 3 * count], refs[3 * count :]
    kept_refs, refs = refs[: 2 * kept], refs[2 * kept :]
    out_refs, scratch = list(refs[: 2 - last]), list(refs[2 - last :])
    if not kept:
        source_ref, query_ref, query_sems = query_ref, scratch.pop(0), scratch.pop(0)
    if last:
        result_ref = out_refs[0]
        out_refs[0], sems = scratch.pop(0), scratch.pop(0)
    tok = query_ref.shape[0]
    dim = own_refs[0].shape[-1] // KV_HEADS
    rows = GROUP * tok
    part_rows = rows // PARTS
    heads = part_rows // tok
    factor = dim ** (-0.5) * math.log2(math.e)
    zz, yy, cc = place(grid)

    pieces = []
    for at, (dz, dy) in enumerate(entries):
        pieces.append((dz, 0, dy, own_refs[at].at[0], own_refs[at].at[1]))
        pieces.append((dz, 1, dy, *core_refs[2 * at : 2 * at + 2]))
    pieces.sort(key=lambda piece: piece[:3])

    if scratch:
        bias_ref = scratch[0]

        row = lax.broadcasted_iota(jnp.int32, (tok, tok), 0)
        key = lax.broadcasted_iota(jnp.int32, (tok, tok), 1)
        for at, (dz, dc, dy, _, _) in enumerate(pieces):
            if dz:
                limit = jnp.where(zz >= dz, 0, tok) + 0 * key
            elif dy:
                limit = jnp.where(yy == 1, 0, tok) + 0 * key
            elif dc:
                limit = jnp.where(cc == 1, 0, tok) + 0 * key
            else:
                limit = key
            bias_ref[:, at * tok : (at + 1) * tok] = jnp.where(limit <= row, 0.0, masked_score)

    def column(index):
        return pl.ds(pl.multiple_of(index * dim, dim), dim)

    def emit(head, part, sums, peak):
        here = slice(part * part_rows, (part + 1) * part_rows)
        if not last:
            out_refs[0][head, here, :] = sums
            out_refs[1][head, here, :] = jnp.broadcast_to(peak, (part_rows, dim))
            return
        result = (sums[:, :dim] * reciprocal(sums[:, dim:])).astype(out_refs[0].dtype)
        for index in range(heads):
            out_refs[0][:, column((head * PARTS + part) * heads + index)] = result[
                index * tok : (index + 1) * tok
            ]

    def attend(used, span):
        def one(head):
            span_of = column(head)
            keys = jnp.concatenate([piece[3][:, span_of] for piece in used], axis=0)
            values = jnp.concatenate([piece[4][:, span_of] for piece in used], axis=0)
            values = jnp.concatenate([values, jnp.ones_like(values)], axis=1)
            first_head = head * GROUP
            for part in range(PARTS):
                here = slice(part * part_rows, (part + 1) * part_rows)
                query = jnp.concatenate(
                    [
                        query_ref[:, column(first_head + index)]
                        for index in range(part * heads, (part + 1) * heads)
                    ],
                    axis=0,
                )
                scores = lax.dot_general(
                    query, keys, (((1,), (1,)), ((), ())), preferred_element_type=jnp.float32
                )
                if span:
                    first = scores[:, :span].reshape(heads, tok, span) + bias_ref[:, :span][None]
                    first = first.reshape(part_rows, span)
                    if span < scores.shape[1]:
                        first = jnp.concatenate([first, scores[:, span:]], axis=1)
                    scores = first
                peak = jnp.max(scores, axis=1, keepdims=True) * factor
                if kept:
                    before = kept_refs[1][head, here, :]
                    peak = jnp.maximum(jnp.broadcast_to(peak, before.shape), before)
                    shifted = jnp.concatenate(
                        [
                            scores[:, at : at + dim] * factor - peak
                            for at in range(0, scores.shape[1], dim)
                        ],
                        axis=1,
                    )
                else:
                    shifted = scores * factor - peak
                weights = jnp.exp2(shifted).astype(jnp.bfloat16)
                sums = jnp.dot(weights, values, preferred_element_type=jnp.float32)
                if kept:
                    carry = jnp.exp2(before - peak)
                    carry = jnp.concatenate([carry, carry], axis=1)
                    sums = sums + carry * kept_refs[0][head, here, :]
                emit(head, part, sums, peak)

        all_heads(one)

    def hand_on():
        def one(head):
            for part in range(PARTS):
                here = slice(part * part_rows, (part + 1) * part_rows)
                emit(head, part, kept_refs[0][head, here, :], kept_refs[1][head, here, :])

        all_heads(one)

    def out_copy(step):
        span = STEP_HEADS * GROUP * dim
        here = pl.ds(pl.multiple_of(step * span, span), span)
        return pltpu.make_async_copy(out_refs[0].at[:, here], result_ref.at[:, here], sems.at[step])

    def query_copy(step):
        span = STEP_HEADS * GROUP * dim
        here = pl.ds(pl.multiple_of(step * span, span), span)
        return pltpu.make_async_copy(
            source_ref.at[:, here], query_ref.at[:, here], query_sems.at[step]
        )

    if not kept:

        @pl.loop(0, KV_HEADS // STEP_HEADS)
        def _(step):
            query_copy(step).start()

    def all_heads(one):
        @pl.loop(0, KV_HEADS // STEP_HEADS)
        def _(step):
            if not kept:
                query_copy(step).wait()
            for index in range(STEP_HEADS):
                one(step * STEP_HEADS + index)
            if last:
                out_copy(step).start()

    near = tok * sum(piece[0] == 0 for piece in pieces)
    levels = sorted({piece[0] for piece in pieces})
    masked = len(levels) > 4
    if masked:
        levels = levels[:1]
    if levels[0] > 0:

        @pl.when(zz < levels[0])
        def _():
            hand_on()

    for level, above in zip(levels, levels[1:] + [depth]):
        used = pieces if masked else [piece for piece in pieces if piece[0] <= level]
        span = len(used) * tok if masked else near

        @pl.when(jnp.logical_and(zz >= level, zz < above))
        def _(used=used, span=span):
            attend(used, span)

    if last:

        @pl.loop(0, KV_HEADS // STEP_HEADS)
        def _(step):
            out_copy(step).wait()


def solution(mesh):
    grid = chip_grid(mesh.shape["tp"])
    depth, width, cores = grid
    assert cores == 2 and depth > 2

    def body(query_rows, key_rows, value_rows):
        tok, columns = query_rows.shape
        dim = key_rows.shape[1] // KV_HEADS
        rows = GROUP * tok
        pinned, key_rows, value_rows = (
            pltpu.with_memory_space_constraint(array, pltpu.HBM)
            for array in (query_rows, key_rows, value_rows)
        )
        whole = pl.BlockSpec(memory_space=pltpu.VMEM)
        state_shapes = [
            jax.ShapeDtypeStruct((KV_HEADS, rows, size), jnp.float32) for size in (2 * dim, dim)
        ]
        steps = KV_HEADS // STEP_HEADS

        def phase(entries, blocks, state, last=False, after=None):
            operands = [blocks[entry] for entry in entries]
            operands += [core_swap(blocks[entry][half], grid) for entry in entries for half in range(2)]
            if after in blocks:
                operands, blocks[after] = lax.optimization_barrier((operands, blocks[after]))
            keys = tok * 2 * len(entries)
            levels = {dz for dz, _ in entries}
            scratch = []
            if not state:
                scratch += [pltpu.VMEM((tok, columns), query_rows.dtype)]
                scratch += [pltpu.SemaphoreType.DMA((steps,))]
            if last:
                scratch += [pltpu.VMEM((tok, columns), query_rows.dtype)]
                scratch += [pltpu.SemaphoreType.DMA((steps,))]
            if 0 in levels or len(levels) > 4:
                scratch += [pltpu.VMEM((tok, keys), jnp.float32)]
            return pl.pallas_call(
                functools.partial(attend_kernel, grid, entries, bool(state), last),
                out_shape=query_rows if last else state_shapes,
                in_specs=[whole if state else pl.BlockSpec(memory_space=pltpu.HBM)]
                + [whole] * (len(operands) + len(state)),
                out_specs=pl.BlockSpec(memory_space=pltpu.HBM) if last else [whole] * 2,
                scratch_shapes=scratch,
                input_output_aliases={} if last or not state else {1 + len(operands) + at: at for at in range(2)},
                compiler_params=pltpu.CompilerParams(vmem_limit_bytes=16 * 2**20),
                cost_estimate=pl.CostEstimate(flops=1000, bytes_accessed=1000, transcendentals=0),
                name="attend_last" if last else f"attend_{entries[0][0]}",
            )(query_rows if state else pinned, *operands, *state)

        batches = [[(0, 0), (1, 0)]] + [[(dz, 0)] for dz in range(2, depth)]
        if width == 2:
            for dz in range(depth - 2):
                batches[dz + 1].append((dz, 1))
            batches.append([(depth - 2, 1), (depth - 1, 1)])
        while len(batches) > 8:
            batches = [sum(batches[at : at + 2], []) for at in range(0, len(batches), 2)]
        blocks = {(0, 0): stack([key_rows, value_rows], "pack")}
        state = []
        for dz in range(depth):
            block = blocks[dz, 0]
            if dz + 1 < depth:
                blocks[dz + 1, 0] = z_forward(block, grid)
            if width == 2:
                blocks[dz, 1] = y_swap(block, grid)
            while len(batches) > 1 and all(entry[0] + 2 * entry[1] <= dz for entry in batches[0]):
                state = phase(batches.pop(0), blocks, state, after=(dz - 1, 1))
            if dz + 1 < depth:
                blocks[dz + 1, 0], state = lax.optimization_barrier((blocks[dz + 1, 0], state))
        tied = batches[0]
        values, state = lax.optimization_barrier(([blocks[entry] for entry in tied], state))
        blocks.update(zip(tied, values))
        return phase(tied, blocks, state, last=True)

    spec = P(("groups", "tp"), None)
    return jax.shard_map(
        body, mesh=mesh, in_specs=(spec, spec, spec), out_specs=spec, check_vma=False
    )
```

```python
import functools
import math

import jax
import jax.numpy as jnp
from jax import lax
from jax.experimental import pallas as pl
from jax.experimental.pallas import tpu as pltpu
from jax.sharding import PartitionSpec as P

HEADS = 128
KV_HEADS = 8
GROUP = HEADS // KV_HEADS
PARTS = 1
STEP_HEADS = 2

masked_score = -1e30


def chip_grid(devices):
    if devices % 2:
        return devices, 1, 1
    chips = devices // 2
    if chips % 2 or chips > 8:
        return chips, 1, 2
    return chips // 2, 2, 2


def place(grid):
    depth, width, cores = grid
    me = lax.axis_index("tp")
    return me // (width * cores), (me // cores) % width, me % cores


def stack(arrays, name):
    def kernel(*refs):
        for at, ref in enumerate(refs[:-1]):
            refs[-1][at] = ref[...]

    count = len(arrays)
    return pl.pallas_call(
        kernel,
        out_shape=jax.ShapeDtypeStruct((count, *arrays[0].shape), arrays[0].dtype),
        in_specs=[pl.BlockSpec(memory_space=pltpu.VMEM)] * count,
        out_specs=pl.BlockSpec(memory_space=pltpu.VMEM),
        compiler_params=pltpu.CompilerParams(vmem_limit_bytes=4 * 2**20),
        name=name,
    )(*arrays)


def z_forward(block, grid):
    depth, width, cores = grid
    count = depth * width * cores
    return lax.ppermute(
        block, "tp", [(at, (at + width * cores) % count) for at in range(count)]
    )


def y_swap(block, grid):
    depth, width, cores = grid
    return lax.ppermute(
        block, "tp", [(at, at ^ cores) for at in range(depth * width * cores)]
    )


def core_swap(blocks, grid):
    depth, width, cores = grid
    return lax.ppermute(blocks, "tp", [(at, at ^ 1) for at in range(depth * width * cores)])


def reciprocal(x):
    guess = pl.reciprocal(x, approx=True)
    return guess * (2.0 - x * guess)


def attend_kernel(grid, entries, kept, last, query_ref, *refs):
    depth, width, cores = grid
    count = len(entries)
    own_refs, core_refs, refs = refs[:count], refs[count : 3 * count], refs[3 * count :]
    kept_refs, refs = refs[: 2 * kept], refs[2 * kept :]
    out_refs, scratch = list(refs[: 2 - last]), list(refs[2 - last :])
    if not kept:
        source_ref, query_ref, query_sems = query_ref, scratch.pop(0), scratch.pop(0)
    if last:
        result_ref = out_refs[0]
        out_refs[0], sems = scratch.pop(0), scratch.pop(0)
    tok = query_ref.shape[0]
    dim = own_refs[0].shape[-1] // KV_HEADS
    rows = GROUP * tok
    part_rows = rows // PARTS
    heads = part_rows // tok
    factor = dim ** (-0.5) * math.log2(math.e)
    zz, yy, cc = place(grid)

    pieces = []
    for at, (dz, dy) in enumerate(entries):
        pieces.append((dz, 0, dy, own_refs[at].at[0], own_refs[at].at[1]))
        pieces.append((dz, 1, dy, *core_refs[2 * at : 2 * at + 2]))
    pieces.sort(key=lambda piece: piece[:3])

    if scratch:
        bias_ref = scratch[0]

        row = lax.broadcasted_iota(jnp.int32, (tok, tok), 0)
        key = lax.broadcasted_iota(jnp.int32, (tok, tok), 1)
        for at, (dz, dc, dy, _, _) in enumerate(pieces):
            if dz:
                limit = jnp.where(zz >= dz, 0, tok) + 0 * key
            elif dy:
                limit = jnp.where(yy == 1, 0, tok) + 0 * key
            elif dc:
                limit = jnp.where(cc == 1, 0, tok) + 0 * key
            else:
                limit = key
            bias_ref[:, at * tok : (at + 1) * tok] = jnp.where(limit <= row, 0.0, masked_score)

    def column(index):
        return pl.ds(pl.multiple_of(index * dim, dim), dim)

    def emit(head, part, sums, peak):
        here = slice(part * part_rows, (part + 1) * part_rows)
        if not last:
            out_refs[0][head, here, :] = sums
            out_refs[1][head, here, :] = jnp.broadcast_to(peak, (part_rows, dim))
            return
        result = (sums[:, :dim] * reciprocal(sums[:, dim:])).astype(out_refs[0].dtype)
        for index in range(heads):
            out_refs[0][:, column((head * PARTS + part) * heads + index)] = result[
                index * tok : (index + 1) * tok
            ]

    def attend(used, span):
        def one(head):
            span_of = column(head)
            keys = jnp.concatenate([piece[3][:, span_of] for piece in used], axis=0)
            values = jnp.concatenate([piece[4][:, span_of] for piece in used], axis=0)
            values = jnp.concatenate([values, jnp.ones_like(values)], axis=1)
            first_head = head * GROUP
            for part in range(PARTS):
                here = slice(part * part_rows, (part + 1) * part_rows)
                query = jnp.concatenate(
                    [
                        query_ref[:, column(first_head + index)]
                        for index in range(part * heads, (part + 1) * heads)
                    ],
                    axis=0,
                )
                scores = lax.dot_general(
                    query, keys, (((1,), (1,)), ((), ())), preferred_element_type=jnp.float32
                )
                if span:
                    first = scores[:, :span].reshape(heads, tok, span) + bias_ref[:, :span][None]
                    first = first.reshape(part_rows, span)
                    if span < scores.shape[1]:
                        first = jnp.concatenate([first, scores[:, span:]], axis=1)
                    scores = first
                peak = jnp.max(scores, axis=1, keepdims=True) * factor
                if kept:
                    before = kept_refs[1][head, here, :]
                    peak = jnp.maximum(jnp.broadcast_to(peak, before.shape), before)
                    shifted = jnp.concatenate(
                        [
                            scores[:, at : at + dim] * factor - peak
                            for at in range(0, scores.shape[1], dim)
                        ],
                        axis=1,
                    )
                else:
                    shifted = scores * factor - peak
                weights = jnp.exp2(shifted).astype(jnp.bfloat16)
                sums = jnp.dot(weights, values, preferred_element_type=jnp.float32)
                if kept:
                    carry = jnp.exp2(before - peak)
                    carry = jnp.concatenate([carry, carry], axis=1)
                    sums = sums + carry * kept_refs[0][head, here, :]
                emit(head, part, sums, peak)

        all_heads(one)

    def hand_on():
        def one(head):
            for part in range(PARTS):
                here = slice(part * part_rows, (part + 1) * part_rows)
                emit(head, part, kept_refs[0][head, here, :], kept_refs[1][head, here, :])

        all_heads(one)

    def out_copy(step):
        span = STEP_HEADS * GROUP * dim
        here = pl.ds(pl.multiple_of(step * span, span), span)
        return pltpu.make_async_copy(out_refs[0].at[:, here], result_ref.at[:, here], sems.at[step])

    def query_copy(step):
        span = STEP_HEADS * GROUP * dim
        here = pl.ds(pl.multiple_of(step * span, span), span)
        return pltpu.make_async_copy(
            source_ref.at[:, here], query_ref.at[:, here], query_sems.at[step]
        )

    if not kept:

        @pl.loop(0, KV_HEADS // STEP_HEADS)
        def _(step):
            query_copy(step).start()

    def all_heads(one):
        @pl.loop(0, KV_HEADS // STEP_HEADS)
        def _(step):
            if not kept:
                query_copy(step).wait()
            for index in range(STEP_HEADS):
                one(step * STEP_HEADS + index)
            if last:
                out_copy(step).start()

    near = tok * sum(piece[0] == 0 for piece in pieces)
    levels = sorted({piece[0] for piece in pieces})
    masked = len(levels) > 4
    if masked:
        levels = levels[:1]
    if levels[0] > 0:

        @pl.when(zz < levels[0])
        def _():
            hand_on()

    for level, above in zip(levels, levels[1:] + [depth]):
        used = pieces if masked else [piece for piece in pieces if piece[0] <= level]
        span = len(used) * tok if masked else near

        @pl.when(jnp.logical_and(zz >= level, zz < above))
        def _(used=used, span=span):
            attend(used, span)

    if last:

        @pl.loop(0, KV_HEADS // STEP_HEADS)
        def _(step):
            out_copy(step).wait()


def solution(mesh):
    grid = chip_grid(mesh.shape["tp"])
    depth, width, cores = grid
    assert cores == 2 and depth > 2

    def body(query_rows, key_rows, value_rows):
        tok, columns = query_rows.shape
        dim = key_rows.shape[1] // KV_HEADS
        rows = GROUP * tok
        pinned, key_rows, value_rows = (
            pltpu.with_memory_space_constraint(array, pltpu.HBM)
            for array in (query_rows, key_rows, value_rows)
        )
        whole = pl.BlockSpec(memory_space=pltpu.VMEM)
        state_shapes = [
            jax.ShapeDtypeStruct((KV_HEADS, rows, size), jnp.float32) for size in (2 * dim, dim)
        ]
        steps = KV_HEADS // STEP_HEADS

        def phase(entries, blocks, state, last=False, after=None):
            operands = [blocks[entry] for entry in entries]
            operands += [core_swap(blocks[entry][half], grid) for entry in entries for half in range(2)]
            if after in blocks:
                operands, blocks[after] = lax.optimization_barrier((operands, blocks[after]))
            keys = tok * 2 * len(entries)
            levels = {dz for dz, _ in entries}
            scratch = []
            if not state:
                scratch += [pltpu.VMEM((tok, columns), query_rows.dtype)]
                scratch += [pltpu.SemaphoreType.DMA((steps,))]
            if last:
                scratch += [pltpu.VMEM((tok, columns), query_rows.dtype)]
                scratch += [pltpu.SemaphoreType.DMA((steps,))]
            if 0 in levels or len(levels) > 4:
                scratch += [pltpu.VMEM((tok, keys), jnp.float32)]
            return pl.pallas_call(
                functools.partial(attend_kernel, grid, entries, bool(state), last),
                out_shape=query_rows if last else state_shapes,
                in_specs=[whole if state else pl.BlockSpec(memory_space=pltpu.HBM)]
                + [whole] * (len(operands) + len(state)),
                out_specs=pl.BlockSpec(memory_space=pltpu.HBM) if last else [whole] * 2,
                scratch_shapes=scratch,
                input_output_aliases={} if last or not state else {1 + len(operands) + at: at for at in range(2)},
                compiler_params=pltpu.CompilerParams(vmem_limit_bytes=16 * 2**20),
                cost_estimate=pl.CostEstimate(flops=1000, bytes_accessed=1000, transcendentals=0),
                name="attend_last" if last else f"attend_{entries[0][0]}",
            )(query_rows if state else pinned, *operands, *state)

        batches = [[(0, 0), (1, 0)]] + [[(dz, 0)] for dz in range(2, depth)]
        if width == 2:
            for dz in range(depth - 2):
                batches[dz + 1].append((dz, 1))
            batches.append([(depth - 2, 1), (depth - 1, 1)])
        while len(batches) > 8:
            batches = [sum(batches[at : at + 2], []) for at in range(0, len(batches), 2)]
        blocks = {(0, 0): stack([key_rows, value_rows], "pack")}
        state = []
        for dz in range(depth):
            block = blocks[dz, 0]
            if dz + 1 < depth:
                blocks[dz + 1, 0] = z_forward(block, grid)
            if width == 2:
                blocks[dz, 1] = y_swap(block, grid)
            while len(batches) > 1 and all(entry[0] + 2 * entry[1] <= dz for entry in batches[0]):
                state = phase(batches.pop(0), blocks, state, after=(dz - 1, 1))
            if dz + 1 < depth:
                blocks[dz + 1, 0], state = lax.optimization_barrier((blocks[dz + 1, 0], state))
        tied = batches[0]
        values, state = lax.optimization_barrier(([blocks[entry] for entry in tied], state))
        blocks.update(zip(tied, values))
        return phase(tied, blocks, state, last=True)

    spec = P(("groups", "tp"), None)
    return jax.shard_map(
        body, mesh=mesh, in_specs=(spec, spec, spec), out_specs=spec, check_vma=False
    )
```

```python
import functools
import math

import jax
import jax.numpy as jnp
from jax import lax
from jax.experimental import pallas as pl
from jax.experimental.pallas import tpu as pltpu
from jax.sharding import PartitionSpec as P

HEADS = 128
KV_HEADS = 8
GROUP = HEADS // KV_HEADS
PARTS = 1
UNROLL = 8

masked_score = -1e30


def chip_grid(devices):
    if devices % 2:
        return devices, 1, 1
    chips = devices // 2
    if chips % 2 or chips > 8:
        return chips, 1, 2
    return chips // 2, 2, 2


def place(grid):
    depth, width, cores = grid
    me = lax.axis_index("tp")
    return me // (width * cores), (me // cores) % width, me % cores


def stack(arrays, name):
    def kernel(*refs):
        for at, ref in enumerate(refs[:-1]):
            refs[-1][at] = ref[...]

    count = len(arrays)
    return pl.pallas_call(
        kernel,
        out_shape=jax.ShapeDtypeStruct((count, *arrays[0].shape), arrays[0].dtype),
        in_specs=[pl.BlockSpec(memory_space=pltpu.VMEM)] * count,
        out_specs=pl.BlockSpec(memory_space=pltpu.VMEM),
        compiler_params=pltpu.CompilerParams(vmem_limit_bytes=4 * 2**20),
        name=name,
    )(*arrays)


def z_forward(block, grid):
    depth, width, cores = grid
    count = depth * width * cores
    return lax.ppermute(
        block, "tp", [(at, (at + width * cores) % count) for at in range(count)]
    )


def y_swap(block, grid):
    depth, width, cores = grid
    return lax.ppermute(
        block, "tp", [(at, at ^ cores) for at in range(depth * width * cores)]
    )


def core_swap(blocks, grid):
    depth, width, cores = grid
    return lax.ppermute(blocks, "tp", [(at, at ^ 1) for at in range(depth * width * cores)])


def reciprocal(x):
    guess = pl.reciprocal(x, approx=True)
    return guess * (2.0 - x * guess)


def attend_kernel(grid, entries, kept, last, query_ref, *refs):
    depth, width, cores = grid
    count = len(entries)
    own_refs, core_refs, refs = refs[:count], refs[count : 3 * count], refs[3 * count :]
    kept_refs, refs = refs[: 2 * kept], refs[2 * kept :]
    out_refs, scratch = list(refs[: 2 - last]), list(refs[2 - last :])
    if not kept:
        source_ref, query_ref, query_sems = query_ref, scratch.pop(0), scratch.pop(0)
    if last:
        result_ref = out_refs[0]
        out_refs[0], sems = scratch.pop(0), scratch.pop(0)
    tok = query_ref.shape[0]
    dim = own_refs[0].shape[-1] // KV_HEADS
    rows = GROUP * tok
    part_rows = rows // PARTS
    heads = part_rows // tok
    factor = dim ** (-0.5) * math.log2(math.e)
    zz, yy, cc = place(grid)

    pieces = []
    for at, (dz, dy) in enumerate(entries):
        pieces.append((dz, 0, dy, own_refs[at].at[0], own_refs[at].at[1]))
        pieces.append((dz, 1, dy, *core_refs[2 * at : 2 * at + 2]))
    pieces.sort(key=lambda piece: piece[:3])

    if scratch:
        bias_ref = scratch[0]

        row = lax.broadcasted_iota(jnp.int32, (tok, tok), 0)
        key = lax.broadcasted_iota(jnp.int32, (tok, tok), 1)
        for at, (dz, dc, dy, _, _) in enumerate(pieces):
            if dz:
                limit = jnp.where(zz >= dz, 0, tok) + 0 * key
            elif dy:
                limit = jnp.where(yy == 1, 0, tok) + 0 * key
            elif dc:
                limit = jnp.where(cc == 1, 0, tok) + 0 * key
            else:
                limit = key
            bias_ref[:, at * tok : (at + 1) * tok] = jnp.where(limit <= row, 0.0, masked_score)

    def column(index):
        if isinstance(index, int):
            return pl.ds(index * dim, dim)
        return pl.ds(pl.multiple_of(index * dim, dim), dim)

    def emit(head, part, sums, peak):
        here = slice(part * part_rows, (part + 1) * part_rows)
        if not last:
            out_refs[0][head, here, :] = sums
            out_refs[1][head, here, :] = jnp.broadcast_to(peak, (part_rows, dim))
            return
        result = (sums[:, :dim] * reciprocal(sums[:, dim:])).astype(out_refs[0].dtype)
        for index in range(heads):
            out_refs[0][:, column((head * PARTS + part) * heads + index)] = result[
                index * tok : (index + 1) * tok
            ]

    def attend(used, span):
        def one(head):
            span_of = column(head)
            keys = jnp.concatenate([piece[3][:, span_of] for piece in used], axis=0)
            values = jnp.concatenate([piece[4][:, span_of] for piece in used], axis=0)
            values = jnp.concatenate([values, jnp.ones_like(values)], axis=1)
            first_head = head * GROUP
            for part in range(PARTS):
                here = slice(part * part_rows, (part + 1) * part_rows)
                query = jnp.concatenate(
                    [
                        query_ref[:, column(first_head + index)]
                        for index in range(part * heads, (part + 1) * heads)
                    ],
                    axis=0,
                )
                scores = lax.dot_general(
                    query, keys, (((1,), (1,)), ((), ())), preferred_element_type=jnp.float32
                )
                if span:
                    first = scores[:, :span].reshape(heads, tok, span) + bias_ref[:, :span][None]
                    first = first.reshape(part_rows, span)
                    if span < scores.shape[1]:
                        first = jnp.concatenate([first, scores[:, span:]], axis=1)
                    scores = first
                peak = jnp.max(scores, axis=1, keepdims=True) * factor
                if kept:
                    before = kept_refs[1][head, here, :]
                    peak = jnp.maximum(jnp.broadcast_to(peak, before.shape), before)
                    shifted = jnp.concatenate(
                        [
                            scores[:, at : at + dim] * factor - peak
                            for at in range(0, scores.shape[1], dim)
                        ],
                        axis=1,
                    )
                else:
                    shifted = scores * factor - peak
                weights = jnp.exp2(shifted).astype(jnp.bfloat16)
                sums = jnp.dot(weights, values, preferred_element_type=jnp.float32)
                if kept:
                    carry = jnp.exp2(before - peak)
                    carry = jnp.concatenate([carry, carry], axis=1)
                    sums = sums + carry * kept_refs[0][head, here, :]
                emit(head, part, sums, peak)

        all_heads(one)

    def hand_on():
        def one(head):
            for part in range(PARTS):
                here = slice(part * part_rows, (part + 1) * part_rows)
                emit(head, part, kept_refs[0][head, here, :], kept_refs[1][head, here, :])

        all_heads(one)

    def copy_of(head, source, target, sems):
        span = GROUP * dim
        start = head * span if isinstance(head, int) else pl.multiple_of(head * span, span)
        here = pl.ds(start, span)
        return pltpu.make_async_copy(source.at[:, here], target.at[:, here], sems.at[head])

    def query_copy(head):
        return copy_of(head, source_ref, query_ref, query_sems)

    def out_copy(head):
        return copy_of(head, out_refs[0], result_ref, sems)

    if not kept:
        for head in range(KV_HEADS):
            query_copy(head).start()

    def all_heads(one):
        def some(first):
            for index in range(UNROLL):
                head = first + index
                if not kept:
                    query_copy(head).wait()
                one(head)
                if last:
                    out_copy(head).start()

        if UNROLL == KV_HEADS:
            some(0)
        else:

            @pl.loop(0, KV_HEADS // UNROLL)
            def _(step):
                some(step * UNROLL)

    near = tok * sum(piece[0] == 0 for piece in pieces)
    levels = sorted({piece[0] for piece in pieces})
    masked = len(levels) > 4
    if masked:
        levels = levels[:1]
    if levels[0] > 0:

        @pl.when(zz < levels[0])
        def _():
            hand_on()

    for level, above in zip(levels, levels[1:] + [depth]):
        used = pieces if masked else [piece for piece in pieces if piece[0] <= level]
        span = len(used) * tok if masked else near

        @pl.when(jnp.logical_and(zz >= level, zz < above))
        def _(used=used, span=span):
            attend(used, span)

    if last:
        for head in range(KV_HEADS):
            out_copy(head).wait()


def solution(mesh):
    grid = chip_grid(mesh.shape["tp"])
    depth, width, cores = grid
    assert cores == 2 and depth > 2

    def body(query_rows, key_rows, value_rows):
        tok, columns = query_rows.shape
        dim = key_rows.shape[1] // KV_HEADS
        rows = GROUP * tok
        pinned, key_rows, value_rows = (
            pltpu.with_memory_space_constraint(array, pltpu.HBM)
            for array in (query_rows, key_rows, value_rows)
        )
        whole = pl.BlockSpec(memory_space=pltpu.VMEM)
        state_shapes = [
            jax.ShapeDtypeStruct((KV_HEADS, rows, size), jnp.float32) for size in (2 * dim, dim)
        ]

        def phase(entries, blocks, state, last=False, after=None):
            operands = [blocks[entry] for entry in entries]
            operands += [core_swap(blocks[entry][half], grid) for entry in entries for half in range(2)]
            if after in blocks:
                operands, blocks[after] = lax.optimization_barrier((operands, blocks[after]))
            keys = tok * 2 * len(entries)
            levels = {dz for dz, _ in entries}
            scratch = []
            if not state:
                scratch += [pltpu.VMEM((tok, columns), query_rows.dtype)]
                scratch += [pltpu.SemaphoreType.DMA((KV_HEADS,))]
            if last:
                scratch += [pltpu.VMEM((tok, columns), query_rows.dtype)]
                scratch += [pltpu.SemaphoreType.DMA((KV_HEADS,))]
            if 0 in levels or len(levels) > 4:
                scratch += [pltpu.VMEM((tok, keys), jnp.float32)]
            return pl.pallas_call(
                functools.partial(attend_kernel, grid, entries, bool(state), last),
                out_shape=query_rows if last else state_shapes,
                in_specs=[whole if state else pl.BlockSpec(memory_space=pltpu.HBM)]
                + [whole] * (len(operands) + len(state)),
                out_specs=pl.BlockSpec(memory_space=pltpu.HBM) if last else [whole] * 2,
                scratch_shapes=scratch,
                input_output_aliases={} if last or not state else {1 + len(operands) + at: at for at in range(2)},
                compiler_params=pltpu.CompilerParams(vmem_limit_bytes=16 * 2**20),
                cost_estimate=pl.CostEstimate(flops=1000, bytes_accessed=1000, transcendentals=0),
                name="attend_last" if last else f"attend_{entries[0][0]}",
            )(query_rows if state else pinned, *operands, *state)

        batches = [[(0, 0), (1, 0)]] + [[(dz, 0)] for dz in range(2, depth)]
        if width == 2:
            for dz in range(depth - 2):
                batches[dz + 1].append((dz, 1))
            batches.append([(depth - 2, 1), (depth - 1, 1)])
        while len(batches) > 8:
            batches = [sum(batches[at : at + 2], []) for at in range(0, len(batches), 2)]
        blocks = {(0, 0): stack([key_rows, value_rows], "pack")}
        state = []
        for dz in range(depth):
            block = blocks[dz, 0]
            if dz + 1 < depth:
                blocks[dz + 1, 0] = z_forward(block, grid)
            if width == 2:
                blocks[dz, 1] = y_swap(block, grid)
            while len(batches) > 1 and all(entry[0] + 2 * entry[1] <= dz for entry in batches[0]):
                state = phase(batches.pop(0), blocks, state, after=(dz - 1, 1))
            if dz + 1 < depth:
                blocks[dz + 1, 0], state = lax.optimization_barrier((blocks[dz + 1, 0], state))
        tied = batches[0]
        values, state = lax.optimization_barrier(([blocks[entry] for entry in tied], state))
        blocks.update(zip(tied, values))
        return phase(tied, blocks, state, last=True)

    spec = P(("groups", "tp"), None)
    return jax.shard_map(
        body, mesh=mesh, in_specs=(spec, spec, spec), out_specs=spec, check_vma=False
    )
```

```python
import functools
import math

import jax
import jax.numpy as jnp
from jax import lax
from jax.experimental import pallas as pl
from jax.experimental.pallas import tpu as pltpu
from jax.sharding import PartitionSpec as P

HEADS = 128
KV_HEADS = 8
GROUP = HEADS // KV_HEADS
STRIPS = 8

masked_score = -1e30


def chip_grid(devices):
    if devices % 2:
        return devices, 1, 1
    chips = devices // 2
    if chips % 2 or chips > 8:
        return chips, 1, 2
    return chips // 2, 2, 2


def place(grid):
    depth, width, cores = grid
    me = lax.axis_index("tp")
    return me // (width * cores), (me // cores) % width, me % cores


def stack(arrays, name):
    def kernel(*refs):
        for at, ref in enumerate(refs[:-1]):
            refs[-1][at] = ref[...]

    count = len(arrays)
    return pl.pallas_call(
        kernel,
        out_shape=jax.ShapeDtypeStruct((count, *arrays[0].shape), arrays[0].dtype),
        in_specs=[pl.BlockSpec(memory_space=pltpu.VMEM)] * count,
        out_specs=pl.BlockSpec(memory_space=pltpu.VMEM),
        compiler_params=pltpu.CompilerParams(vmem_limit_bytes=4 * 2**20),
        name=name,
    )(*arrays)


def fetch(array):
    def kernel(array_ref, out_ref, sem):
        copy = pltpu.make_async_copy(array_ref, out_ref, sem)
        copy.start()
        copy.wait()

    return pl.pallas_call(
        kernel,
        out_shape=jax.ShapeDtypeStruct(array.shape, array.dtype),
        in_specs=[pl.BlockSpec(memory_space=pltpu.HBM)],
        out_specs=pl.BlockSpec(memory_space=pltpu.VMEM),
        scratch_shapes=[pltpu.SemaphoreType.DMA],
        compiler_params=pltpu.CompilerParams(vmem_limit_bytes=4 * 2**20),
        name="fetch",
    )(array)


def z_forward(block, grid):
    depth, width, cores = grid
    count = depth * width * cores
    return lax.ppermute(
        block, "tp", [(at, (at + width * cores) % count) for at in range(count)]
    )


def y_swap(block, grid):
    depth, width, cores = grid
    return lax.ppermute(
        block, "tp", [(at, at ^ cores) for at in range(depth * width * cores)]
    )


def core_swap(blocks, grid):
    depth, width, cores = grid
    return lax.ppermute(blocks, "tp", [(at, at ^ 1) for at in range(depth * width * cores)])


def reciprocal(x):
    guess = pl.reciprocal(x, approx=True)
    return guess * (2.0 - x * guess)


def attend_kernel(grid, entries, kept, last, query_ref, *refs):
    depth, width, cores = grid
    count = len(entries)
    own_refs, core_refs, refs = refs[:count], refs[count : 3 * count], refs[3 * count :]
    kept_refs, refs = refs[: 2 * kept], refs[2 * kept :]
    out_refs, scratch = list(refs[: 2 - last]), list(refs[2 - last :])
    scores_refs, weights_refs, carry_refs = (
        (scratch.pop(0), scratch.pop(0)) for _ in range(3)
    )
    if last:
        result_ref = out_refs[0]
        out_refs[0], sems = scratch.pop(0), scratch.pop(0)
    tok = query_ref.shape[0]
    dim = own_refs[0].shape[-1] // KV_HEADS
    rows = GROUP * tok
    strip = rows // STRIPS
    heads = strip // tok
    factor = dim ** (-0.5) * math.log2(math.e)
    zz, yy, cc = place(grid)

    pieces = []
    for at, (dz, dy) in enumerate(entries):
        pieces.append((dz, 0, dy, own_refs[at].at[0], own_refs[at].at[1]))
        pieces.append((dz, 1, dy, *core_refs[2 * at : 2 * at + 2]))
    pieces.sort(key=lambda piece: piece[:3])

    if scratch:
        bias_ref = scratch[0]

        row = lax.broadcasted_iota(jnp.int32, (tok, tok), 0)
        key = lax.broadcasted_iota(jnp.int32, (tok, tok), 1)
        for at, (dz, dc, dy, _, _) in enumerate(pieces):
            if dz:
                limit = jnp.where(zz >= dz, 0, tok) + 0 * key
            elif dy:
                limit = jnp.where(yy == 1, 0, tok) + 0 * key
            elif dc:
                limit = jnp.where(cc == 1, 0, tok) + 0 * key
            else:
                limit = key
            bias_ref[:, at * tok : (at + 1) * tok] = jnp.where(limit <= row, 0.0, masked_score)

    def column(index):
        return pl.ds(pl.multiple_of(index * dim, dim), dim)

    def strips():
        return [slice(at * strip, (at + 1) * strip) for at in range(STRIPS)]

    def finish(head, at, sums):
        result = (sums[:, :dim] * reciprocal(sums[:, dim:])).astype(out_refs[0].dtype)
        for index in range(heads):
            out_refs[0][:, column(head * GROUP + at * heads + index)] = result[
                index * tok : (index + 1) * tok
            ]

    def out_copy(head):
        span = GROUP * dim
        here = pl.ds(pl.multiple_of(head * span, span), span)
        return pltpu.make_async_copy(out_refs[0].at[:, here], result_ref.at[:, here], sems.at[head])

    def attend(used, span):
        count = len(used) * tok

        def fill(slot, head):
            keys = jnp.concatenate([piece[3][:, column(head)] for piece in used], axis=0)
            query = jnp.concatenate(
                [query_ref[:, column(head * GROUP + index)] for index in range(GROUP)], axis=0
            )
            scores_refs[slot][:, :count] = lax.dot_general(
                query, keys, (((1,), (1,)), ((), ())), preferred_element_type=jnp.float32
            )

        def absorb(slot, head):
            for here in strips():
                scores = scores_refs[slot][here, :count]
                if span:
                    first = scores[:, :span].reshape(heads, tok, span) + bias_ref[:, :span][None]
                    first = first.reshape(strip, span)
                    if span < count:
                        first = jnp.concatenate([first, scores[:, span:]], axis=1)
                    scores = first
                peak = jnp.max(scores, axis=1, keepdims=True) * factor
                peak = jnp.broadcast_to(peak, (strip, dim))
                if kept:
                    before = kept_refs[1][head, here, :]
                    peak = jnp.maximum(peak, before)
                    carry_refs[slot][here, :] = jnp.exp2(before - peak)
                if not last:
                    out_refs[1][head, here, :] = peak
                for at in range(0, count, dim):
                    width_here = min(dim, count - at)
                    shifted = scores[:, at : at + width_here] * factor - peak[:, :width_here]
                    weights_refs[slot][here, at : at + width_here] = jnp.exp2(shifted).astype(
                        jnp.bfloat16
                    )
            values = jnp.concatenate([piece[4][:, column(head)] for piece in used], axis=0)
            values = jnp.concatenate([values, jnp.ones_like(values)], axis=1)
            sums = jnp.dot(
                weights_refs[slot][:, :count], values, preferred_element_type=jnp.float32
            )
            for at, here in enumerate(strips()):
                total = sums[here]
                if kept:
                    carry = carry_refs[slot][here, :]
                    total = total + jnp.concatenate([carry, carry], axis=1) * kept_refs[0][head, here, :]
                if last:
                    finish(head, at, total)
                else:
                    out_refs[0][head, here, :] = total
            if last:
                out_copy(head).start()

        fill(0, 0)

        @pl.loop(0, KV_HEADS // 2)
        def _(pair):
            head = 2 * pair
            fill(1, head + 1)
            absorb(0, head)
            fill(0, jnp.minimum(head + 2, KV_HEADS - 1))
            absorb(1, head + 1)

    def hand_on():
        @pl.loop(0, KV_HEADS)
        def _(head):
            for at, here in enumerate(strips()):
                if last:
                    finish(head, at, kept_refs[0][head, here, :])
                else:
                    out_refs[0][head, here, :] = kept_refs[0][head, here, :]
                    out_refs[1][head, here, :] = kept_refs[1][head, here, :]
            if last:
                out_copy(head).start()

    near = tok * sum(piece[0] == 0 for piece in pieces)
    levels = sorted({piece[0] for piece in pieces})
    masked = len(levels) > 4
    if masked:
        levels = levels[:1]
    if levels[0] > 0:

        @pl.when(zz < levels[0])
        def _():
            hand_on()

    for level, above in zip(levels, levels[1:] + [depth]):
        used = pieces if masked else [piece for piece in pieces if piece[0] <= level]
        span = len(used) * tok if masked else near

        @pl.when(jnp.logical_and(zz >= level, zz < above))
        def _(used=used, span=span):
            attend(used, span)

    if last:

        @pl.loop(0, KV_HEADS)
        def _(head):
            out_copy(head).wait()


def solution(mesh):
    grid = chip_grid(mesh.shape["tp"])
    depth, width, cores = grid
    assert cores == 2 and depth > 2

    def body(query_rows, key_rows, value_rows):
        tok, columns = query_rows.shape
        dim = key_rows.shape[1] // KV_HEADS
        rows = GROUP * tok
        query_rows, key_rows, value_rows = (
            pltpu.with_memory_space_constraint(array, pltpu.HBM)
            for array in (query_rows, key_rows, value_rows)
        )
        whole = pl.BlockSpec(memory_space=pltpu.VMEM)
        state_shapes = [
            jax.ShapeDtypeStruct((KV_HEADS, rows, size), jnp.float32) for size in (2 * dim, dim)
        ]

        def phase(entries, blocks, state, last=False, after=None):
            operands = [blocks[entry] for entry in entries]
            operands += [core_swap(blocks[entry][half], grid) for entry in entries for half in range(2)]
            if after in blocks:
                operands, blocks[after] = lax.optimization_barrier((operands, blocks[after]))
            keys = tok * 2 * len(entries)
            levels = {dz for dz, _ in entries}
            scratch = [pltpu.VMEM((rows, keys), jnp.float32)] * 2
            scratch += [pltpu.VMEM((rows, keys), jnp.bfloat16)] * 2
            scratch += [pltpu.VMEM((rows, dim), jnp.float32)] * 2
            if last:
                scratch += [pltpu.VMEM((tok, columns), query_rows.dtype)]
                scratch += [pltpu.SemaphoreType.DMA((KV_HEADS,))]
            if 0 in levels or len(levels) > 4:
                scratch += [pltpu.VMEM((tok, keys), jnp.float32)]
            return pl.pallas_call(
                functools.partial(attend_kernel, grid, entries, bool(state), last),
                out_shape=query_rows if last else state_shapes,
                in_specs=[whole] * (1 + len(operands) + len(state)),
                out_specs=pl.BlockSpec(memory_space=pltpu.HBM) if last else [whole] * 2,
                scratch_shapes=scratch,
                input_output_aliases={} if last or not state else {1 + len(operands) + at: at for at in range(2)},
                compiler_params=pltpu.CompilerParams(vmem_limit_bytes=16 * 2**20),
                cost_estimate=pl.CostEstimate(flops=1000, bytes_accessed=1000, transcendentals=0),
                name="attend_last" if last else f"attend_{entries[0][0]}",
            )(queries, *operands, *state)

        batches = [[(0, 0), (1, 0)]] + [[(dz, 0)] for dz in range(2, depth)]
        if width == 2:
            for dz in range(depth - 2):
                batches[dz + 1].append((dz, 1))
            batches.append([(depth - 2, 1), (depth - 1, 1)])
        while len(batches) > 8:
            batches = [sum(batches[at : at + 2], []) for at in range(0, len(batches), 2)]
        blocks = {(0, 0): stack([key_rows, value_rows], "pack")}
        queries = fetch(query_rows)
        state = []
        for dz in range(depth):
            block = blocks[dz, 0]
            if dz + 1 < depth:
                blocks[dz + 1, 0] = z_forward(block, grid)
            if width == 2:
                blocks[dz, 1] = y_swap(block, grid)
            while len(batches) > 1 and all(entry[0] + 2 * entry[1] <= dz for entry in batches[0]):
                state = phase(batches.pop(0), blocks, state, after=(dz - 1, 1))
            if dz + 1 < depth:
                blocks[dz + 1, 0], state, queries = lax.optimization_barrier(
                    (blocks[dz + 1, 0], state, queries)
                )
        tied = batches[0]
        values, state = lax.optimization_barrier(([blocks[entry] for entry in tied], state))
        blocks.update(zip(tied, values))
        return phase(tied, blocks, state, last=True)

    spec = P(("groups", "tp"), None)
    return jax.shard_map(
        body, mesh=mesh, in_specs=(spec, spec, spec), out_specs=spec, check_vma=False
    )
```

```python
import functools
import math

import jax
import jax.numpy as jnp
from jax import lax
from jax.experimental import pallas as pl
from jax.experimental.pallas import tpu as pltpu
from jax.sharding import PartitionSpec as P

HEADS = 128
KV_HEADS = 8
GROUP = HEADS // KV_HEADS
PARTS = 2
STEP_HEADS = 2

masked_score = -1e30


def chip_grid(devices):
    if devices % 2:
        return devices, 1, 1
    chips = devices // 2
    if chips % 2 or chips > 8:
        return chips, 1, 2
    return chips // 2, 2, 2


def place(grid):
    depth, width, cores = grid
    me = lax.axis_index("tp")
    return me // (width * cores), (me // cores) % width, me % cores


def stack(arrays, name):
    def kernel(*refs):
        for at, ref in enumerate(refs[:-1]):
            refs[-1][at] = ref[...]

    count = len(arrays)
    return pl.pallas_call(
        kernel,
        out_shape=jax.ShapeDtypeStruct((count, *arrays[0].shape), arrays[0].dtype),
        in_specs=[pl.BlockSpec(memory_space=pltpu.VMEM)] * count,
        out_specs=pl.BlockSpec(memory_space=pltpu.VMEM),
        compiler_params=pltpu.CompilerParams(vmem_limit_bytes=4 * 2**20),
        name=name,
    )(*arrays)


def fetch(array):
    def kernel(array_ref, out_ref, sem):
        copy = pltpu.make_async_copy(array_ref, out_ref, sem)
        copy.start()
        copy.wait()

    return pl.pallas_call(
        kernel,
        out_shape=jax.ShapeDtypeStruct(array.shape, array.dtype),
        in_specs=[pl.BlockSpec(memory_space=pltpu.HBM)],
        out_specs=pl.BlockSpec(memory_space=pltpu.VMEM),
        scratch_shapes=[pltpu.SemaphoreType.DMA],
        compiler_params=pltpu.CompilerParams(vmem_limit_bytes=4 * 2**20),
        name="fetch",
    )(array)


def z_forward(block, grid, dz):
    depth, width, cores = grid
    side = width * cores
    pairs = []
    for z in range(depth):
        target = z if z < dz - 1 else dz - 1 if z == depth - 1 else z + 1
        pairs += [(z * side + at, target * side + at) for at in range(side)]
    return lax.ppermute(block, "tp", pairs)


def y_swap(block, grid):
    depth, width, cores = grid
    return lax.ppermute(
        block, "tp", [(at, at ^ cores) for at in range(depth * width * cores)]
    )


def core_swap(blocks, grid):
    depth, width, cores = grid
    return lax.ppermute(blocks, "tp", [(at, at ^ 1) for at in range(depth * width * cores)])


def reciprocal(x):
    guess = pl.reciprocal(x, approx=True)
    return guess * (2.0 - x * guess)


def attend_kernel(grid, entries, kept, last, query_ref, *refs):
    depth, width, cores = grid
    count = len(entries)
    own_refs, core_refs, refs = refs[:count], refs[count : 3 * count], refs[3 * count :]
    kept_refs, refs = refs[: 2 * kept], refs[2 * kept :]
    out_refs, scratch = list(refs[: 2 - last]), list(refs[2 - last :])
    if last:
        result_ref = out_refs[0]
        out_refs[0], sems = scratch.pop(0), scratch.pop(0)
    tok = query_ref.shape[0]
    dim = own_refs[0].shape[-1] // KV_HEADS
    rows = GROUP * tok
    part_rows = rows // PARTS
    heads = part_rows // tok
    factor = dim ** (-0.5) * math.log2(math.e)
    zz, yy, cc = place(grid)

    pieces = []
    for at, (dz, dy) in enumerate(entries):
        pieces.append((dz, 0, dy, own_refs[at].at[0], own_refs[at].at[1]))
        pieces.append((dz, 1, dy, *core_refs[2 * at : 2 * at + 2]))
    pieces.sort(key=lambda piece: piece[:3])

    if scratch:
        bias_ref = scratch[0]

        row = lax.broadcasted_iota(jnp.int32, (tok, tok), 0)
        key = lax.broadcasted_iota(jnp.int32, (tok, tok), 1)
        for at, (dz, dc, dy, _, _) in enumerate(pieces):
            if dz:
                limit = jnp.where(zz >= dz, 0, tok) + 0 * key
            elif dy:
                limit = jnp.where(yy == 1, 0, tok) + 0 * key
            elif dc:
                limit = jnp.where(cc == 1, 0, tok) + 0 * key
            else:
                limit = key
            bias_ref[:, at * tok : (at + 1) * tok] = jnp.where(limit <= row, 0.0, masked_score)

    def column(index):
        return pl.ds(pl.multiple_of(index * dim, dim), dim)

    def emit(head, part, sums, peak):
        here = slice(part * part_rows, (part + 1) * part_rows)
        if not last:
            out_refs[0][head, here, :] = sums
            out_refs[1][head, here, :] = jnp.broadcast_to(peak, (part_rows, dim))
            return
        result = (sums[:, :dim] * reciprocal(sums[:, dim:])).astype(out_refs[0].dtype)
        for index in range(heads):
            out_refs[0][:, column((head * PARTS + part) * heads + index)] = result[
                index * tok : (index + 1) * tok
            ]

    def attend(used, span):
        def one(head):
            span_of = column(head)
            keys = jnp.concatenate([piece[3][:, span_of] for piece in used], axis=0)
            values = jnp.concatenate([piece[4][:, span_of] for piece in used], axis=0)
            values = jnp.concatenate([values, jnp.ones_like(values)], axis=1)
            first_head = head * GROUP
            for part in range(PARTS):
                here = slice(part * part_rows, (part + 1) * part_rows)
                query = jnp.concatenate(
                    [
                        query_ref[:, column(first_head + index)]
                        for index in range(part * heads, (part + 1) * heads)
                    ],
                    axis=0,
                )
                scores = lax.dot_general(
                    query, keys, (((1,), (1,)), ((), ())), preferred_element_type=jnp.float32
                )
                if span:
                    first = scores[:, :span].reshape(heads, tok, span) + bias_ref[:, :span][None]
                    first = first.reshape(part_rows, span)
                    if span < scores.shape[1]:
                        first = jnp.concatenate([first, scores[:, span:]], axis=1)
                    scores = first
                peak = jnp.max(scores, axis=1, keepdims=True) * factor
                if kept:
                    before = kept_refs[1][head, here, :]
                    peak = jnp.maximum(jnp.broadcast_to(peak, before.shape), before)
                    shifted = jnp.concatenate(
                        [
                            scores[:, at : at + dim] * factor - peak
                            for at in range(0, scores.shape[1], dim)
                        ],
                        axis=1,
                    )
                else:
                    shifted = scores * factor - peak
                weights = jnp.exp2(shifted).astype(jnp.bfloat16)
                sums = jnp.dot(weights, values, preferred_element_type=jnp.float32)
                if kept:
                    carry = jnp.exp2(before - peak)
                    carry = jnp.concatenate([carry, carry], axis=1)
                    sums = sums + carry * kept_refs[0][head, here, :]
                emit(head, part, sums, peak)

        all_heads(one)

    def hand_on():
        def one(head):
            for part in range(PARTS):
                here = slice(part * part_rows, (part + 1) * part_rows)
                emit(head, part, kept_refs[0][head, here, :], kept_refs[1][head, here, :])

        all_heads(one)

    def out_copy(step):
        span = STEP_HEADS * GROUP * dim
        here = pl.ds(pl.multiple_of(step * span, span), span)
        return pltpu.make_async_copy(out_refs[0].at[:, here], result_ref.at[:, here], sems.at[step])

    def all_heads(one):
        @pl.loop(0, KV_HEADS // STEP_HEADS)
        def _(step):
            for index in range(STEP_HEADS):
                one(step * STEP_HEADS + index)
            if last:
                out_copy(step).start()

    near = tok * sum(piece[0] == 0 for piece in pieces)
    levels = sorted({piece[0] for piece in pieces})
    masked = len(levels) > 4
    if masked:
        levels = levels[:1]
    if levels[0] > 0:

        @pl.when(zz < levels[0])
        def _():
            hand_on()

    for level, above in zip(levels, levels[1:] + [depth]):
        used = pieces if masked else [piece for piece in pieces if piece[0] <= level]
        span = len(used) * tok if masked else near

        @pl.when(jnp.logical_and(zz >= level, zz < above))
        def _(used=used, span=span):
            attend(used, span)

    if last:

        @pl.loop(0, KV_HEADS // STEP_HEADS)
        def _(step):
            out_copy(step).wait()


def solution(mesh):
    grid = chip_grid(mesh.shape["tp"])
    depth, width, cores = grid
    assert cores == 2 and depth > 2

    def body(query_rows, key_rows, value_rows):
        tok, columns = query_rows.shape
        dim = key_rows.shape[1] // KV_HEADS
        rows = GROUP * tok
        query_rows, key_rows, value_rows = (
            pltpu.with_memory_space_constraint(array, pltpu.HBM)
            for array in (query_rows, key_rows, value_rows)
        )
        whole = pl.BlockSpec(memory_space=pltpu.VMEM)
        state_shapes = [
            jax.ShapeDtypeStruct((KV_HEADS, rows, size), jnp.float32) for size in (2 * dim, dim)
        ]
        steps = KV_HEADS // STEP_HEADS

        swaps = {}

        def swapped(entry):
            if entry not in swaps:
                swaps[entry] = [core_swap(blocks[entry][half], grid) for half in range(2)]
            return swaps[entry]

        def phase(entries, blocks, state, last=False, after=None):
            operands = [blocks[entry] for entry in entries]
            operands += [half for entry in entries for half in swapped(entry)]
            if after:
                operands, blocks[after] = lax.optimization_barrier((operands, blocks[after]))
            keys = tok * 2 * len(entries)
            levels = {dz for dz, _ in entries}
            scratch = []
            if last:
                scratch += [pltpu.VMEM((tok, columns), query_rows.dtype)]
                scratch += [pltpu.SemaphoreType.DMA((steps,))]
            if 0 in levels or len(levels) > 4:
                scratch += [pltpu.VMEM((tok, keys), jnp.float32)]
            return pl.pallas_call(
                functools.partial(attend_kernel, grid, entries, bool(state), last),
                out_shape=query_rows if last else state_shapes,
                in_specs=[whole] * (1 + len(operands) + len(state)),
                out_specs=pl.BlockSpec(memory_space=pltpu.HBM) if last else [whole] * 2,
                scratch_shapes=scratch,
                input_output_aliases={} if last or not state else {1 + len(operands) + at: at for at in range(2)},
                compiler_params=pltpu.CompilerParams(vmem_limit_bytes=16 * 2**20),
                cost_estimate=pl.CostEstimate(flops=1000, bytes_accessed=1000, transcendentals=0),
                name="attend_last" if last else f"attend_{entries[0][0]}",
            )(queries, *operands, *state)

        batches = [[(0, 0), (1, 0)]] + [[(dz, 0)] for dz in range(2, depth)]
        if width == 2:
            for dz in range(depth - 2):
                batches[dz + 1].append((dz, 1))
            batches.append([(depth - 2, 1), (depth - 1, 1)])
        while len(batches) > 8:
            batches = [sum(batches[at : at + 2], []) for at in range(0, len(batches), 2)]
        blocks = {(0, 0): stack([key_rows, value_rows], "pack")}
        queries = fetch(query_rows)
        state = []
        for dz in range(depth):
            block = blocks[dz, 0]
            if dz + 1 < depth:
                blocks[dz + 1, 0] = z_forward(block, grid, dz + 1)
            if width == 2:
                blocks[dz, 1] = y_swap(block, grid)
            while len(batches) > 1 and all(entry[0] + 2 * entry[1] <= dz for entry in batches[0]):
                state = phase(batches.pop(0), blocks, state, after=(dz - 1, 1) if width == 2 else None)
            if dz + 1 < depth:
                blocks[dz + 1, 0], state, queries = lax.optimization_barrier(
                    (blocks[dz + 1, 0], state, queries)
                )
        tied = batches[0]
        values, state = lax.optimization_barrier(([blocks[entry] for entry in tied], state))
        blocks.update(zip(tied, values))
        return phase(tied, blocks, state, last=True)

    spec = P(("groups", "tp"), None)
    return jax.shard_map(
        body, mesh=mesh, in_specs=(spec, spec, spec), out_specs=spec, check_vma=False
    )
```

```python
import functools
import math

import jax
import jax.numpy as jnp
from jax import lax
from jax.experimental import pallas as pl
from jax.experimental.pallas import tpu as pltpu
from jax.sharding import PartitionSpec as P

HEADS = 128
KV_HEADS = 8
GROUP = HEADS // KV_HEADS
PARTS = 2
STEP_HEADS = 2

masked_score = -1e30


def chip_grid(devices):
    if devices % 2:
        return devices, 1, 1
    chips = devices // 2
    if chips % 2 or chips > 8:
        return chips, 1, 2
    return chips // 2, 2, 2


def place(grid):
    depth, width, cores = grid
    me = lax.axis_index("tp")
    return me // (width * cores), (me // cores) % width, me % cores


def stack(arrays, name):
    def kernel(*refs):
        for at, ref in enumerate(refs[:-1]):
            refs[-1][at] = ref[...]

    count = len(arrays)
    return pl.pallas_call(
        kernel,
        out_shape=jax.ShapeDtypeStruct((count, *arrays[0].shape), arrays[0].dtype),
        in_specs=[pl.BlockSpec(memory_space=pltpu.VMEM)] * count,
        out_specs=pl.BlockSpec(memory_space=pltpu.VMEM),
        compiler_params=pltpu.CompilerParams(vmem_limit_bytes=4 * 2**20),
        name=name,
    )(*arrays)


def fetch(array):
    def kernel(array_ref, out_ref, sem):
        copy = pltpu.make_async_copy(array_ref, out_ref, sem)
        copy.start()
        copy.wait()

    return pl.pallas_call(
        kernel,
        out_shape=jax.ShapeDtypeStruct(array.shape, array.dtype),
        in_specs=[pl.BlockSpec(memory_space=pltpu.HBM)],
        out_specs=pl.BlockSpec(memory_space=pltpu.VMEM),
        scratch_shapes=[pltpu.SemaphoreType.DMA],
        compiler_params=pltpu.CompilerParams(vmem_limit_bytes=4 * 2**20),
        name="fetch",
    )(array)


def z_forward(block, grid, dz):
    depth, width, cores = grid
    side = width * cores
    pairs = []
    for z in range(depth):
        target = z ^ 1 if dz == depth - 1 and depth % 2 == 0 else (z + 1) % depth
        pairs += [(z * side + at, target * side + at) for at in range(side)]
    return lax.ppermute(block, "tp", pairs)


def y_swap(block, grid):
    depth, width, cores = grid
    return lax.ppermute(
        block, "tp", [(at, at ^ cores) for at in range(depth * width * cores)]
    )


def core_swap(blocks, grid):
    depth, width, cores = grid
    return lax.ppermute(blocks, "tp", [(at, at ^ 1) for at in range(depth * width * cores)])


def reciprocal(x):
    guess = pl.reciprocal(x, approx=True)
    return guess * (2.0 - x * guess)


def attend_kernel(grid, entries, kept, last, query_ref, *refs):
    depth, width, cores = grid
    count = len(entries)
    halves = 1 if last else 2
    own_refs, refs = refs[:count], refs[count:]
    core_refs, refs = refs[: halves * count], refs[halves * count :]
    kept_refs, refs = refs[: 2 * kept], refs[2 * kept :]
    out_refs, scratch = list(refs[: 2 - last]), list(refs[2 - last :])
    if last:
        result_ref = out_refs[0]
        out_refs[0], sems = scratch.pop(0), scratch.pop(0)
    tok = query_ref.shape[0]
    dim = own_refs[0].shape[-1] // KV_HEADS
    rows = GROUP * tok
    part_rows = rows // PARTS
    heads = part_rows // tok
    factor = dim ** (-0.5) * math.log2(math.e)
    zz, yy, cc = place(grid)

    pieces = []
    for at, (dz, dy) in enumerate(entries):
        pieces.append((dz, 0, dy, own_refs[at].at[0], own_refs[at].at[1]))
        if last:
            pieces.append((dz, 1, dy, core_refs[at].at[0], core_refs[at].at[1]))
        else:
            pieces.append((dz, 1, dy, *core_refs[2 * at : 2 * at + 2]))
    pieces.sort(key=lambda piece: piece[:3])

    if scratch:
        bias_ref = scratch[0]

        row = lax.broadcasted_iota(jnp.int32, (tok, tok), 0)
        key = lax.broadcasted_iota(jnp.int32, (tok, tok), 1)
        for at, (dz, dc, dy, _, _) in enumerate(pieces):
            if dz:
                limit = jnp.where(zz >= dz, 0, tok) + 0 * key
            elif dy:
                limit = jnp.where(yy == 1, 0, tok) + 0 * key
            elif dc:
                limit = jnp.where(cc == 1, 0, tok) + 0 * key
            else:
                limit = key
            bias_ref[:, at * tok : (at + 1) * tok] = jnp.where(limit <= row, 0.0, masked_score)

    def column(index):
        return pl.ds(pl.multiple_of(index * dim, dim), dim)

    def emit(head, part, sums, peak):
        here = slice(part * part_rows, (part + 1) * part_rows)
        if not last:
            out_refs[0][head, here, :] = sums
            out_refs[1][head, here, :] = jnp.broadcast_to(peak, (part_rows, dim))
            return
        result = (sums[:, :dim] * reciprocal(sums[:, dim:])).astype(out_refs[0].dtype)
        for index in range(heads):
            out_refs[0][:, column((head * PARTS + part) * heads + index)] = result[
                index * tok : (index + 1) * tok
            ]

    def attend(used, span):
        def one(head):
            span_of = column(head)
            keys = jnp.concatenate([piece[3][:, span_of] for piece in used], axis=0)
            values = jnp.concatenate([piece[4][:, span_of] for piece in used], axis=0)
            values = jnp.concatenate([values, jnp.ones_like(values)], axis=1)
            first_head = head * GROUP
            for part in range(PARTS):
                here = slice(part * part_rows, (part + 1) * part_rows)
                query = jnp.concatenate(
                    [
                        query_ref[:, column(first_head + index)]
                        for index in range(part * heads, (part + 1) * heads)
                    ],
                    axis=0,
                )
                scores = lax.dot_general(
                    query, keys, (((1,), (1,)), ((), ())), preferred_element_type=jnp.float32
                )
                if span:
                    first = scores[:, :span].reshape(heads, tok, span) + bias_ref[:, :span][None]
                    first = first.reshape(part_rows, span)
                    if span < scores.shape[1]:
                        first = jnp.concatenate([first, scores[:, span:]], axis=1)
                    scores = first
                peak = jnp.max(scores, axis=1, keepdims=True) * factor
                if kept:
                    before = kept_refs[1][head, here, :]
                    peak = jnp.maximum(jnp.broadcast_to(peak, before.shape), before)
                    shifted = jnp.concatenate(
                        [
                            scores[:, at : at + dim] * factor - peak
                            for at in range(0, scores.shape[1], dim)
                        ],
                        axis=1,
                    )
                else:
                    shifted = scores * factor - peak
                weights = jnp.exp2(shifted).astype(jnp.bfloat16)
                sums = jnp.dot(weights, values, preferred_element_type=jnp.float32)
                if kept:
                    carry = jnp.exp2(before - peak)
                    carry = jnp.concatenate([carry, carry], axis=1)
                    sums = sums + carry * kept_refs[0][head, here, :]
                emit(head, part, sums, peak)

        all_heads(one)

    def hand_on():
        def one(head):
            for part in range(PARTS):
                here = slice(part * part_rows, (part + 1) * part_rows)
                emit(head, part, kept_refs[0][head, here, :], kept_refs[1][head, here, :])

        all_heads(one)

    def out_copy(step):
        span = STEP_HEADS * GROUP * dim
        here = pl.ds(pl.multiple_of(step * span, span), span)
        return pltpu.make_async_copy(out_refs[0].at[:, here], result_ref.at[:, here], sems.at[step])

    def all_heads(one):
        @pl.loop(0, KV_HEADS // STEP_HEADS)
        def _(step):
            for index in range(STEP_HEADS):
                one(step * STEP_HEADS + index)
            if last:
                out_copy(step).start()

    near = tok * sum(piece[0] == 0 for piece in pieces)
    levels = sorted({piece[0] for piece in pieces})
    masked = len(levels) > 4
    if masked:
        levels = levels[:1]
    if levels[0] > 0:

        @pl.when(zz < levels[0])
        def _():
            hand_on()

    for level, above in zip(levels, levels[1:] + [depth]):
        used = pieces if masked else [piece for piece in pieces if piece[0] <= level]
        span = len(used) * tok if masked else near

        @pl.when(jnp.logical_and(zz >= level, zz < above))
        def _(used=used, span=span):
            attend(used, span)

    if last:

        @pl.loop(0, KV_HEADS // STEP_HEADS)
        def _(step):
            out_copy(step).wait()


def solution(mesh):
    grid = chip_grid(mesh.shape["tp"])
    depth, width, cores = grid
    assert cores == 2 and depth > 2

    def body(query_rows, key_rows, value_rows):
        tok, columns = query_rows.shape
        dim = key_rows.shape[1] // KV_HEADS
        rows = GROUP * tok
        query_rows, key_rows, value_rows = (
            pltpu.with_memory_space_constraint(array, pltpu.HBM)
            for array in (query_rows, key_rows, value_rows)
        )
        whole = pl.BlockSpec(memory_space=pltpu.VMEM)
        state_shapes = [
            jax.ShapeDtypeStruct((KV_HEADS, rows, size), jnp.float32) for size in (2 * dim, dim)
        ]
        steps = KV_HEADS // STEP_HEADS

        swaps = {}

        def swapped(entry):
            if entry not in swaps:
                swaps[entry] = [core_swap(blocks[entry][half], grid) for half in range(2)]
            return swaps[entry]

        def phase(entries, blocks, state, last=False, after=None):
            operands = [blocks[entry] for entry in entries]
            if last:
                operands += [core_swap(block, grid) for block in operands]
            else:
                operands += [half for entry in entries for half in swapped(entry)]
            if after:
                operands, blocks[after] = lax.optimization_barrier((operands, blocks[after]))
            keys = tok * 2 * len(entries)
            levels = {dz for dz, _ in entries}
            scratch = []
            if last:
                scratch += [pltpu.VMEM((tok, columns), query_rows.dtype)]
                scratch += [pltpu.SemaphoreType.DMA((steps,))]
            if 0 in levels or len(levels) > 4:
                scratch += [pltpu.VMEM((tok, keys), jnp.float32)]
            return pl.pallas_call(
                functools.partial(attend_kernel, grid, entries, bool(state), last),
                out_shape=query_rows if last else state_shapes,
                in_specs=[whole] * (1 + len(operands) + len(state)),
                out_specs=pl.BlockSpec(memory_space=pltpu.HBM) if last else [whole] * 2,
                scratch_shapes=scratch,
                input_output_aliases={} if last or not state else {1 + len(operands) + at: at for at in range(2)},
                compiler_params=pltpu.CompilerParams(vmem_limit_bytes=16 * 2**20),
                cost_estimate=pl.CostEstimate(flops=1000, bytes_accessed=1000, transcendentals=0),
                name="attend_last" if last else f"attend_{entries[0][0]}",
            )(queries, *operands, *state)

        batches = [[(0, 0), (1, 0)]] + [[(dz, 0)] for dz in range(2, depth)]
        if width == 2:
            for dz in range(depth - 2):
                batches[dz + 1].append((dz, 1))
            batches.append([(depth - 2, 1), (depth - 1, 1)])
        while len(batches) > 8:
            batches = [sum(batches[at : at + 2], []) for at in range(0, len(batches), 2)]
        blocks = {(0, 0): stack([key_rows, value_rows], "pack")}
        queries = fetch(query_rows)
        state = []
        for dz in range(depth):
            block = blocks[dz, 0]
            if dz + 1 < depth:
                blocks[dz + 1, 0] = z_forward(block, grid, dz + 1)
            if width == 2:
                blocks[dz, 1] = y_swap(block, grid)
            while len(batches) > 1 and all(entry[0] + 2 * entry[1] <= dz for entry in batches[0]):
                state = phase(batches.pop(0), blocks, state, after=(dz - 1, 1) if width == 2 else None)
            if dz + 1 < depth:
                blocks[dz + 1, 0], state, queries = lax.optimization_barrier(
                    (blocks[dz + 1, 0], state, queries)
                )
        tied = batches[0]
        values, state = lax.optimization_barrier(([blocks[entry] for entry in tied], state))
        blocks.update(zip(tied, values))
        return phase(tied, blocks, state, last=True)

    spec = P(("groups", "tp"), None)
    return jax.shard_map(
        body, mesh=mesh, in_specs=(spec, spec, spec), out_specs=spec, check_vma=False
    )
```

```python
import functools
import math

import jax
import jax.numpy as jnp
from jax import lax
from jax.experimental import pallas as pl
from jax.experimental.pallas import tpu as pltpu
from jax.sharding import PartitionSpec as P

HEADS = 128
KV_HEADS = 8
GROUP = HEADS // KV_HEADS
PARTS = 8
STEP_HEADS = 2

masked_score = -1e30


def chip_grid(devices):
    if devices % 2:
        return devices, 1, 1
    chips = devices // 2
    if chips % 2 or chips > 8:
        return chips, 1, 2
    return chips // 2, 2, 2


def place(grid):
    depth, width, cores = grid
    me = lax.axis_index("tp")
    return me // (width * cores), (me // cores) % width, me % cores


def stack(arrays, name):
    def kernel(*refs):
        for at, ref in enumerate(refs[:-1]):
            refs[-1][at] = ref[...]

    count = len(arrays)
    return pl.pallas_call(
        kernel,
        out_shape=jax.ShapeDtypeStruct((count, *arrays[0].shape), arrays[0].dtype),
        in_specs=[pl.BlockSpec(memory_space=pltpu.VMEM)] * count,
        out_specs=pl.BlockSpec(memory_space=pltpu.VMEM),
        compiler_params=pltpu.CompilerParams(vmem_limit_bytes=4 * 2**20),
        name=name,
    )(*arrays)


def fetch(array):
    def kernel(array_ref, out_ref, sem):
        copy = pltpu.make_async_copy(array_ref, out_ref, sem)
        copy.start()
        copy.wait()

    return pl.pallas_call(
        kernel,
        out_shape=jax.ShapeDtypeStruct(array.shape, array.dtype),
        in_specs=[pl.BlockSpec(memory_space=pltpu.HBM)],
        out_specs=pl.BlockSpec(memory_space=pltpu.VMEM),
        scratch_shapes=[pltpu.SemaphoreType.DMA],
        compiler_params=pltpu.CompilerParams(vmem_limit_bytes=4 * 2**20),
        name="fetch",
    )(array)


def z_forward(block, grid, dz):
    depth, width, cores = grid
    side = width * cores
    pairs = []
    for z in range(depth):
        target = z ^ 1 if dz == depth - 1 and depth % 2 == 0 else (z + 1) % depth
        pairs += [(z * side + at, target * side + at) for at in range(side)]
    return lax.ppermute(block, "tp", pairs)


def y_swap(block, grid):
    depth, width, cores = grid
    return lax.ppermute(
        block, "tp", [(at, at ^ cores) for at in range(depth * width * cores)]
    )


def core_swap(blocks, grid):
    depth, width, cores = grid
    return lax.ppermute(blocks, "tp", [(at, at ^ 1) for at in range(depth * width * cores)])


def reciprocal(x):
    guess = pl.reciprocal(x, approx=True)
    return guess * (2.0 - x * guess)


def attend_kernel(grid, entries, kept, last, query_ref, *refs):
    depth, width, cores = grid
    count = len(entries)
    halves = 1 if last else 2
    own_refs, refs = refs[:count], refs[count:]
    core_refs, refs = refs[: halves * count], refs[halves * count :]
    kept_refs, refs = refs[: 2 * kept], refs[2 * kept :]
    out_refs, scratch = list(refs[: 2 - last]), list(refs[2 - last :])
    if last:
        result_ref = out_refs[0]
        out_refs[0], sems = scratch.pop(0), scratch.pop(0)
    tok = query_ref.shape[0]
    dim = own_refs[0].shape[-1] // KV_HEADS
    rows = GROUP * tok
    part_rows = rows // PARTS
    heads = part_rows // tok
    factor = dim ** (-0.5) * math.log2(math.e)
    zz, yy, cc = place(grid)

    pieces = []
    for at, (dz, dy) in enumerate(entries):
        pieces.append((dz, 0, dy, own_refs[at].at[0], own_refs[at].at[1]))
        if last:
            pieces.append((dz, 1, dy, core_refs[at].at[0], core_refs[at].at[1]))
        else:
            pieces.append((dz, 1, dy, *core_refs[2 * at : 2 * at + 2]))
    pieces.sort(key=lambda piece: piece[:3])

    if scratch:
        bias_ref = scratch[0]

        row = lax.broadcasted_iota(jnp.int32, (tok, tok), 0)
        key = lax.broadcasted_iota(jnp.int32, (tok, tok), 1)
        for at, (dz, dc, dy, _, _) in enumerate(pieces):
            if dz:
                limit = jnp.where(zz >= dz, 0, tok) + 0 * key
            elif dy:
                limit = jnp.where(yy == 1, 0, tok) + 0 * key
            elif dc:
                limit = jnp.where(cc == 1, 0, tok) + 0 * key
            else:
                limit = key
            bias_ref[:, at * tok : (at + 1) * tok] = jnp.where(limit <= row, 0.0, masked_score)

    def column(index):
        return pl.ds(pl.multiple_of(index * dim, dim), dim)

    def emit(head, part, sums, peak):
        here = slice(part * part_rows, (part + 1) * part_rows)
        if not last:
            out_refs[0][head, here, :] = sums
            out_refs[1][head, here, :] = jnp.broadcast_to(peak, (part_rows, dim))
            return
        result = (sums[:, :dim] * reciprocal(sums[:, dim:])).astype(out_refs[0].dtype)
        for index in range(heads):
            out_refs[0][:, column((head * PARTS + part) * heads + index)] = result[
                index * tok : (index + 1) * tok
            ]

    def attend(used, span):
        def one(head):
            span_of = column(head)
            keys = jnp.concatenate([piece[3][:, span_of] for piece in used], axis=0)
            values = jnp.concatenate([piece[4][:, span_of] for piece in used], axis=0)
            values = jnp.concatenate([values, jnp.ones_like(values)], axis=1)
            first_head = head * GROUP
            for part in range(PARTS):
                here = slice(part * part_rows, (part + 1) * part_rows)
                query = jnp.concatenate(
                    [
                        query_ref[:, column(first_head + index)]
                        for index in range(part * heads, (part + 1) * heads)
                    ],
                    axis=0,
                )
                scores = lax.dot_general(
                    query, keys, (((1,), (1,)), ((), ())), preferred_element_type=jnp.float32
                )
                if span:
                    first = scores[:, :span].reshape(heads, tok, span) + bias_ref[:, :span][None]
                    first = first.reshape(part_rows, span)
                    if span < scores.shape[1]:
                        first = jnp.concatenate([first, scores[:, span:]], axis=1)
                    scores = first
                peak = jnp.max(scores, axis=1, keepdims=True) * factor
                if kept:
                    before = kept_refs[1][head, here, :]
                    peak = jnp.maximum(jnp.broadcast_to(peak, before.shape), before)
                    shifted = jnp.concatenate(
                        [
                            scores[:, at : at + dim] * factor - peak
                            for at in range(0, scores.shape[1], dim)
                        ],
                        axis=1,
                    )
                else:
                    shifted = scores * factor - peak
                weights = jnp.exp2(shifted).astype(jnp.bfloat16)
                sums = jnp.dot(weights, values, preferred_element_type=jnp.float32)
                if kept:
                    carry = jnp.exp2(before - peak)
                    carry = jnp.concatenate([carry, carry], axis=1)
                    sums = sums + carry * kept_refs[0][head, here, :]
                emit(head, part, sums, peak)

        all_heads(one)

    def hand_on():
        def one(head):
            for part in range(PARTS):
                here = slice(part * part_rows, (part + 1) * part_rows)
                emit(head, part, kept_refs[0][head, here, :], kept_refs[1][head, here, :])

        all_heads(one)

    def out_copy(step):
        span = STEP_HEADS * GROUP * dim
        here = pl.ds(pl.multiple_of(step * span, span), span)
        return pltpu.make_async_copy(out_refs[0].at[:, here], result_ref.at[:, here], sems.at[step])

    def all_heads(one):
        @pl.loop(0, KV_HEADS // STEP_HEADS)
        def _(step):
            for index in range(STEP_HEADS):
                one(step * STEP_HEADS + index)
            if last:
                out_copy(step).start()

    near = tok * sum(piece[0] == 0 for piece in pieces)
    lowest, highest = pieces[0][0], pieces[-1][0]

    @pl.when(zz >= highest)
    def _():
        attend(pieces, near)

    if lowest < highest:

        @pl.when(jnp.logical_and(zz >= lowest, zz < highest))
        def _():
            attend(pieces, len(pieces) * tok)

    if lowest > 0:

        @pl.when(zz < lowest)
        def _():
            hand_on()

    if last:

        @pl.loop(0, KV_HEADS // STEP_HEADS)
        def _(step):
            out_copy(step).wait()


def solution(mesh):
    grid = chip_grid(mesh.shape["tp"])
    depth, width, cores = grid
    assert cores == 2 and depth > 2

    def body(query_rows, key_rows, value_rows):
        tok, columns = query_rows.shape
        dim = key_rows.shape[1] // KV_HEADS
        rows = GROUP * tok
        query_rows, key_rows, value_rows = (
            pltpu.with_memory_space_constraint(array, pltpu.HBM)
            for array in (query_rows, key_rows, value_rows)
        )
        whole = pl.BlockSpec(memory_space=pltpu.VMEM)
        state_shapes = [
            jax.ShapeDtypeStruct((KV_HEADS, rows, size), jnp.float32) for size in (2 * dim, dim)
        ]
        steps = KV_HEADS // STEP_HEADS

        swaps = {}

        def phase(entries, blocks, state, last=False, after=None):
            operands = [blocks[entry] for entry in entries]
            if last:
                operands += [
                    swaps[entry] if entry in swaps else core_swap(blocks[entry], grid) for entry in entries
                ]
            else:
                operands += [
                    core_swap(blocks[entry][half], grid) for entry in entries for half in range(2)
                ]
            if after:
                if dz + 1 == depth:
                    swaps[after] = core_swap(blocks[after], grid)
                    operands, swaps[after] = lax.optimization_barrier((operands, swaps[after]))
                else:
                    operands, blocks[after] = lax.optimization_barrier((operands, blocks[after]))
            keys = tok * 2 * len(entries)
            levels = {dz for dz, _ in entries}
            scratch = []
            if last:
                scratch += [pltpu.VMEM((tok, columns), query_rows.dtype)]
                scratch += [pltpu.SemaphoreType.DMA((steps,))]
            if 0 in levels or len(levels) > 1:
                scratch += [pltpu.VMEM((tok, keys), jnp.float32)]
            return pl.pallas_call(
                functools.partial(attend_kernel, grid, entries, bool(state), last),
                out_shape=query_rows if last else state_shapes,
                in_specs=[whole] * (1 + len(operands) + len(state)),
                out_specs=pl.BlockSpec(memory_space=pltpu.HBM) if last else [whole] * 2,
                scratch_shapes=scratch,
                input_output_aliases={} if last or not state else {1 + len(operands) + at: at for at in range(2)},
                compiler_params=pltpu.CompilerParams(vmem_limit_bytes=16 * 2**20),
                cost_estimate=pl.CostEstimate(flops=1000, bytes_accessed=1000, transcendentals=0),
                name="attend_last" if last else f"attend_{entries[0][0]}",
            )(queries, *operands, *state)

        batches = [[(0, 0), (1, 0)]] + [[(dz, 0)] for dz in range(2, depth)]
        if width == 2:
            for dz in range(depth - 2):
                batches[dz + 1].append((dz, 1))
            batches.append([(depth - 2, 1), (depth - 1, 1)])
        while len(batches) > 8:
            batches = [sum(batches[at : at + 2], []) for at in range(0, len(batches), 2)]
        blocks = {(0, 0): stack([key_rows, value_rows], "pack")}
        queries = fetch(query_rows)
        state = []
        for dz in range(depth):
            block = blocks[dz, 0]
            if dz + 1 < depth:
                blocks[dz + 1, 0] = z_forward(block, grid, dz + 1)
            if width == 2:
                blocks[dz, 1] = y_swap(block, grid)
            while len(batches) > 1 and all(entry[0] + 2 * entry[1] <= dz for entry in batches[0]):
                state = phase(batches.pop(0), blocks, state, after=(dz - 1, 1) if width == 2 else None)
            if dz + 1 < depth:
                blocks[dz + 1, 0], state, queries = lax.optimization_barrier(
                    (blocks[dz + 1, 0], state, queries)
                )
        tied = batches[0]
        values, state = lax.optimization_barrier(([blocks[entry] for entry in tied], state))
        blocks.update(zip(tied, values))
        return phase(tied, blocks, state, last=True)

    spec = P(("groups", "tp"), None)
    return jax.shard_map(
        body, mesh=mesh, in_specs=(spec, spec, spec), out_specs=spec, check_vma=False
    )
```

```python
import functools
import math

import jax
import jax.numpy as jnp
from jax import lax
from jax.experimental import pallas as pl
from jax.experimental.pallas import tpu as pltpu
from jax.sharding import PartitionSpec as P

HEADS = 128
KV_HEADS = 8
GROUP = HEADS // KV_HEADS
PARTS = 8
STEP_HEADS = 2

masked_score = -1e30


def chip_grid(devices):
    if devices % 2:
        return devices, 1, 1
    chips = devices // 2
    if chips % 2 or chips > 8:
        return chips, 1, 2
    return chips // 2, 2, 2


def place(grid):
    depth, width, cores = grid
    me = lax.axis_index("tp")
    return me // (width * cores), (me // cores) % width, me % cores


def stack(arrays, name):
    def kernel(*refs):
        for at, ref in enumerate(refs[:-1]):
            refs[-1][at] = ref[...]

    count = len(arrays)
    return pl.pallas_call(
        kernel,
        out_shape=jax.ShapeDtypeStruct((count, *arrays[0].shape), arrays[0].dtype),
        in_specs=[pl.BlockSpec(memory_space=pltpu.VMEM)] * count,
        out_specs=pl.BlockSpec(memory_space=pltpu.VMEM),
        compiler_params=pltpu.CompilerParams(vmem_limit_bytes=4 * 2**20),
        name=name,
    )(*arrays)


def fetch(array):
    def kernel(array_ref, out_ref, sem):
        copy = pltpu.make_async_copy(array_ref, out_ref, sem)
        copy.start()
        copy.wait()

    return pl.pallas_call(
        kernel,
        out_shape=jax.ShapeDtypeStruct(array.shape, array.dtype),
        in_specs=[pl.BlockSpec(memory_space=pltpu.HBM)],
        out_specs=pl.BlockSpec(memory_space=pltpu.VMEM),
        scratch_shapes=[pltpu.SemaphoreType.DMA],
        compiler_params=pltpu.CompilerParams(vmem_limit_bytes=4 * 2**20),
        name="fetch",
    )(array)


def z_forward(block, grid, dz):
    depth, width, cores = grid
    side = width * cores
    pairs = []
    for z in range(depth):
        target = z ^ 1 if dz == depth - 1 and depth % 2 == 0 else (z + 1) % depth
        pairs += [(z * side + at, target * side + at) for at in range(side)]
    return lax.ppermute(block, "tp", pairs)


def y_swap(block, grid):
    depth, width, cores = grid
    return lax.ppermute(
        block, "tp", [(at, at ^ cores) for at in range(depth * width * cores)]
    )


def core_swap(blocks, grid):
    depth, width, cores = grid
    return lax.ppermute(blocks, "tp", [(at, at ^ 1) for at in range(depth * width * cores)])


def reciprocal(x):
    guess = pl.reciprocal(x, approx=True)
    return guess * (2.0 - x * guess)


def attend_kernel(grid, sources, kept, last, query_ref, *refs):
    depth, width, cores = grid
    blocks_refs, refs = refs[: len(sources)], refs[len(sources) :]
    kept_refs, refs = refs[: 2 * kept], refs[2 * kept :]
    out_refs, scratch = list(refs[: 2 - last]), list(refs[2 - last :])
    if last:
        result_ref = out_refs[0]
        out_refs[0], sems = scratch.pop(0), scratch.pop(0)
    tok = query_ref.shape[0]
    dim = blocks_refs[0].shape[-1] // KV_HEADS
    rows = GROUP * tok
    part_rows = rows // PARTS
    heads = part_rows // tok
    factor = dim ** (-0.5) * math.log2(math.e)
    zz, yy, cc = place(grid)

    pieces = []
    for places, ref in zip(sources, blocks_refs):
        for (dz, dy, dc), at in places:
            pieces.append((dz, dc, dy, ref.at[0], ref.at[1]))
    pieces.sort(key=lambda piece: piece[:3])

    if scratch:
        bias_ref = scratch[0]

        row = lax.broadcasted_iota(jnp.int32, (tok, tok), 0)
        key = lax.broadcasted_iota(jnp.int32, (tok, tok), 1)
        for at, (dz, dc, dy, _, _) in enumerate(pieces):
            if dz:
                limit = jnp.where(zz >= dz, 0, tok) + 0 * key
            elif dy:
                limit = jnp.where(yy == 1, 0, tok) + 0 * key
            elif dc:
                limit = jnp.where(cc == 1, 0, tok) + 0 * key
            else:
                limit = key
            bias_ref[:, at * tok : (at + 1) * tok] = jnp.where(limit <= row, 0.0, masked_score)

    def column(index):
        return pl.ds(pl.multiple_of(index * dim, dim), dim)

    def emit(head, part, sums, peak):
        here = slice(part * part_rows, (part + 1) * part_rows)
        if not last:
            out_refs[0][head, here, :] = sums
            out_refs[1][head, here, :] = jnp.broadcast_to(peak, (part_rows, dim))
            return
        result = (sums[:, :dim] * reciprocal(sums[:, dim:])).astype(out_refs[0].dtype)
        for index in range(heads):
            out_refs[0][:, column((head * PARTS + part) * heads + index)] = result[
                index * tok : (index + 1) * tok
            ]

    def attend(used, span):
        def one(head):
            span_of = column(head)
            keys = jnp.concatenate([piece[3][:, span_of] for piece in used], axis=0)
            values = jnp.concatenate([piece[4][:, span_of] for piece in used], axis=0)
            values = jnp.concatenate([values, jnp.ones_like(values)], axis=1)
            first_head = head * GROUP
            for part in range(PARTS):
                here = slice(part * part_rows, (part + 1) * part_rows)
                query = jnp.concatenate(
                    [
                        query_ref[:, column(first_head + index)]
                        for index in range(part * heads, (part + 1) * heads)
                    ],
                    axis=0,
                )
                scores = lax.dot_general(
                    query, keys, (((1,), (1,)), ((), ())), preferred_element_type=jnp.float32
                )
                if span:
                    first = scores[:, :span].reshape(heads, tok, span) + bias_ref[:, :span][None]
                    first = first.reshape(part_rows, span)
                    if span < scores.shape[1]:
                        first = jnp.concatenate([first, scores[:, span:]], axis=1)
                    scores = first
                peak = jnp.max(scores, axis=1, keepdims=True) * factor
                if kept:
                    before = kept_refs[1][head, here, :]
                    peak = jnp.maximum(jnp.broadcast_to(peak, before.shape), before)
                    shifted = jnp.concatenate(
                        [
                            scores[:, at : at + dim] * factor - peak[:, : scores.shape[1] - at]
                            for at in range(0, scores.shape[1], dim)
                        ],
                        axis=1,
                    )
                else:
                    shifted = scores * factor - peak
                weights = jnp.exp2(shifted).astype(jnp.bfloat16)
                sums = jnp.dot(weights, values, preferred_element_type=jnp.float32)
                if kept:
                    carry = jnp.exp2(before - peak)
                    carry = jnp.concatenate([carry, carry], axis=1)
                    sums = sums + carry * kept_refs[0][head, here, :]
                emit(head, part, sums, peak)

        all_heads(one)

    def hand_on():
        def one(head):
            for part in range(PARTS):
                here = slice(part * part_rows, (part + 1) * part_rows)
                emit(head, part, kept_refs[0][head, here, :], kept_refs[1][head, here, :])

        all_heads(one)

    def out_copy(step):
        span = STEP_HEADS * GROUP * dim
        here = pl.ds(pl.multiple_of(step * span, span), span)
        return pltpu.make_async_copy(out_refs[0].at[:, here], result_ref.at[:, here], sems.at[step])

    def all_heads(one):
        @pl.loop(0, KV_HEADS // STEP_HEADS)
        def _(step):
            for index in range(STEP_HEADS):
                one(step * STEP_HEADS + index)
            if last:
                out_copy(step).start()

    near = tok * sum(piece[0] == 0 for piece in pieces)
    near = min(-(-near // dim) * dim, len(pieces) * tok)
    lowest, highest = pieces[0][0], pieces[-1][0]

    @pl.when(zz >= highest)
    def _():
        attend(pieces, near)

    if lowest < highest:

        @pl.when(jnp.logical_and(zz >= lowest, zz < highest))
        def _():
            attend(pieces, len(pieces) * tok)

    if lowest > 0:

        @pl.when(zz < lowest)
        def _():
            hand_on()

    if last:

        @pl.loop(0, KV_HEADS // STEP_HEADS)
        def _(step):
            out_copy(step).wait()


def solution(mesh):
    grid = chip_grid(mesh.shape["tp"])
    depth, width, cores = grid
    assert cores == 2 and depth > 2

    def body(query_rows, key_rows, value_rows):
        tok, columns = query_rows.shape
        dim = key_rows.shape[1] // KV_HEADS
        rows = GROUP * tok
        query_rows, key_rows, value_rows = (
            pltpu.with_memory_space_constraint(array, pltpu.HBM)
            for array in (query_rows, key_rows, value_rows)
        )
        whole = pl.BlockSpec(memory_space=pltpu.VMEM)
        state_shapes = [
            jax.ShapeDtypeStruct((KV_HEADS, rows, size), jnp.float32) for size in (2 * dim, dim)
        ]
        steps = KV_HEADS // STEP_HEADS

        arrays, found = {}, {}

        def keep(name, array, places):
            arrays[name] = array
            found.update({place: (name, at) for at, place in enumerate(places)})

        def phase(places, state, last=False):
            names = list(dict.fromkeys(found[place][0] for place in places))
            sources = [
                [(place, found[place][1]) for place in places if found[place][0] == name]
                for name in names
            ]
            operands = [arrays[name] for name in names]
            keys = tok * len(places)
            levels = {dz for dz, _, _ in places}
            scratch = []
            if last:
                scratch += [pltpu.VMEM((tok, columns), query_rows.dtype)]
                scratch += [pltpu.SemaphoreType.DMA((steps,))]
            if 0 in levels or len(levels) > 1:
                scratch += [pltpu.VMEM((tok, keys), jnp.float32)]
            return pl.pallas_call(
                functools.partial(attend_kernel, grid, sources, bool(state), last),
                out_shape=query_rows if last else state_shapes,
                in_specs=[whole] * (1 + len(operands) + len(state)),
                out_specs=pl.BlockSpec(memory_space=pltpu.HBM) if last else [whole] * 2,
                scratch_shapes=scratch,
                input_output_aliases={}
                if last or not state
                else {1 + len(operands) + at: at for at in range(2)},
                compiler_params=pltpu.CompilerParams(vmem_limit_bytes=16 * 2**20),
                cost_estimate=pl.CostEstimate(flops=1000, bytes_accessed=1000, transcendentals=0),
                name="attend_last" if last else "attend",
            )(queries, *operands, *state)

        batches = []
        for dz in range(1, depth):
            batches.append([(dz, 0, 0), (dz - 1, 0, 1)])
            if width == 2:
                batches[-1] += [(dz - 1, 1, 0)] + [(dz - 2, 1, 1)] * (dz > 1)
        batches[0].append((0, 0, 0))
        final = [(depth - 1, 0, 1)]
        if width == 2:
            final += [(depth - 1, 1, 0), (depth - 2, 1, 1), (depth - 1, 1, 1)]
        while len(batches) > 8:
            batches = [sum(batches[at : at + 2], []) for at in range(0, len(batches), 2)]

        keep("z0", stack([key_rows, value_rows], "pack"), [(0, 0, 0)])
        queries = fetch(query_rows)
        state = []
        for dz in range(depth):
            block = arrays[f"z{dz}"]
            if dz + 1 < depth:
                keep(f"z{dz + 1}", z_forward(block, grid, dz + 1), [(dz + 1, 0, 0)])
            if width == 2:
                keep(f"y{dz}", y_swap(block, grid), [(dz, 1, 0)])
            if dz and all(place in found for place in batches[0]):
                state = phase(batches.pop(0), state)
            keep(f"c{dz}", core_swap(block, grid), [(dz, 0, 1)])
            if dz and width == 2:
                keep(f"d{dz}", core_swap(arrays[f"y{dz - 1}"], grid), [(dz - 1, 1, 1)])
            if dz + 1 < depth:
                tied = [f"z{dz + 1}"]
                values, state, queries = lax.optimization_barrier(
                    ([arrays[name] for name in tied], state, queries)
                )
                arrays.update(zip(tied, values))
        if width == 2:
            block, state = lax.optimization_barrier((arrays[f"y{depth - 1}"], state))
            arrays[f"y{depth - 1}"] = block
            keep("c", core_swap(block, grid), [(depth - 1, 1, 1)])
        return phase(final, state, last=True)

    spec = P(("groups", "tp"), None)
    return jax.shard_map(
        body, mesh=mesh, in_specs=(spec, spec, spec), out_specs=spec, check_vma=False
    )
```

```python
import functools
import math

import jax
import jax.numpy as jnp
from jax import lax
from jax.experimental import pallas as pl
from jax.experimental.pallas import tpu as pltpu
from jax.sharding import PartitionSpec as P

HEADS = 128
KV_HEADS = 8
GROUP = HEADS // KV_HEADS
PARTS = 8
STEP_HEADS = 2

masked_score = -1e30


def chip_grid(devices):
    if devices % 2:
        return devices, 1, 1
    chips = devices // 2
    if chips % 2 or chips > 8:
        return chips, 1, 2
    return chips // 2, 2, 2


def place(grid):
    depth, width, cores = grid
    me = lax.axis_index("tp")
    return me // (width * cores), (me // cores) % width, me % cores


def stack(arrays, name):
    def kernel(*refs):
        for at, ref in enumerate(refs[:-1]):
            refs[-1][at] = ref[...]

    count = len(arrays)
    return pl.pallas_call(
        kernel,
        out_shape=jax.ShapeDtypeStruct((count, *arrays[0].shape), arrays[0].dtype),
        in_specs=[pl.BlockSpec(memory_space=pltpu.VMEM)] * count,
        out_specs=pl.BlockSpec(memory_space=pltpu.VMEM),
        compiler_params=pltpu.CompilerParams(vmem_limit_bytes=4 * 2**20),
        name=name,
    )(*arrays)


def fetch(array):
    def kernel(array_ref, out_ref, sem):
        copy = pltpu.make_async_copy(array_ref, out_ref, sem)
        copy.start()
        copy.wait()

    return pl.pallas_call(
        kernel,
        out_shape=jax.ShapeDtypeStruct(array.shape, array.dtype),
        in_specs=[pl.BlockSpec(memory_space=pltpu.HBM)],
        out_specs=pl.BlockSpec(memory_space=pltpu.VMEM),
        scratch_shapes=[pltpu.SemaphoreType.DMA],
        compiler_params=pltpu.CompilerParams(vmem_limit_bytes=4 * 2**20),
        name="fetch",
    )(array)


def z_forward(block, grid, dz):
    depth, width, cores = grid
    side = width * cores
    pairs = []
    for z in range(depth):
        target = z ^ 1 if dz == depth - 1 and depth % 2 == 0 else (z + 1) % depth
        pairs += [(z * side + at, target * side + at) for at in range(side)]
    return lax.ppermute(block, "tp", pairs)


def y_swap(block, grid):
    depth, width, cores = grid
    return lax.ppermute(
        block, "tp", [(at, at ^ cores) for at in range(depth * width * cores)]
    )


def far_swap(block, grid, groups):
    depth, width, cores = grid
    count = depth * width * cores
    pairs = []
    for group in range(groups):
        for at in range(count):
            z, side = divmod(at, width * cores)
            if z in (0, depth - 1):
                target = group * count + (depth - 1 - z) * width * cores + (side ^ cores)
            else:
                target = (group ^ 1) * count + at
            pairs.append((group * count + at, target))
    return lax.ppermute(block, ("groups", "tp"), pairs)


def core_swap(blocks, grid):
    depth, width, cores = grid
    return lax.ppermute(blocks, "tp", [(at, at ^ 1) for at in range(depth * width * cores)])


def reciprocal(x):
    guess = pl.reciprocal(x, approx=True)
    return guess * (2.0 - x * guess)


def attend_kernel(grid, sources, kept, last, query_ref, *refs):
    depth, width, cores = grid
    blocks_refs, refs = refs[: len(sources)], refs[len(sources) :]
    kept_refs, refs = refs[: 2 * kept], refs[2 * kept :]
    out_refs, scratch = list(refs[: 2 - last]), list(refs[2 - last :])
    if last:
        result_ref = out_refs[0]
        out_refs[0], sems = scratch.pop(0), scratch.pop(0)
    tok = query_ref.shape[0]
    dim = blocks_refs[0].shape[-1] // KV_HEADS
    rows = GROUP * tok
    part_rows = rows // PARTS
    heads = part_rows // tok
    factor = dim ** (-0.5) * math.log2(math.e)
    zz, yy, cc = place(grid)

    pieces = []
    for places, ref in zip(sources, blocks_refs):
        for (dz, dy, dc), at in places:
            pieces.append((dz, dc, dy, ref.at[0], ref.at[1]))
    pieces.sort(key=lambda piece: piece[:3])

    if scratch:
        bias_ref = scratch[0]

        row = lax.broadcasted_iota(jnp.int32, (tok, tok), 0)
        key = lax.broadcasted_iota(jnp.int32, (tok, tok), 1)
        for at, (dz, dc, dy, _, _) in enumerate(pieces):
            if dz:
                limit = jnp.where(zz >= dz, 0, tok) + 0 * key
            elif dy:
                limit = jnp.where(yy == 1, 0, tok) + 0 * key
            elif dc:
                limit = jnp.where(cc == 1, 0, tok) + 0 * key
            else:
                limit = key
            bias_ref[:, at * tok : (at + 1) * tok] = jnp.where(limit <= row, 0.0, masked_score)

    def column(index):
        return pl.ds(pl.multiple_of(index * dim, dim), dim)

    def emit(head, part, sums, peak):
        here = slice(part * part_rows, (part + 1) * part_rows)
        if not last:
            out_refs[0][head, here, :] = sums
            out_refs[1][head, here, :] = jnp.broadcast_to(peak, (part_rows, dim))
            return
        result = (sums[:, :dim] * reciprocal(sums[:, dim:])).astype(out_refs[0].dtype)
        for index in range(heads):
            out_refs[0][:, column((head * PARTS + part) * heads + index)] = result[
                index * tok : (index + 1) * tok
            ]

    def attend(used, span):
        def one(head):
            span_of = column(head)
            keys = jnp.concatenate([piece[3][:, span_of] for piece in used], axis=0)
            values = jnp.concatenate([piece[4][:, span_of] for piece in used], axis=0)
            values = jnp.concatenate([values, jnp.ones_like(values)], axis=1)
            first_head = head * GROUP
            for part in range(PARTS):
                here = slice(part * part_rows, (part + 1) * part_rows)
                query = jnp.concatenate(
                    [
                        query_ref[:, column(first_head + index)]
                        for index in range(part * heads, (part + 1) * heads)
                    ],
                    axis=0,
                )
                scores = lax.dot_general(
                    query, keys, (((1,), (1,)), ((), ())), preferred_element_type=jnp.float32
                )
                if span:
                    first = scores[:, :span].reshape(heads, tok, span) + bias_ref[:, :span][None]
                    first = first.reshape(part_rows, span)
                    if span < scores.shape[1]:
                        first = jnp.concatenate([first, scores[:, span:]], axis=1)
                    scores = first
                peak = jnp.max(scores, axis=1, keepdims=True) * factor
                if kept:
                    before = kept_refs[1][head, here, :]
                    peak = jnp.maximum(jnp.broadcast_to(peak, before.shape), before)
                    shifted = jnp.concatenate(
                        [
                            scores[:, at : at + dim] * factor - peak[:, : scores.shape[1] - at]
                            for at in range(0, scores.shape[1], dim)
                        ],
                        axis=1,
                    )
                else:
                    shifted = scores * factor - peak
                weights = jnp.exp2(shifted).astype(jnp.bfloat16)
                sums = jnp.dot(weights, values, preferred_element_type=jnp.float32)
                if kept:
                    carry = jnp.exp2(before - peak)
                    carry = jnp.concatenate([carry, carry], axis=1)
                    sums = sums + carry * kept_refs[0][head, here, :]
                emit(head, part, sums, peak)

        all_heads(one)

    def hand_on():
        def one(head):
            for part in range(PARTS):
                here = slice(part * part_rows, (part + 1) * part_rows)
                emit(head, part, kept_refs[0][head, here, :], kept_refs[1][head, here, :])

        all_heads(one)

    def out_copy(step):
        span = STEP_HEADS * GROUP * dim
        here = pl.ds(pl.multiple_of(step * span, span), span)
        return pltpu.make_async_copy(out_refs[0].at[:, here], result_ref.at[:, here], sems.at[step])

    def all_heads(one):
        @pl.loop(0, KV_HEADS // STEP_HEADS)
        def _(step):
            for index in range(STEP_HEADS):
                one(step * STEP_HEADS + index)
            if last:
                out_copy(step).start()

    near = tok * sum(piece[0] == 0 for piece in pieces)
    near = min(-(-near // dim) * dim, len(pieces) * tok)
    lowest, highest = pieces[0][0], pieces[-1][0]

    @pl.when(zz >= highest)
    def _():
        attend(pieces, near)

    if lowest < highest:

        @pl.when(jnp.logical_and(zz >= lowest, zz < highest))
        def _():
            attend(pieces, len(pieces) * tok)

    if lowest > 0:

        @pl.when(zz < lowest)
        def _():
            hand_on()

    if last:

        @pl.loop(0, KV_HEADS // STEP_HEADS)
        def _(step):
            out_copy(step).wait()


def solution(mesh):
    grid = chip_grid(mesh.shape["tp"])
    depth, width, cores = grid
    groups = mesh.shape["groups"]
    assert cores == 2 and depth > 2
    straight = width == 2 and groups % 2 == 0
    assert straight or width == 1

    def body(query_rows, key_rows, value_rows):
        tok, columns = query_rows.shape
        dim = key_rows.shape[1] // KV_HEADS
        rows = GROUP * tok
        query_rows, key_rows, value_rows = (
            pltpu.with_memory_space_constraint(array, pltpu.HBM)
            for array in (query_rows, key_rows, value_rows)
        )
        whole = pl.BlockSpec(memory_space=pltpu.VMEM)
        state_shapes = [
            jax.ShapeDtypeStruct((KV_HEADS, rows, size), jnp.float32) for size in (2 * dim, dim)
        ]
        steps = KV_HEADS // STEP_HEADS

        arrays, found = {}, {}

        def keep(name, array, places):
            arrays[name] = array
            found.update({place: (name, at) for at, place in enumerate(places)})

        def phase(places, state, last=False):
            names = list(dict.fromkeys(found[place][0] for place in places))
            sources = [
                [(place, found[place][1]) for place in places if found[place][0] == name]
                for name in names
            ]
            operands = [arrays[name] for name in names]
            keys = tok * len(places)
            levels = {dz for dz, _, _ in places}
            scratch = []
            if last:
                scratch += [pltpu.VMEM((tok, columns), query_rows.dtype)]
                scratch += [pltpu.SemaphoreType.DMA((steps,))]
            if 0 in levels or len(levels) > 1:
                scratch += [pltpu.VMEM((tok, keys), jnp.float32)]
            return pl.pallas_call(
                functools.partial(attend_kernel, grid, sources, bool(state), last),
                out_shape=query_rows if last else state_shapes,
                in_specs=[whole] * (1 + len(operands) + len(state)),
                out_specs=pl.BlockSpec(memory_space=pltpu.HBM) if last else [whole] * 2,
                scratch_shapes=scratch,
                input_output_aliases={}
                if last or not state
                else {1 + len(operands) + at: at for at in range(2)},
                compiler_params=pltpu.CompilerParams(vmem_limit_bytes=16 * 2**20),
                cost_estimate=pl.CostEstimate(flops=1000, bytes_accessed=1000, transcendentals=0),
                name="attend_last" if last else "attend",
            )(queries, *operands, *state)

        batches = []
        for dz in range(1, depth):
            batches.append([(dz, 0, 0), (dz - 1, 0, 1)])
            if width == 2:
                batches[-1] += [(dz - 1, 1, 0)] + [(dz - 2, 1, 1)] * (dz > 1)
        batches[0].append((0, 0, 0))
        final = [(depth - 1, 0, 1)]
        if straight:
            final += [(depth - 1, 0, 0), (depth - 2, 1, 0), (depth - 2, 1, 1)]
            batches[-1] = [(depth - 1, 1, 0), (depth - 1, 1, 1), (depth - 2, 0, 1), (depth - 3, 1, 1)]
        while len(batches) > 8:
            batches = [sum(batches[at : at + 2], []) for at in range(0, len(batches), 2)]

        keep("z0", stack([key_rows, value_rows], "pack"), [(0, 0, 0)])
        queries = fetch(query_rows)
        state = []
        for dz in range(depth):
            block = arrays[f"z{dz}"]
            if dz + 1 < depth:
                keep(f"z{dz + 1}", z_forward(block, grid, dz + 1), [(dz + 1, 0, 0)])
            if straight and dz + 1 < depth:
                keep(f"y{dz}", y_swap(block, grid), [(dz, 1, 0)])
            if straight and dz == 0:
                keep("w", far_swap(block, grid, groups), [(depth - 1, 1, 0)])
            if straight and dz == 1:
                keep("cw", core_swap(arrays["w"], grid), [(depth - 1, 1, 1)])
            if dz and all(place in found for place in batches[0]):
                state = phase(batches.pop(0), state)
            keep(f"c{dz}", core_swap(block, grid), [(dz, 0, 1)])
            if dz and straight:
                keep(f"d{dz}", core_swap(arrays[f"y{dz - 1}"], grid), [(dz - 1, 1, 1)])
            if dz + 1 < depth:
                tied = [f"z{dz + 1}"]
                values, state, queries = lax.optimization_barrier(
                    ([arrays[name] for name in tied], state, queries)
                )
                arrays.update(zip(tied, values))
        return phase(final, state, last=True)

    spec = P(("groups", "tp"), None)
    return jax.shard_map(
        body, mesh=mesh, in_specs=(spec, spec, spec), out_specs=spec, check_vma=False
    )
```

```python
import functools
import math

import jax
import jax.numpy as jnp
from jax import lax
from jax.experimental import pallas as pl
from jax.experimental.pallas import tpu as pltpu
from jax.sharding import PartitionSpec as P

HEADS = 128
KV_HEADS = 8
GROUP = HEADS // KV_HEADS
PARTS = 8
STEP_HEADS = 2

masked_score = -1e30


def chip_grid(devices):
    if devices % 2:
        return devices, 1, 1
    chips = devices // 2
    if chips % 2 or chips > 8:
        return chips, 1, 2
    return chips // 2, 2, 2


def place(grid):
    depth, width, cores = grid
    me = lax.axis_index("tp")
    return me // (width * cores), (me // cores) % width, me % cores


def stack(arrays, name):
    def kernel(*refs):
        for at, ref in enumerate(refs[:-1]):
            refs[-1][at] = ref[...]

    count = len(arrays)
    return pl.pallas_call(
        kernel,
        out_shape=jax.ShapeDtypeStruct((count, *arrays[0].shape), arrays[0].dtype),
        in_specs=[pl.BlockSpec(memory_space=pltpu.VMEM)] * count,
        out_specs=pl.BlockSpec(memory_space=pltpu.VMEM),
        compiler_params=pltpu.CompilerParams(vmem_limit_bytes=4 * 2**20),
        name=name,
    )(*arrays)


def fetch(array):
    def kernel(array_ref, out_ref, sem):
        copy = pltpu.make_async_copy(array_ref, out_ref, sem)
        copy.start()
        copy.wait()

    return pl.pallas_call(
        kernel,
        out_shape=jax.ShapeDtypeStruct(array.shape, array.dtype),
        in_specs=[pl.BlockSpec(memory_space=pltpu.HBM)],
        out_specs=pl.BlockSpec(memory_space=pltpu.VMEM),
        scratch_shapes=[pltpu.SemaphoreType.DMA],
        compiler_params=pltpu.CompilerParams(vmem_limit_bytes=4 * 2**20),
        name="fetch",
    )(array)


def z_forward(block, grid, dz):
    depth, width, cores = grid
    side = width * cores
    pairs = []
    for z in range(depth):
        target = z ^ 1 if dz == depth - 1 and depth % 2 == 0 else (z + 1) % depth
        pairs += [(z * side + at, target * side + at) for at in range(side)]
    return lax.ppermute(block, "tp", pairs)


def y_swap(block, grid):
    depth, width, cores = grid
    return lax.ppermute(
        block, "tp", [(at, at ^ cores) for at in range(depth * width * cores)]
    )


def far_swap(block, grid, groups):
    depth, width, cores = grid
    count = depth * width * cores
    pairs = []
    for group in range(groups):
        for at in range(count):
            z, side = divmod(at, width * cores)
            if z in (0, depth - 1):
                target = group * count + (depth - 1 - z) * width * cores + (side ^ cores)
            else:
                target = (group ^ 1) * count + at
            pairs.append((group * count + at, target))
    return lax.ppermute(block, ("groups", "tp"), pairs)


def core_swap(blocks, grid):
    depth, width, cores = grid
    return lax.ppermute(blocks, "tp", [(at, at ^ 1) for at in range(depth * width * cores)])


def reciprocal(x):
    guess = pl.reciprocal(x, approx=True)
    return guess * (2.0 - x * guess)


def attend_kernel(grid, sources, kept, last, query_ref, *refs):
    depth, width, cores = grid
    blocks_refs, refs = refs[: len(sources)], refs[len(sources) :]
    kept_refs, refs = refs[: 2 * kept], refs[2 * kept :]
    out_refs, scratch = list(refs[: 2 - last]), list(refs[2 - last :])
    if last:
        result_ref = out_refs[0]
        out_refs[0], sems = scratch.pop(0), scratch.pop(0)
    tok = query_ref.shape[0]
    dim = blocks_refs[0].shape[-1] // KV_HEADS
    rows = GROUP * tok
    part_rows = rows // PARTS
    heads = part_rows // tok
    factor = dim ** (-0.5) * math.log2(math.e)
    zz, yy, cc = place(grid)

    pieces = []
    for places, ref in zip(sources, blocks_refs):
        for (dz, dy, dc), at in places:
            pieces.append((dz, dc, dy, ref.at[0], ref.at[1]))
    pieces.sort(key=lambda piece: piece[:3])

    if scratch:
        bias_ref = scratch[0]

        row = lax.broadcasted_iota(jnp.int32, (tok, tok), 0)
        key = lax.broadcasted_iota(jnp.int32, (tok, tok), 1)
        for at, (dz, dc, dy, _, _) in enumerate(pieces):
            if dz:
                limit = jnp.where(zz >= dz, 0, tok) + 0 * key
            elif dy:
                limit = jnp.where(yy == 1, 0, tok) + 0 * key
            elif dc:
                limit = jnp.where(cc == 1, 0, tok) + 0 * key
            else:
                limit = key
            bias_ref[:, at * tok : (at + 1) * tok] = jnp.where(limit <= row, 0.0, masked_score)

    def column(index):
        return pl.ds(pl.multiple_of(index * dim, dim), dim)

    def emit(head, part, sums, peak):
        here = slice(part * part_rows, (part + 1) * part_rows)
        if not last:
            out_refs[0][head, here, :] = sums
            out_refs[1][head, here, :] = jnp.broadcast_to(peak, (part_rows, dim))
            return
        result = (sums[:, :dim] * reciprocal(sums[:, dim:])).astype(out_refs[0].dtype)
        for index in range(heads):
            out_refs[0][:, column((head * PARTS + part) * heads + index)] = result[
                index * tok : (index + 1) * tok
            ]

    def attend(used, span):
        def one(head):
            span_of = column(head)
            keys = jnp.concatenate([piece[3][:, span_of] for piece in used], axis=0)
            values = jnp.concatenate([piece[4][:, span_of] for piece in used], axis=0)
            values = jnp.concatenate([values, jnp.ones_like(values)], axis=1)
            first_head = head * GROUP
            for part in range(PARTS):
                here = slice(part * part_rows, (part + 1) * part_rows)
                query = jnp.concatenate(
                    [
                        query_ref[:, column(first_head + index)]
                        for index in range(part * heads, (part + 1) * heads)
                    ],
                    axis=0,
                )
                scores = lax.dot_general(
                    query, keys, (((1,), (1,)), ((), ())), preferred_element_type=jnp.float32
                )
                if span:
                    first = scores[:, :span].reshape(heads, tok, span) + bias_ref[:, :span][None]
                    first = first.reshape(part_rows, span)
                    if span < scores.shape[1]:
                        first = jnp.concatenate([first, scores[:, span:]], axis=1)
                    scores = first
                peak = jnp.max(scores, axis=1, keepdims=True) * factor
                if kept:
                    before = kept_refs[1][head, here, :]
                    peak = jnp.maximum(jnp.broadcast_to(peak, before.shape), before)
                    shifted = jnp.concatenate(
                        [
                            scores[:, at : at + dim] * factor - peak[:, : scores.shape[1] - at]
                            for at in range(0, scores.shape[1], dim)
                        ],
                        axis=1,
                    )
                else:
                    shifted = scores * factor - peak
                weights = jnp.exp2(shifted).astype(jnp.bfloat16)
                sums = jnp.dot(weights, values, preferred_element_type=jnp.float32)
                if kept:
                    carry = jnp.exp2(before - peak)
                    carry = jnp.concatenate([carry, carry], axis=1)
                    sums = sums + carry * kept_refs[0][head, here, :]
                emit(head, part, sums, peak)

        all_heads(one)

    def hand_on():
        def one(head):
            for part in range(PARTS):
                here = slice(part * part_rows, (part + 1) * part_rows)
                emit(head, part, kept_refs[0][head, here, :], kept_refs[1][head, here, :])

        all_heads(one)

    def out_copy(step):
        span = STEP_HEADS * GROUP * dim
        here = pl.ds(pl.multiple_of(step * span, span), span)
        return pltpu.make_async_copy(out_refs[0].at[:, here], result_ref.at[:, here], sems.at[step])

    def all_heads(one):
        @pl.loop(0, KV_HEADS // STEP_HEADS)
        def _(step):
            for index in range(STEP_HEADS):
                one(step * STEP_HEADS + index)
            if last:
                out_copy(step).start()

    near = tok * sum(piece[0] == 0 for piece in pieces)
    near = min(-(-near // dim) * dim, len(pieces) * tok)
    lowest, highest = pieces[0][0], pieces[-1][0]

    @pl.when(zz >= highest)
    def _():
        attend(pieces, near)

    if lowest < highest:

        @pl.when(jnp.logical_and(zz >= lowest, zz < highest))
        def _():
            attend(pieces, len(pieces) * tok)

    if lowest > 0:

        @pl.when(zz < lowest)
        def _():
            hand_on()

    if last:

        @pl.loop(0, KV_HEADS // STEP_HEADS)
        def _(step):
            out_copy(step).wait()


def solution(mesh):
    grid = chip_grid(mesh.shape["tp"])
    depth, width, cores = grid
    groups = mesh.shape["groups"]
    assert cores == 2 and depth > 2
    straight = width == 2 and groups % 2 == 0
    assert straight or width == 1

    def body(query_rows, key_rows, value_rows):
        tok, columns = query_rows.shape
        dim = key_rows.shape[1] // KV_HEADS
        rows = GROUP * tok
        query_rows, key_rows, value_rows = (
            pltpu.with_memory_space_constraint(array, pltpu.HBM)
            for array in (query_rows, key_rows, value_rows)
        )
        whole = pl.BlockSpec(memory_space=pltpu.VMEM)
        state_shapes = [
            jax.ShapeDtypeStruct((KV_HEADS, rows, size), jnp.float32) for size in (2 * dim, dim)
        ]
        steps = KV_HEADS // STEP_HEADS

        arrays, found = {}, {}

        def keep(name, array, places):
            arrays[name] = array
            found.update({place: (name, at) for at, place in enumerate(places)})

        def phase(places, state, last=False, after=None):
            names = list(dict.fromkeys(found[place][0] for place in places))
            sources = [
                [(place, found[place][1]) for place in places if found[place][0] == name]
                for name in names
            ]
            operands = [arrays[name] for name in names]
            if after:
                operands, arrays[after] = lax.optimization_barrier((operands, arrays[after]))
            keys = tok * len(places)
            levels = {dz for dz, _, _ in places}
            scratch = []
            if last:
                scratch += [pltpu.VMEM((tok, columns), query_rows.dtype)]
                scratch += [pltpu.SemaphoreType.DMA((steps,))]
            if 0 in levels or len(levels) > 1:
                scratch += [pltpu.VMEM((tok, keys), jnp.float32)]
            return pl.pallas_call(
                functools.partial(attend_kernel, grid, sources, bool(state), last),
                out_shape=query_rows if last else state_shapes,
                in_specs=[whole] * (1 + len(operands) + len(state)),
                out_specs=pl.BlockSpec(memory_space=pltpu.HBM) if last else [whole] * 2,
                scratch_shapes=scratch,
                input_output_aliases={}
                if last or not state
                else {1 + len(operands) + at: at for at in range(2)},
                compiler_params=pltpu.CompilerParams(vmem_limit_bytes=16 * 2**20),
                cost_estimate=pl.CostEstimate(flops=1000, bytes_accessed=1000, transcendentals=0),
                name="attend_last" if last else "attend",
            )(queries, *operands, *state)

        batches = []
        for dz in range(1, depth):
            batches.append([(dz, 0, 0), (dz - 1, 0, 1)])
            if width == 2:
                batches[-1] += [(dz - 1, 1, 0)] + [(dz - 2, 1, 1)] * (dz > 1)
        batches[0].append((0, 0, 0))
        final = [(depth - 1, 0, 1)]
        if straight:
            final += [(depth - 2, 1, 0), (depth - 2, 1, 1), (depth - 1, 1, 1)]
            batches[-1] = [(depth - 1, 1, 0), (depth - 1, 0, 0), (depth - 2, 0, 1), (depth - 3, 1, 1)]
        while len(batches) > 8:
            batches = [sum(batches[at : at + 2], []) for at in range(0, len(batches), 2)]

        keep("z0", stack([key_rows, value_rows], "pack"), [(0, 0, 0)])
        queries = fetch(query_rows)
        state = []
        for dz in range(depth):
            block = arrays[f"z{dz}"]
            if dz + 1 < depth:
                keep(f"z{dz + 1}", z_forward(block, grid, dz + 1), [(dz + 1, 0, 0)])
            if straight and dz + 1 < depth:
                keep(f"y{dz}", y_swap(block, grid), [(dz, 1, 0)])
            if straight and dz == 0:
                keep("w", far_swap(block, grid, groups), [(depth - 1, 1, 0)])
            if straight and dz == depth - 1:
                keep("cw", core_swap(arrays["w"], grid), [(depth - 1, 1, 1)])
            if dz and all(place in found for place in batches[0]):
                state = phase(batches.pop(0), state, after="w" if straight and dz == 1 else None)
            keep(f"c{dz}", core_swap(block, grid), [(dz, 0, 1)])
            if dz and straight:
                keep(f"d{dz}", core_swap(arrays[f"y{dz - 1}"], grid), [(dz - 1, 1, 1)])
            if dz + 1 < depth:
                tied = [f"z{dz + 1}"]
                values, state, queries = lax.optimization_barrier(
                    ([arrays[name] for name in tied], state, queries)
                )
                arrays.update(zip(tied, values))
        return phase(final, state, last=True)

    spec = P(("groups", "tp"), None)
    return jax.shard_map(
        body, mesh=mesh, in_specs=(spec, spec, spec), out_specs=spec, check_vma=False
    )
```

```python
import functools
import math

import jax
import jax.numpy as jnp
from jax import lax
from jax.experimental import pallas as pl
from jax.experimental.pallas import tpu as pltpu
from jax.sharding import PartitionSpec as P

HEADS = 128
KV_HEADS = 8
GROUP = HEADS // KV_HEADS
PARTS = 8
STEP_HEADS = 2

masked_score = -1e30


def chip_grid(devices):
    if devices % 2:
        return devices, 1, 1
    chips = devices // 2
    if chips % 2 or chips > 8:
        return chips, 1, 2
    return chips // 2, 2, 2


def place(grid):
    depth, width, cores = grid
    me = lax.axis_index("tp")
    return me // (width * cores), (me // cores) % width, me % cores


def stack(arrays, name):
    def kernel(*refs):
        for at, ref in enumerate(refs[:-1]):
            refs[-1][at] = ref[...]

    count = len(arrays)
    return pl.pallas_call(
        kernel,
        out_shape=jax.ShapeDtypeStruct((count, *arrays[0].shape), arrays[0].dtype),
        in_specs=[pl.BlockSpec(memory_space=pltpu.VMEM)] * count,
        out_specs=pl.BlockSpec(memory_space=pltpu.VMEM),
        compiler_params=pltpu.CompilerParams(vmem_limit_bytes=4 * 2**20),
        name=name,
    )(*arrays)


def fetch(array):
    def kernel(array_ref, out_ref, sem):
        copy = pltpu.make_async_copy(array_ref, out_ref, sem)
        copy.start()
        copy.wait()

    return pl.pallas_call(
        kernel,
        out_shape=jax.ShapeDtypeStruct(array.shape, array.dtype),
        in_specs=[pl.BlockSpec(memory_space=pltpu.HBM)],
        out_specs=pl.BlockSpec(memory_space=pltpu.VMEM),
        scratch_shapes=[pltpu.SemaphoreType.DMA],
        compiler_params=pltpu.CompilerParams(vmem_limit_bytes=4 * 2**20),
        name="fetch",
    )(array)


def z_forward(block, grid, dz):
    depth, width, cores = grid
    side = width * cores
    pairs = []
    for z in range(depth):
        target = z ^ 1 if dz == depth - 1 and depth % 2 == 0 else (z + 1) % depth
        pairs += [(z * side + at, target * side + at) for at in range(side)]
    return lax.ppermute(block, "tp", pairs)


def y_swap(block, grid):
    depth, width, cores = grid
    return lax.ppermute(
        block, "tp", [(at, at ^ cores) for at in range(depth * width * cores)]
    )


def core_swap(blocks, grid):
    depth, width, cores = grid
    return lax.ppermute(blocks, "tp", [(at, at ^ 1) for at in range(depth * width * cores)])


def reciprocal(x):
    guess = pl.reciprocal(x, approx=True)
    return guess * (2.0 - x * guess)


def attend_kernel(grid, sources, kept, last, query_ref, *refs):
    depth, width, cores = grid
    blocks_refs, refs = refs[: len(sources)], refs[len(sources) :]
    kept_refs, refs = refs[: 2 * kept], refs[2 * kept :]
    out_refs, scratch = list(refs[: 2 - last]), list(refs[2 - last :])
    if last:
        result_ref = out_refs[0]
        out_refs[0], sems = scratch.pop(0), scratch.pop(0)
    tok = query_ref.shape[0]
    dim = blocks_refs[0].shape[-1] // KV_HEADS
    rows = GROUP * tok
    part_rows = rows // PARTS
    heads = part_rows // tok
    factor = dim ** (-0.5) * math.log2(math.e)
    zz, yy, cc = place(grid)

    pieces = []
    for places, ref in zip(sources, blocks_refs):
        for (dz, dy, dc), at in places:
            pieces.append((dz, dc, dy, ref.at[0], ref.at[1]))
    pieces.sort(key=lambda piece: piece[:3])

    if scratch:
        bias_ref = scratch[0]

        row = lax.broadcasted_iota(jnp.int32, (tok, tok), 0)
        key = lax.broadcasted_iota(jnp.int32, (tok, tok), 1)
        for at, (dz, dc, dy, _, _) in enumerate(pieces):
            if dz:
                limit = jnp.where(zz >= dz, 0, tok) + 0 * key
            elif dy:
                limit = jnp.where(yy == 1, 0, tok) + 0 * key
            elif dc:
                limit = jnp.where(cc == 1, 0, tok) + 0 * key
            else:
                limit = key
            bias_ref[:, at * tok : (at + 1) * tok] = jnp.where(limit <= row, 0.0, masked_score)

    def column(index):
        return pl.ds(pl.multiple_of(index * dim, dim), dim)

    def emit(head, part, sums, peak):
        here = slice(part * part_rows, (part + 1) * part_rows)
        if not last:
            out_refs[0][head, here, :] = sums
            out_refs[1][head, here, :] = jnp.broadcast_to(peak, (part_rows, dim))
            return
        result = (sums[:, :dim] * reciprocal(sums[:, dim:])).astype(out_refs[0].dtype)
        for index in range(heads):
            out_refs[0][:, column((head * PARTS + part) * heads + index)] = result[
                index * tok : (index + 1) * tok
            ]

    def attend(used, span):
        def one(head):
            span_of = column(head)
            keys = jnp.concatenate([piece[3][:, span_of] for piece in used], axis=0)
            values = jnp.concatenate([piece[4][:, span_of] for piece in used], axis=0)
            values = jnp.concatenate([values, jnp.ones_like(values)], axis=1)
            first_head = head * GROUP
            for part in range(PARTS):
                here = slice(part * part_rows, (part + 1) * part_rows)
                query = jnp.concatenate(
                    [
                        query_ref[:, column(first_head + index)]
                        for index in range(part * heads, (part + 1) * heads)
                    ],
                    axis=0,
                )
                scores = lax.dot_general(
                    query, keys, (((1,), (1,)), ((), ())), preferred_element_type=jnp.float32
                )
                if span:
                    first = scores[:, :span].reshape(heads, tok, span) + bias_ref[:, :span][None]
                    first = first.reshape(part_rows, span)
                    if span < scores.shape[1]:
                        first = jnp.concatenate([first, scores[:, span:]], axis=1)
                    scores = first
                peak = jnp.max(scores, axis=1, keepdims=True) * factor
                if kept:
                    before = kept_refs[1][head, here, :]
                    peak = jnp.maximum(jnp.broadcast_to(peak, before.shape), before)
                    shifted = jnp.concatenate(
                        [
                            scores[:, at : at + dim] * factor - peak[:, : scores.shape[1] - at]
                            for at in range(0, scores.shape[1], dim)
                        ],
                        axis=1,
                    )
                else:
                    shifted = scores * factor - peak
                weights = jnp.exp2(shifted).astype(jnp.bfloat16)
                sums = jnp.dot(weights, values, preferred_element_type=jnp.float32)
                if kept:
                    carry = jnp.exp2(before - peak)
                    carry = jnp.concatenate([carry, carry], axis=1)
                    sums = sums + carry * kept_refs[0][head, here, :]
                emit(head, part, sums, peak)

        all_heads(one)

    def hand_on():
        def one(head):
            for part in range(PARTS):
                here = slice(part * part_rows, (part + 1) * part_rows)
                emit(head, part, kept_refs[0][head, here, :], kept_refs[1][head, here, :])

        all_heads(one)

    def out_copy(head):
        span = GROUP * dim
        here = pl.ds(pl.multiple_of(head * span, span), span)
        return pltpu.make_async_copy(out_refs[0].at[:, here], result_ref.at[:, here], sems.at[head])

    def all_heads(one):
        @pl.loop(0, KV_HEADS // STEP_HEADS)
        def _(step):
            for index in range(STEP_HEADS):
                head = step * STEP_HEADS + index
                one(head)
                if last:
                    out_copy(head).start()

    near = tok * sum(piece[0] == 0 for piece in pieces)
    near = min(-(-near // dim) * dim, len(pieces) * tok)
    lowest, highest = pieces[0][0], pieces[-1][0]

    @pl.when(zz >= highest)
    def _():
        attend(pieces, near)

    if lowest < highest:

        @pl.when(jnp.logical_and(zz >= lowest, zz < highest))
        def _():
            attend(pieces, len(pieces) * tok)

    if lowest > 0:

        @pl.when(zz < lowest)
        def _():
            hand_on()

    if last:

        @pl.loop(0, KV_HEADS)
        def _(head):
            out_copy(head).wait()


def solution(mesh):
    grid = chip_grid(mesh.shape["tp"])
    depth, width, cores = grid
    assert cores == 2 and depth > 2

    def body(query_rows, key_rows, value_rows):
        tok, columns = query_rows.shape
        dim = key_rows.shape[1] // KV_HEADS
        rows = GROUP * tok
        query_rows, *own = (
            pltpu.with_memory_space_constraint(array, pltpu.HBM)
            for array in (query_rows, key_rows, value_rows)
        )
        whole = pl.BlockSpec(memory_space=pltpu.VMEM)
        state_shapes = [
            jax.ShapeDtypeStruct((KV_HEADS, rows, size), jnp.float32) for size in (2 * dim, dim)
        ]

        arrays, found = {}, {}

        def keep(name, array, places):
            arrays[name] = array
            found.update({place: (name, at) for at, place in enumerate(places)})

        def phase(places, state, last=False):
            names = list(dict.fromkeys(found[place][0] for place in places))
            sources = [
                [(place, found[place][1]) for place in places if found[place][0] == name]
                for name in names
            ]
            operands = [arrays[name] for name in names]
            keys = tok * len(places)
            levels = {dz for dz, _, _ in places}
            scratch = []
            if last:
                scratch += [pltpu.VMEM((tok, columns), query_rows.dtype)]
                scratch += [pltpu.SemaphoreType.DMA((KV_HEADS,))]
            if 0 in levels or len(levels) > 1:
                scratch += [pltpu.VMEM((tok, keys), jnp.float32)]
            return pl.pallas_call(
                functools.partial(attend_kernel, grid, sources, bool(state), last),
                out_shape=query_rows if last else state_shapes,
                in_specs=[whole] * (1 + len(operands) + len(state)),
                out_specs=pl.BlockSpec(memory_space=pltpu.HBM) if last else [whole] * 2,
                scratch_shapes=scratch,
                input_output_aliases={}
                if last or not state
                else {1 + len(operands) + at: at for at in range(2)},
                compiler_params=pltpu.CompilerParams(vmem_limit_bytes=16 * 2**20),
                cost_estimate=pl.CostEstimate(flops=1000, bytes_accessed=1000, transcendentals=0),
                name="attend_last" if last else "attend",
            )(queries, *operands, *state)

        batches = []
        for dz in range(1, depth):
            batches.append([(dz, 0, 0), (dz - 1, 0, 1)])
            if width == 2:
                batches[-1] += [(dz - 1, 1, 0)] + [(dz - 2, 1, 1)] * (dz > 1)
        batches[0].append((0, 0, 0))
        final = [(depth - 1, 0, 1)]
        if width == 2:
            final += [(depth - 1, 1, 0), (depth - 2, 1, 1), (depth - 1, 1, 1)]
        while len(batches) > 8:
            batches = [sum(batches[at : at + 2], []) for at in range(0, len(batches), 2)]

        keep("z0", stack(own, "pack"), [(0, 0, 0)])
        queries = fetch(query_rows)
        state = []
        for dz in range(depth):
            block = arrays[f"z{dz}"]
            if dz == 0:
                parts = [z_forward(array, grid, 1) for array in (key_rows, value_rows)]
            elif dz + 1 < depth:
                keep(f"z{dz + 1}", z_forward(block, grid, dz + 1), [(dz + 1, 0, 0)])
            if width == 2:
                keep(f"y{dz}", y_swap(block, grid), [(dz, 1, 0)])
            if dz and all(place in found for place in batches[0]):
                state = phase(batches.pop(0), state)
            keep(f"c{dz}", core_swap(block, grid), [(dz, 0, 1)])
            if dz and width == 2:
                keep(f"d{dz}", core_swap(arrays[f"y{dz - 1}"], grid), [(dz - 1, 1, 1)])
            if dz == 0:
                parts, state, queries = lax.optimization_barrier((parts, state, queries))
                keep("z1", stack(parts, "pack"), [(1, 0, 0)])
            elif dz + 1 < depth:
                tied = [f"z{dz + 1}"]
                values, state, queries = lax.optimization_barrier(
                    ([arrays[name] for name in tied], state, queries)
                )
                arrays.update(zip(tied, values))
        if width == 2:
            block, state = lax.optimization_barrier((arrays[f"y{depth - 1}"], state))
            arrays[f"y{depth - 1}"] = block
            keep("c", core_swap(block, grid), [(depth - 1, 1, 1)])
        return phase(final, state, last=True)

    spec = P(("groups", "tp"), None)
    return jax.shard_map(
        body, mesh=mesh, in_specs=(spec, spec, spec), out_specs=spec, check_vma=False
    )
```

```python
import functools
import math

import jax
import jax.numpy as jnp
from jax import lax
from jax.experimental import pallas as pl
from jax.experimental.pallas import tpu as pltpu
from jax.sharding import PartitionSpec as P

HEADS = 128
KV_HEADS = 8
GROUP = HEADS // KV_HEADS
PARTS = 8
STEP_HEADS = 2

masked_score = -1e30


def chip_grid(devices):
    if devices % 2:
        return devices, 1, 1
    chips = devices // 2
    if chips % 2 or chips > 8:
        return chips, 1, 2
    return chips // 2, 2, 2


def place(grid):
    depth, width, cores = grid
    me = lax.axis_index("tp")
    return me // (width * cores), (me // cores) % width, me % cores


def stack(arrays, name):
    def kernel(*refs):
        for at, ref in enumerate(refs[:-1]):
            refs[-1][at] = ref[...]

    count = len(arrays)
    return pl.pallas_call(
        kernel,
        out_shape=jax.ShapeDtypeStruct((count, *arrays[0].shape), arrays[0].dtype),
        in_specs=[pl.BlockSpec(memory_space=pltpu.VMEM)] * count,
        out_specs=pl.BlockSpec(memory_space=pltpu.VMEM),
        compiler_params=pltpu.CompilerParams(vmem_limit_bytes=4 * 2**20),
        name=name,
    )(*arrays)


def fetch(array):
    def kernel(array_ref, out_ref, sem):
        copy = pltpu.make_async_copy(array_ref, out_ref, sem)
        copy.start()
        copy.wait()

    return pl.pallas_call(
        kernel,
        out_shape=jax.ShapeDtypeStruct(array.shape, array.dtype),
        in_specs=[pl.BlockSpec(memory_space=pltpu.HBM)],
        out_specs=pl.BlockSpec(memory_space=pltpu.VMEM),
        scratch_shapes=[pltpu.SemaphoreType.DMA],
        compiler_params=pltpu.CompilerParams(vmem_limit_bytes=4 * 2**20),
        name="fetch",
    )(array)


def z_forward(block, grid, dz):
    depth, width, cores = grid
    side = width * cores
    pairs = []
    for z in range(depth):
        target = z ^ 1 if dz == depth - 1 and depth % 2 == 0 else (z + 1) % depth
        pairs += [(z * side + at, target * side + at) for at in range(side)]
    return lax.ppermute(block, "tp", pairs)


def y_swap(block, grid):
    depth, width, cores = grid
    return lax.ppermute(
        block, "tp", [(at, at ^ cores) for at in range(depth * width * cores)]
    )


def core_swap(blocks, grid):
    depth, width, cores = grid
    return lax.ppermute(blocks, "tp", [(at, at ^ 1) for at in range(depth * width * cores)])


def reciprocal(x):
    guess = pl.reciprocal(x, approx=True)
    return guess * (2.0 - x * guess)


def attend_kernel(grid, sources, kept, last, query_ref, *refs):
    depth, width, cores = grid
    blocks_refs, refs = refs[: len(sources)], refs[len(sources) :]
    kept_refs, refs = refs[: 2 * kept], refs[2 * kept :]
    out_refs, scratch = list(refs[: 2 - last]), list(refs[2 - last :])
    if last:
        result_ref = out_refs[0]
        out_refs[0], sems = scratch.pop(0), scratch.pop(0)
    tok = query_ref.shape[0]
    dim = blocks_refs[0].shape[-1] // KV_HEADS
    rows = GROUP * tok
    part_rows = rows // PARTS
    heads = part_rows // tok
    factor = dim ** (-0.5) * math.log2(math.e)
    zz, yy, cc = place(grid)

    pieces = []
    for places, ref in zip(sources, blocks_refs):
        for (dz, dy, dc), at in places:
            pieces.append((dz, dc, dy, ref.at[0], ref.at[1]))
    pieces.sort(key=lambda piece: piece[:3])

    if scratch:
        bias_ref = scratch[0]

        row = lax.broadcasted_iota(jnp.int32, (tok, tok), 0)
        key = lax.broadcasted_iota(jnp.int32, (tok, tok), 1)
        for at, (dz, dc, dy, _, _) in enumerate(pieces):
            if dz:
                limit = jnp.where(zz >= dz, 0, tok) + 0 * key
            elif dy:
                limit = jnp.where(yy == 1, 0, tok) + 0 * key
            elif dc:
                limit = jnp.where(cc == 1, 0, tok) + 0 * key
            else:
                limit = key
            bias_ref[:, at * tok : (at + 1) * tok] = jnp.where(limit <= row, 0.0, masked_score)

    def column(index):
        if isinstance(index, int):
            return pl.ds(index * dim, dim)
        return pl.ds(pl.multiple_of(index * dim, dim), dim)

    def emit(head, part, sums, peak):
        here = slice(part * part_rows, (part + 1) * part_rows)
        if not last:
            out_refs[0][head, here, :] = sums
            out_refs[1][head, here, :] = jnp.broadcast_to(peak, (part_rows, dim))
            return
        result = (sums[:, :dim] * reciprocal(sums[:, dim:])).astype(out_refs[0].dtype)
        for index in range(heads):
            out_refs[0][:, column((head * PARTS + part) * heads + index)] = result[
                index * tok : (index + 1) * tok
            ]

    def attend(used, span):
        def one(head):
            span_of = column(head)
            keys = jnp.concatenate([piece[3][:, span_of] for piece in used], axis=0)
            values = jnp.concatenate([piece[4][:, span_of] for piece in used], axis=0)
            values = jnp.concatenate([values, jnp.ones_like(values)], axis=1)
            first_head = head * GROUP
            for part in range(PARTS):
                here = slice(part * part_rows, (part + 1) * part_rows)
                query = jnp.concatenate(
                    [
                        query_ref[:, column(first_head + index)]
                        for index in range(part * heads, (part + 1) * heads)
                    ],
                    axis=0,
                )
                scores = lax.dot_general(
                    query, keys, (((1,), (1,)), ((), ())), preferred_element_type=jnp.float32
                )
                if span:
                    first = scores[:, :span].reshape(heads, tok, span) + bias_ref[:, :span][None]
                    first = first.reshape(part_rows, span)
                    if span < scores.shape[1]:
                        first = jnp.concatenate([first, scores[:, span:]], axis=1)
                    scores = first
                peak = jnp.max(scores, axis=1, keepdims=True) * factor
                if kept:
                    before = kept_refs[1][head, here, :]
                    peak = jnp.maximum(jnp.broadcast_to(peak, before.shape), before)
                    shifted = jnp.concatenate(
                        [
                            scores[:, at : at + dim] * factor - peak[:, : scores.shape[1] - at]
                            for at in range(0, scores.shape[1], dim)
                        ],
                        axis=1,
                    )
                else:
                    shifted = scores * factor - peak
                weights = jnp.exp2(shifted).astype(jnp.bfloat16)
                sums = jnp.dot(weights, values, preferred_element_type=jnp.float32)
                if kept:
                    carry = jnp.exp2(before - peak)
                    carry = jnp.concatenate([carry, carry], axis=1)
                    sums = sums + carry * kept_refs[0][head, here, :]
                emit(head, part, sums, peak)

        all_heads(one)

    def hand_on():
        def one(head):
            for part in range(PARTS):
                here = slice(part * part_rows, (part + 1) * part_rows)
                emit(head, part, kept_refs[0][head, here, :], kept_refs[1][head, here, :])

        all_heads(one)

    def out_copy(head):
        span = GROUP * dim
        start = head * span if isinstance(head, int) else pl.multiple_of(head * span, span)
        here = pl.ds(start, span)
        return pltpu.make_async_copy(out_refs[0].at[:, here], result_ref.at[:, here], sems.at[head])

    def all_heads(one):
        if last:
            for head in range(KV_HEADS):
                one(head)
                out_copy(head).start()
            return

        @pl.loop(0, KV_HEADS // STEP_HEADS)
        def _(step):
            for index in range(STEP_HEADS):
                one(step * STEP_HEADS + index)

    near = tok * sum(piece[0] == 0 for piece in pieces)
    near = min(-(-near // dim) * dim, len(pieces) * tok)
    lowest, highest = pieces[0][0], pieces[-1][0]

    @pl.when(zz >= highest)
    def _():
        attend(pieces, near)

    if lowest < highest:

        @pl.when(jnp.logical_and(zz >= lowest, zz < highest))
        def _():
            attend(pieces, len(pieces) * tok)

    if lowest > 0:

        @pl.when(zz < lowest)
        def _():
            hand_on()

    if last:

        @pl.loop(0, KV_HEADS)
        def _(head):
            out_copy(head).wait()


def solution(mesh):
    grid = chip_grid(mesh.shape["tp"])
    depth, width, cores = grid
    assert cores == 2 and depth > 2

    def body(query_rows, key_rows, value_rows):
        tok, columns = query_rows.shape
        dim = key_rows.shape[1] // KV_HEADS
        rows = GROUP * tok
        query_rows, *own = (
            pltpu.with_memory_space_constraint(array, pltpu.HBM)
            for array in (query_rows, key_rows, value_rows)
        )
        whole = pl.BlockSpec(memory_space=pltpu.VMEM)
        state_shapes = [
            jax.ShapeDtypeStruct((KV_HEADS, rows, size), jnp.float32) for size in (2 * dim, dim)
        ]

        arrays, found = {}, {}

        def keep(name, array, places):
            arrays[name] = array
            found.update({place: (name, at) for at, place in enumerate(places)})

        def phase(places, state, last=False):
            names = list(dict.fromkeys(found[place][0] for place in places))
            sources = [
                [(place, found[place][1]) for place in places if found[place][0] == name]
                for name in names
            ]
            operands = [arrays[name] for name in names]
            keys = tok * len(places)
            levels = {dz for dz, _, _ in places}
            scratch = []
            if last:
                scratch += [pltpu.VMEM((tok, columns), query_rows.dtype)]
                scratch += [pltpu.SemaphoreType.DMA((KV_HEADS,))]
            if 0 in levels or len(levels) > 1:
                scratch += [pltpu.VMEM((tok, keys), jnp.float32)]
            return pl.pallas_call(
                functools.partial(attend_kernel, grid, sources, bool(state), last),
                out_shape=query_rows if last else state_shapes,
                in_specs=[whole] * (1 + len(operands) + len(state)),
                out_specs=pl.BlockSpec(memory_space=pltpu.HBM) if last else [whole] * 2,
                scratch_shapes=scratch,
                input_output_aliases={}
                if last or not state
                else {1 + len(operands) + at: at for at in range(2)},
                compiler_params=pltpu.CompilerParams(vmem_limit_bytes=16 * 2**20),
                cost_estimate=pl.CostEstimate(flops=1000, bytes_accessed=1000, transcendentals=0),
                name="attend_last" if last else "attend",
            )(queries, *operands, *state)

        batches = []
        for dz in range(1, depth):
            batches.append([(dz, 0, 0), (dz - 1, 0, 1)])
            if width == 2:
                batches[-1] += [(dz - 1, 1, 0)] + [(dz - 2, 1, 1)] * (dz > 1)
        batches[0].append((0, 0, 0))
        final = [(depth - 1, 0, 1)]
        if width == 2:
            final += [(depth - 1, 1, 0), (depth - 2, 1, 1), (depth - 1, 1, 1)]
        while len(batches) > 8:
            batches = [sum(batches[at : at + 2], []) for at in range(0, len(batches), 2)]

        keep("z0", stack(own, "pack"), [(0, 0, 0)])
        queries = fetch(query_rows)
        state = []
        for dz in range(depth):
            block = arrays[f"z{dz}"]
            if dz == 0:
                parts = [z_forward(array, grid, 1) for array in (key_rows, value_rows)]
            elif dz + 1 < depth:
                keep(f"z{dz + 1}", z_forward(block, grid, dz + 1), [(dz + 1, 0, 0)])
            if width == 2:
                keep(f"y{dz}", y_swap(block, grid), [(dz, 1, 0)])
            if dz and all(place in found for place in batches[0]):
                state = phase(batches.pop(0), state)
            keep(f"c{dz}", core_swap(block, grid), [(dz, 0, 1)])
            if dz and width == 2:
                keep(f"d{dz}", core_swap(arrays[f"y{dz - 1}"], grid), [(dz - 1, 1, 1)])
            if dz == 0:
                parts, state, queries = lax.optimization_barrier((parts, state, queries))
                keep("z1", stack(parts, "pack"), [(1, 0, 0)])
            elif dz + 1 < depth:
                tied = [f"z{dz + 1}"]
                values, state, queries = lax.optimization_barrier(
                    ([arrays[name] for name in tied], state, queries)
                )
                arrays.update(zip(tied, values))
        if width == 2:
            block, state = lax.optimization_barrier((arrays[f"y{depth - 1}"], state))
            arrays[f"y{depth - 1}"] = block
            keep("c", core_swap(block, grid), [(depth - 1, 1, 1)])
        return phase(final, state, last=True)

    spec = P(("groups", "tp"), None)
    return jax.shard_map(
        body, mesh=mesh, in_specs=(spec, spec, spec), out_specs=spec, check_vma=False
    )
```

```python
import functools
import math

import jax
import jax.numpy as jnp
from jax import lax
from jax.experimental import pallas as pl
from jax.experimental.pallas import tpu as pltpu
from jax.sharding import PartitionSpec as P

HEADS = 128
KV_HEADS = 8
GROUP = HEADS // KV_HEADS
PARTS = 8
STEP_HEADS = 2

masked_score = -1e30


def chip_grid(devices):
    if devices % 2:
        return devices, 1, 1
    chips = devices // 2
    if chips % 2 or chips > 8:
        return chips, 1, 2
    return chips // 2, 2, 2


def place(grid):
    depth, width, cores = grid
    me = lax.axis_index("tp")
    return me // (width * cores), (me // cores) % width, me % cores


def stack(arrays, name):
    def kernel(*refs):
        for at, ref in enumerate(refs[:-1]):
            refs[-1][at] = ref[...]

    count = len(arrays)
    return pl.pallas_call(
        kernel,
        out_shape=jax.ShapeDtypeStruct((count, *arrays[0].shape), arrays[0].dtype),
        in_specs=[pl.BlockSpec(memory_space=pltpu.VMEM)] * count,
        out_specs=pl.BlockSpec(memory_space=pltpu.VMEM),
        compiler_params=pltpu.CompilerParams(vmem_limit_bytes=4 * 2**20),
        name=name,
    )(*arrays)


def fetch(array):
    def kernel(array_ref, out_ref, sem):
        copy = pltpu.make_async_copy(array_ref, out_ref, sem)
        copy.start()
        copy.wait()

    return pl.pallas_call(
        kernel,
        out_shape=jax.ShapeDtypeStruct(array.shape, array.dtype),
        in_specs=[pl.BlockSpec(memory_space=pltpu.HBM)],
        out_specs=pl.BlockSpec(memory_space=pltpu.VMEM),
        scratch_shapes=[pltpu.SemaphoreType.DMA],
        compiler_params=pltpu.CompilerParams(vmem_limit_bytes=4 * 2**20),
        name="fetch",
    )(array)


def z_forward(block, grid, dz, groups):
    depth, width, cores = grid
    side = width * cores
    count = depth * side
    pairs = []
    for group in range(groups):
        for at in range(count):
            z, place_in = divmod(at, side)
            target_group = group
            if dz == depth - 1 and depth % 2 == 0:
                target = z ^ 1
            elif groups % 2 or z >= dz - 1:
                lowest = 0 if groups % 2 else dz - 1
                target = z + 1 if z + 1 < depth else lowest
            else:
                target, target_group = z, group ^ 1
            pairs.append((group * count + at, target_group * count + target * side + place_in))
    return lax.ppermute(block, ("groups", "tp"), pairs)


def y_swap(block, grid):
    depth, width, cores = grid
    return lax.ppermute(
        block, "tp", [(at, at ^ cores) for at in range(depth * width * cores)]
    )


def core_swap(blocks, grid):
    depth, width, cores = grid
    return lax.ppermute(blocks, "tp", [(at, at ^ 1) for at in range(depth * width * cores)])


def reciprocal(x):
    guess = pl.reciprocal(x, approx=True)
    return guess * (2.0 - x * guess)


def attend_kernel(grid, sources, kept, last, query_ref, *refs):
    depth, width, cores = grid
    blocks_refs, refs = refs[: len(sources)], refs[len(sources) :]
    kept_refs, refs = refs[: 2 * kept], refs[2 * kept :]
    out_refs, scratch = list(refs[: 2 - last]), list(refs[2 - last :])
    if last:
        result_ref = out_refs[0]
        out_refs[0], sems = scratch.pop(0), scratch.pop(0)
    tok = query_ref.shape[0]
    dim = blocks_refs[0].shape[-1] // KV_HEADS
    rows = GROUP * tok
    part_rows = rows // PARTS
    heads = part_rows // tok
    factor = dim ** (-0.5) * math.log2(math.e)
    zz, yy, cc = place(grid)

    pieces = []
    for places, ref in zip(sources, blocks_refs):
        for (dz, dy, dc), at in places:
            pieces.append((dz, dc, dy, ref.at[0], ref.at[1]))
    pieces.sort(key=lambda piece: piece[:3])

    if scratch:
        bias_ref = scratch[0]

        row = lax.broadcasted_iota(jnp.int32, (tok, tok), 0)
        key = lax.broadcasted_iota(jnp.int32, (tok, tok), 1)
        for at, (dz, dc, dy, _, _) in enumerate(pieces):
            if dz:
                limit = jnp.where(zz >= dz, 0, tok) + 0 * key
            elif dy:
                limit = jnp.where(yy == 1, 0, tok) + 0 * key
            elif dc:
                limit = jnp.where(cc == 1, 0, tok) + 0 * key
            else:
                limit = key
            bias_ref[:, at * tok : (at + 1) * tok] = jnp.where(limit <= row, 0.0, masked_score)

    def column(index):
        if isinstance(index, int):
            return pl.ds(index * dim, dim)
        return pl.ds(pl.multiple_of(index * dim, dim), dim)

    def emit(head, part, sums, peak):
        here = slice(part * part_rows, (part + 1) * part_rows)
        if not last:
            out_refs[0][head, here, :] = sums
            out_refs[1][head, here, :] = jnp.broadcast_to(peak, (part_rows, dim))
            return
        result = (sums[:, :dim] * reciprocal(sums[:, dim:])).astype(out_refs[0].dtype)
        for index in range(heads):
            out_refs[0][:, column((head * PARTS + part) * heads + index)] = result[
                index * tok : (index + 1) * tok
            ]

    def attend(used, span):
        def one(head):
            span_of = column(head)
            keys = jnp.concatenate([piece[3][:, span_of] for piece in used], axis=0)
            values = jnp.concatenate([piece[4][:, span_of] for piece in used], axis=0)
            values = jnp.concatenate([values, jnp.ones_like(values)], axis=1)
            first_head = head * GROUP
            for part in range(PARTS):
                here = slice(part * part_rows, (part + 1) * part_rows)
                query = jnp.concatenate(
                    [
                        query_ref[:, column(first_head + index)]
                        for index in range(part * heads, (part + 1) * heads)
                    ],
                    axis=0,
                )
                scores = lax.dot_general(
                    query, keys, (((1,), (1,)), ((), ())), preferred_element_type=jnp.float32
                )
                if span:
                    first = scores[:, :span].reshape(heads, tok, span) + bias_ref[:, :span][None]
                    first = first.reshape(part_rows, span)
                    if span < scores.shape[1]:
                        first = jnp.concatenate([first, scores[:, span:]], axis=1)
                    scores = first
                peak = jnp.max(scores, axis=1, keepdims=True) * factor
                if kept:
                    before = kept_refs[1][head, here, :]
                    peak = jnp.maximum(jnp.broadcast_to(peak, before.shape), before)
                    shifted = jnp.concatenate(
                        [
                            scores[:, at : at + dim] * factor - peak[:, : scores.shape[1] - at]
                            for at in range(0, scores.shape[1], dim)
                        ],
                        axis=1,
                    )
                else:
                    shifted = scores * factor - peak
                weights = jnp.exp2(shifted).astype(jnp.bfloat16)
                sums = jnp.dot(weights, values, preferred_element_type=jnp.float32)
                if kept:
                    carry = jnp.exp2(before - peak)
                    carry = jnp.concatenate([carry, carry], axis=1)
                    sums = sums + carry * kept_refs[0][head, here, :]
                emit(head, part, sums, peak)

        all_heads(one)

    def hand_on():
        def one(head):
            for part in range(PARTS):
                here = slice(part * part_rows, (part + 1) * part_rows)
                emit(head, part, kept_refs[0][head, here, :], kept_refs[1][head, here, :])

        all_heads(one)

    def out_copy(head):
        span = GROUP * dim
        start = head * span if isinstance(head, int) else pl.multiple_of(head * span, span)
        here = pl.ds(start, span)
        return pltpu.make_async_copy(out_refs[0].at[:, here], result_ref.at[:, here], sems.at[head])

    def all_heads(one):
        if last:
            for head in range(KV_HEADS):
                one(head)
                out_copy(head).start()
            return

        @pl.loop(0, KV_HEADS // STEP_HEADS)
        def _(step):
            for index in range(STEP_HEADS):
                one(step * STEP_HEADS + index)

    near = tok * sum(piece[0] == 0 for piece in pieces)
    near = min(-(-near // dim) * dim, len(pieces) * tok)
    lowest, highest = pieces[0][0], pieces[-1][0]

    @pl.when(zz >= highest)
    def _():
        attend(pieces, near)

    if lowest < highest:

        @pl.when(jnp.logical_and(zz >= lowest, zz < highest))
        def _():
            attend(pieces, len(pieces) * tok)

    if lowest > 0:

        @pl.when(zz < lowest)
        def _():
            hand_on()

    if last:

        @pl.loop(0, KV_HEADS)
        def _(head):
            out_copy(head).wait()


def solution(mesh):
    grid = chip_grid(mesh.shape["tp"])
    depth, width, cores = grid
    groups = mesh.shape["groups"]
    assert cores == 2 and depth > 2

    def body(query_rows, key_rows, value_rows):
        tok, columns = query_rows.shape
        dim = key_rows.shape[1] // KV_HEADS
        rows = GROUP * tok
        query_rows, *own = (
            pltpu.with_memory_space_constraint(array, pltpu.HBM)
            for array in (query_rows, key_rows, value_rows)
        )
        whole = pl.BlockSpec(memory_space=pltpu.VMEM)
        state_shapes = [
            jax.ShapeDtypeStruct((KV_HEADS, rows, size), jnp.float32) for size in (2 * dim, dim)
        ]

        arrays, found = {}, {}

        def keep(name, array, places):
            arrays[name] = array
            found.update({place: (name, at) for at, place in enumerate(places)})

        def phase(places, state, last=False):
            names = list(dict.fromkeys(found[place][0] for place in places))
            sources = [
                [(place, found[place][1]) for place in places if found[place][0] == name]
                for name in names
            ]
            operands = [arrays[name] for name in names]
            keys = tok * len(places)
            levels = {dz for dz, _, _ in places}
            scratch = []
            if last:
                scratch += [pltpu.VMEM((tok, columns), query_rows.dtype)]
                scratch += [pltpu.SemaphoreType.DMA((KV_HEADS,))]
            if 0 in levels or len(levels) > 1:
                scratch += [pltpu.VMEM((tok, keys), jnp.float32)]
            return pl.pallas_call(
                functools.partial(attend_kernel, grid, sources, bool(state), last),
                out_shape=query_rows if last else state_shapes,
                in_specs=[whole] * (1 + len(operands) + len(state)),
                out_specs=pl.BlockSpec(memory_space=pltpu.HBM) if last else [whole] * 2,
                scratch_shapes=scratch,
                input_output_aliases={}
                if last or not state
                else {1 + len(operands) + at: at for at in range(2)},
                compiler_params=pltpu.CompilerParams(vmem_limit_bytes=16 * 2**20),
                cost_estimate=pl.CostEstimate(flops=1000, bytes_accessed=1000, transcendentals=0),
                name="attend_last" if last else "attend",
            )(queries, *operands, *state)

        batches = []
        for dz in range(1, depth):
            batches.append([(dz, 0, 0), (dz - 1, 0, 1)])
            if width == 2:
                batches[-1] += [(dz - 1, 1, 0)] + [(dz - 2, 1, 1)] * (dz > 1)
        batches[0].append((0, 0, 0))
        final = [(depth - 1, 0, 1)]
        if width == 2:
            final += [(depth - 1, 1, 0), (depth - 2, 1, 1), (depth - 1, 1, 1)]
        while len(batches) > 8:
            batches = [sum(batches[at : at + 2], []) for at in range(0, len(batches), 2)]

        keep("z0", stack(own, "pack"), [(0, 0, 0)])
        queries = fetch(query_rows)
        state = []
        for dz in range(depth):
            block = arrays[f"z{dz}"]
            if dz == 0:
                parts = [z_forward(array, grid, 1, groups) for array in (key_rows, value_rows)]
            elif dz + 1 < depth:
                keep(f"z{dz + 1}", z_forward(block, grid, dz + 1, groups), [(dz + 1, 0, 0)])
            if width == 2:
                keep(f"y{dz}", y_swap(block, grid), [(dz, 1, 0)])
            if dz and all(place in found for place in batches[0]):
                state = phase(batches.pop(0), state)
            keep(f"c{dz}", core_swap(block, grid), [(dz, 0, 1)])
            if dz and width == 2:
                keep(f"d{dz}", core_swap(arrays[f"y{dz - 1}"], grid), [(dz - 1, 1, 1)])
            if dz == 0:
                parts, state, queries = lax.optimization_barrier((parts, state, queries))
                keep("z1", stack(parts, "pack"), [(1, 0, 0)])
            elif dz + 1 < depth:
                tied = [f"z{dz + 1}"]
                values, state, queries = lax.optimization_barrier(
                    ([arrays[name] for name in tied], state, queries)
                )
                arrays.update(zip(tied, values))
        if width == 2:
            block, state = lax.optimization_barrier((arrays[f"y{depth - 1}"], state))
            arrays[f"y{depth - 1}"] = block
            keep("c", core_swap(block, grid), [(depth - 1, 1, 1)])
        return phase(final, state, last=True)

    spec = P(("groups", "tp"), None)
    return jax.shard_map(
        body, mesh=mesh, in_specs=(spec, spec, spec), out_specs=spec, check_vma=False
    )
```

```python
import functools
import math

import jax
import jax.numpy as jnp
from jax import lax
from jax.experimental import pallas as pl
from jax.experimental.pallas import tpu as pltpu
from jax.sharding import PartitionSpec as P

HEADS = 128
KV_HEADS = 8
GROUP = HEADS // KV_HEADS
PARTS = 8
STEP_HEADS = 2

masked_score = -1e30


def chip_grid(devices):
    if devices % 2:
        return devices, 1, 1
    chips = devices // 2
    if chips % 2 or chips > 8:
        return chips, 1, 2
    return chips // 2, 2, 2


def place(grid):
    depth, width, cores = grid
    me = lax.axis_index("tp")
    return me // (width * cores), (me // cores) % width, me % cores


def stack(arrays, name):
    def kernel(*refs):
        for at, ref in enumerate(refs[:-1]):
            refs[-1][at] = ref[...]

    count = len(arrays)
    return pl.pallas_call(
        kernel,
        out_shape=jax.ShapeDtypeStruct((count, *arrays[0].shape), arrays[0].dtype),
        in_specs=[pl.BlockSpec(memory_space=pltpu.VMEM)] * count,
        out_specs=pl.BlockSpec(memory_space=pltpu.VMEM),
        compiler_params=pltpu.CompilerParams(vmem_limit_bytes=4 * 2**20),
        name=name,
    )(*arrays)


def fetch(array):
    def kernel(array_ref, out_ref, sem):
        copy = pltpu.make_async_copy(array_ref, out_ref, sem)
        copy.start()
        copy.wait()

    return pl.pallas_call(
        kernel,
        out_shape=jax.ShapeDtypeStruct(array.shape, array.dtype),
        in_specs=[pl.BlockSpec(memory_space=pltpu.HBM)],
        out_specs=pl.BlockSpec(memory_space=pltpu.VMEM),
        scratch_shapes=[pltpu.SemaphoreType.DMA],
        compiler_params=pltpu.CompilerParams(vmem_limit_bytes=4 * 2**20),
        name="fetch",
    )(array)


def z_forward(block, grid, dz, groups):
    depth, width, cores = grid
    side = width * cores
    count = depth * side
    pairs = []
    for group in range(groups):
        for at in range(count):
            z, place_in = divmod(at, side)
            target_group = group
            if dz == depth - 1 and depth % 2 == 0:
                target = z ^ 1
            elif groups % 2 or z >= dz - 1:
                lowest = 0 if groups % 2 else dz - 1
                target = z + 1 if z + 1 < depth else lowest
            else:
                target, target_group = z, group ^ 1
            pairs.append((group * count + at, target_group * count + target * side + place_in))
    return lax.ppermute(block, ("groups", "tp"), pairs)


def y_swap(block, grid):
    depth, width, cores = grid
    return lax.ppermute(
        block, "tp", [(at, at ^ cores) for at in range(depth * width * cores)]
    )


def core_swap(blocks, grid):
    depth, width, cores = grid
    return lax.ppermute(blocks, "tp", [(at, at ^ 1) for at in range(depth * width * cores)])


def reciprocal(x):
    guess = pl.reciprocal(x, approx=True)
    return guess * (2.0 - x * guess)


def attend_kernel(grid, sources, kept, last, query_ref, *refs):
    depth, width, cores = grid
    blocks_refs, refs = refs[: len(sources)], refs[len(sources) :]
    kept_refs, refs = refs[: 2 * kept], refs[2 * kept :]
    out_refs, scratch = list(refs[: 2 - last]), list(refs[2 - last :])
    if last:
        result_ref = out_refs[0]
        out_refs[0], sems = scratch.pop(0), scratch.pop(0)
    tok = query_ref.shape[0]
    dim = blocks_refs[0].shape[-1] // KV_HEADS
    rows = GROUP * tok
    part_rows = rows // PARTS
    heads = part_rows // tok
    factor = dim ** (-0.5) * math.log2(math.e)
    zz, yy, cc = place(grid)

    pieces = []
    for places, ref in zip(sources, blocks_refs):
        for (dz, dy, dc), at in places:
            pieces.append((dz, dc, dy, ref.at[0], ref.at[1]))
    pieces.sort(key=lambda piece: piece[:3])

    if scratch:
        bias_ref = scratch[0]

        row = lax.broadcasted_iota(jnp.int32, (tok, tok), 0)
        key = lax.broadcasted_iota(jnp.int32, (tok, tok), 1)
        for at, (dz, dc, dy, _, _) in enumerate(pieces):
            if dz:
                limit = jnp.where(zz >= dz, 0, tok) + 0 * key
            elif dy:
                limit = jnp.where(yy == 1, 0, tok) + 0 * key
            elif dc:
                limit = jnp.where(cc == 1, 0, tok) + 0 * key
            else:
                limit = key
            bias_ref[:, at * tok : (at + 1) * tok] = jnp.where(limit <= row, 0.0, masked_score)

    def column(index):
        if isinstance(index, int):
            return pl.ds(index * dim, dim)
        return pl.ds(pl.multiple_of(index * dim, dim), dim)

    def emit(head, part, sums, peak):
        here = slice(part * part_rows, (part + 1) * part_rows)
        if not last:
            out_refs[0][head, here, :] = sums
            out_refs[1][head, here, :] = jnp.broadcast_to(peak, (part_rows, dim))
            return
        result = (sums[:, :dim] * reciprocal(sums[:, dim:])).astype(out_refs[0].dtype)
        for index in range(heads):
            out_refs[0][:, column((head * PARTS + part) * heads + index)] = result[
                index * tok : (index + 1) * tok
            ]

    def attend(used, span):
        def one(head):
            span_of = column(head)
            keys = jnp.concatenate([piece[3][:, span_of] for piece in used], axis=0)
            values = jnp.concatenate([piece[4][:, span_of] for piece in used], axis=0)
            values = jnp.concatenate([values, jnp.ones_like(values)], axis=1)
            first_head = head * GROUP
            for part in range(PARTS):
                here = slice(part * part_rows, (part + 1) * part_rows)
                query = jnp.concatenate(
                    [
                        query_ref[:, column(first_head + index)]
                        for index in range(part * heads, (part + 1) * heads)
                    ],
                    axis=0,
                )
                scores = lax.dot_general(
                    query, keys, (((1,), (1,)), ((), ())), preferred_element_type=jnp.float32
                )
                if span:
                    first = scores[:, :span].reshape(heads, tok, span) + bias_ref[:, :span][None]
                    first = first.reshape(part_rows, span)
                    if span < scores.shape[1]:
                        first = jnp.concatenate([first, scores[:, span:]], axis=1)
                    scores = first
                peak = jnp.max(scores, axis=1, keepdims=True) * factor
                if kept:
                    before = kept_refs[1][head, here, :]
                    peak = jnp.maximum(jnp.broadcast_to(peak, before.shape), before)
                    shifted = jnp.concatenate(
                        [
                            scores[:, at : at + dim] * factor - peak[:, : scores.shape[1] - at]
                            for at in range(0, scores.shape[1], dim)
                        ],
                        axis=1,
                    )
                else:
                    shifted = scores * factor - peak
                weights = jnp.exp2(shifted).astype(jnp.bfloat16)
                sums = jnp.dot(weights, values, preferred_element_type=jnp.float32)
                if kept:
                    carry = jnp.exp2(before - peak)
                    carry = jnp.concatenate([carry, carry], axis=1)
                    sums = sums + carry * kept_refs[0][head, here, :]
                emit(head, part, sums, peak)

        all_heads(one)

    def hand_on():
        def one(head):
            for part in range(PARTS):
                here = slice(part * part_rows, (part + 1) * part_rows)
                emit(head, part, kept_refs[0][head, here, :], kept_refs[1][head, here, :])

        all_heads(one)

    def out_copy(head):
        span = GROUP * dim
        start = head * span if isinstance(head, int) else pl.multiple_of(head * span, span)
        here = pl.ds(start, span)
        return pltpu.make_async_copy(out_refs[0].at[:, here], result_ref.at[:, here], sems.at[head])

    def all_heads(one):
        if last:
            for head in range(KV_HEADS):
                one(head)
                out_copy(head).start()
            return

        @pl.loop(0, KV_HEADS // STEP_HEADS)
        def _(step):
            for index in range(STEP_HEADS):
                one(step * STEP_HEADS + index)

    near = tok * sum(piece[0] == 0 for piece in pieces)
    near = min(-(-near // dim) * dim, len(pieces) * tok)
    lowest, highest = pieces[0][0], pieces[-1][0]

    @pl.when(zz >= highest)
    def _():
        attend(pieces, near)

    if lowest < highest:

        @pl.when(jnp.logical_and(zz >= lowest, zz < highest))
        def _():
            attend(pieces, len(pieces) * tok)

    if lowest > 0:

        @pl.when(zz < lowest)
        def _():
            hand_on()

    if last:

        @pl.loop(0, KV_HEADS)
        def _(head):
            out_copy(head).wait()


def solution(mesh):
    grid = chip_grid(mesh.shape["tp"])
    depth, width, cores = grid
    groups = mesh.shape["groups"]
    assert cores == 2 and depth > 2

    def body(query_rows, key_rows, value_rows):
        tok, columns = query_rows.shape
        dim = key_rows.shape[1] // KV_HEADS
        rows = GROUP * tok
        query_rows, *own = (
            pltpu.with_memory_space_constraint(array, pltpu.HBM)
            for array in (query_rows, key_rows, value_rows)
        )
        whole = pl.BlockSpec(memory_space=pltpu.VMEM)
        state_shapes = [
            jax.ShapeDtypeStruct((KV_HEADS, rows, size), jnp.float32) for size in (2 * dim, dim)
        ]

        arrays, found = {}, {}

        def keep(name, array, places):
            arrays[name] = array
            found.update({place: (name, at) for at, place in enumerate(places)})

        def phase(places, state, last=False):
            names = list(dict.fromkeys(found[place][0] for place in places))
            sources = [
                [(place, found[place][1]) for place in places if found[place][0] == name]
                for name in names
            ]
            operands = [arrays[name] for name in names]
            keys = tok * len(places)
            levels = {dz for dz, _, _ in places}
            scratch = []
            if last:
                scratch += [pltpu.VMEM((tok, columns), query_rows.dtype)]
                scratch += [pltpu.SemaphoreType.DMA((KV_HEADS,))]
            if 0 in levels or len(levels) > 1:
                scratch += [pltpu.VMEM((tok, keys), jnp.float32)]
            return pl.pallas_call(
                functools.partial(attend_kernel, grid, sources, bool(state), last),
                out_shape=query_rows if last else state_shapes,
                in_specs=[whole] * (1 + len(operands) + len(state)),
                out_specs=pl.BlockSpec(memory_space=pltpu.HBM) if last else [whole] * 2,
                scratch_shapes=scratch,
                input_output_aliases={}
                if last or not state
                else {1 + len(operands) + at: at for at in range(2)},
                compiler_params=pltpu.CompilerParams(vmem_limit_bytes=16 * 2**20),
                cost_estimate=pl.CostEstimate(flops=1000, bytes_accessed=1000, transcendentals=0),
                name="attend_last" if last else "attend",
            )(queries, *operands, *state)

        batches = []
        for dz in range(1, depth):
            batches.append([(dz, 0, 0), (dz - 1, 0, 1)])
            if width == 2:
                batches[-1] += [(dz - 1, 1, 0)] + [(dz - 2, 1, 1)] * (dz > 1)
        batches[0].append((0, 0, 0))
        final = [(depth - 1, 0, 1)]
        if width == 2:
            final += [(depth - 1, 0, 0), (depth - 1, 1, 0), (depth - 1, 1, 1)]
            batches[-1].remove((depth - 1, 0, 0))
            batches[-1].append((depth - 2, 1, 1))
        while len(batches) > 8:
            batches = [sum(batches[at : at + 2], []) for at in range(0, len(batches), 2)]

        keep("z0", stack(own, "pack"), [(0, 0, 0)])
        queries = fetch(query_rows)
        state = []
        for dz in range(depth):
            block = arrays[f"z{dz}"]
            if dz == 0:
                parts = [z_forward(array, grid, 1, groups) for array in (key_rows, value_rows)]
            elif dz + 1 < depth:
                keep(f"z{dz + 1}", z_forward(block, grid, dz + 1, groups), [(dz + 1, 0, 0)])
            if width == 2:
                keep(f"y{dz}", y_swap(block, grid), [(dz, 1, 0)])
            keep(f"c{dz}", core_swap(block, grid), [(dz, 0, 1)])
            if dz and width == 2:
                swapped = arrays[f"y{dz - 1}"]
                if dz + 1 == depth:
                    swapped, _ = lax.optimization_barrier((swapped, block))
                    swapped = stack([core_swap(swapped[half], grid) for half in range(2)], "pack")
                else:
                    swapped = core_swap(swapped, grid)
                keep(f"d{dz}", swapped, [(dz - 1, 1, 1)])
            if dz and batches and all(place in found for place in batches[0]):
                state = phase(batches.pop(0), state)
            if dz == 0:
                parts, state, queries = lax.optimization_barrier((parts, state, queries))
                keep("z1", stack(parts, "pack"), [(1, 0, 0)])
            elif dz + 1 < depth:
                tied = [f"z{dz + 1}"]
                values, state, queries = lax.optimization_barrier(
                    ([arrays[name] for name in tied], state, queries)
                )
                arrays.update(zip(tied, values))
        if width == 2:
            block, state = lax.optimization_barrier((arrays[f"y{depth - 1}"], state))
            arrays[f"y{depth - 1}"] = block
            keep("c", core_swap(block, grid), [(depth - 1, 1, 1)])
        assert not batches
        return phase(final, state, last=True)

    spec = P(("groups", "tp"), None)
    return jax.shard_map(
        body, mesh=mesh, in_specs=(spec, spec, spec), out_specs=spec, check_vma=False
    )
```

```python
import functools
import math

import jax
import jax.numpy as jnp
from jax import lax
from jax.experimental import pallas as pl
from jax.experimental.pallas import tpu as pltpu
from jax.sharding import PartitionSpec as P

HEADS = 128
KV_HEADS = 8
GROUP = HEADS // KV_HEADS
PARTS = 8
STEP_HEADS = 2

masked_score = -1e30


def chip_grid(devices):
    if devices % 2:
        return devices, 1, 1
    chips = devices // 2
    if chips % 2 or chips > 8:
        return chips, 1, 2
    return chips // 2, 2, 2


def place(grid):
    depth, width, cores = grid
    me = lax.axis_index("tp")
    return me // (width * cores), (me // cores) % width, me % cores


def stack(arrays, name):
    def kernel(*refs):
        for at, ref in enumerate(refs[:-1]):
            refs[-1][at] = ref[...]

    count = len(arrays)
    return pl.pallas_call(
        kernel,
        out_shape=jax.ShapeDtypeStruct((count, *arrays[0].shape), arrays[0].dtype),
        in_specs=[pl.BlockSpec(memory_space=pltpu.VMEM)] * count,
        out_specs=pl.BlockSpec(memory_space=pltpu.VMEM),
        compiler_params=pltpu.CompilerParams(vmem_limit_bytes=4 * 2**20),
        name=name,
    )(*arrays)


def fetch(array):
    def kernel(array_ref, out_ref, sem):
        copy = pltpu.make_async_copy(array_ref, out_ref, sem)
        copy.start()
        copy.wait()

    return pl.pallas_call(
        kernel,
        out_shape=jax.ShapeDtypeStruct(array.shape, array.dtype),
        in_specs=[pl.BlockSpec(memory_space=pltpu.HBM)],
        out_specs=pl.BlockSpec(memory_space=pltpu.VMEM),
        scratch_shapes=[pltpu.SemaphoreType.DMA],
        compiler_params=pltpu.CompilerParams(vmem_limit_bytes=4 * 2**20),
        name="fetch",
    )(array)


def z_forward(block, grid, dz, groups):
    depth, width, cores = grid
    side = width * cores
    count = depth * side
    pairs = []
    for group in range(groups):
        for at in range(count):
            z, place_in = divmod(at, side)
            target_group = group
            if dz == depth - 1 and depth % 2 == 0:
                target = z ^ 1
            elif groups % 2 or z >= dz - 1:
                lowest = 0 if groups % 2 else dz - 1
                target = z + 1 if z + 1 < depth else lowest
            else:
                target, target_group = z, group ^ 1
            pairs.append((group * count + at, target_group * count + target * side + place_in))
    return lax.ppermute(block, ("groups", "tp"), pairs)


def y_swap(block, grid, dz):
    depth, width, cores = grid
    pairs = []
    for at in range(depth * width * cores):
        served = at // (width * cores) >= dz
        pairs.append((at, at ^ cores if served else at ^ 1))
    return lax.ppermute(block, "tp", pairs)


def core_swap(blocks, grid):
    depth, width, cores = grid
    return lax.ppermute(blocks, "tp", [(at, at ^ 1) for at in range(depth * width * cores)])


def reciprocal(x):
    guess = pl.reciprocal(x, approx=True)
    return guess * (2.0 - x * guess)


def attend_kernel(grid, sources, kept, last, query_ref, *refs):
    depth, width, cores = grid
    blocks_refs, refs = refs[: len(sources)], refs[len(sources) :]
    kept_refs, refs = refs[: 2 * kept], refs[2 * kept :]
    out_refs, scratch = list(refs[: 2 - last]), list(refs[2 - last :])
    if last:
        result_ref = out_refs[0]
        out_refs[0], sems = scratch.pop(0), scratch.pop(0)
    tok = query_ref.shape[0]
    dim = blocks_refs[0].shape[-1] // KV_HEADS
    rows = GROUP * tok
    part_rows = rows // PARTS
    heads = part_rows // tok
    factor = dim ** (-0.5) * math.log2(math.e)
    zz, yy, cc = place(grid)

    pieces = []
    for places, ref in zip(sources, blocks_refs):
        for (dz, dy, dc), at in places:
            pieces.append((dz, dc, dy, ref.at[0], ref.at[1]))
    pieces.sort(key=lambda piece: piece[:3])

    if scratch:
        bias_ref = scratch[0]

        row = lax.broadcasted_iota(jnp.int32, (tok, tok), 0)
        key = lax.broadcasted_iota(jnp.int32, (tok, tok), 1)
        for at, (dz, dc, dy, _, _) in enumerate(pieces):
            if dz:
                limit = jnp.where(zz >= dz, 0, tok) + 0 * key
            elif dy:
                limit = jnp.where(yy == 1, 0, tok) + 0 * key
            elif dc:
                limit = jnp.where(cc == 1, 0, tok) + 0 * key
            else:
                limit = key
            bias_ref[:, at * tok : (at + 1) * tok] = jnp.where(limit <= row, 0.0, masked_score)

    def column(index):
        if isinstance(index, int):
            return pl.ds(index * dim, dim)
        return pl.ds(pl.multiple_of(index * dim, dim), dim)

    def emit(head, part, sums, peak):
        here = slice(part * part_rows, (part + 1) * part_rows)
        if not last:
            out_refs[0][head, here, :] = sums
            out_refs[1][head, here, :] = jnp.broadcast_to(peak, (part_rows, dim))
            return
        result = (sums[:, :dim] * reciprocal(sums[:, dim:])).astype(out_refs[0].dtype)
        for index in range(heads):
            out_refs[0][:, column((head * PARTS + part) * heads + index)] = result[
                index * tok : (index + 1) * tok
            ]

    def attend(used, span):
        def one(head):
            span_of = column(head)
            keys = jnp.concatenate([piece[3][:, span_of] for piece in used], axis=0)
            values = jnp.concatenate([piece[4][:, span_of] for piece in used], axis=0)
            values = jnp.concatenate([values, jnp.ones_like(values)], axis=1)
            first_head = head * GROUP
            for part in range(PARTS):
                here = slice(part * part_rows, (part + 1) * part_rows)
                query = jnp.concatenate(
                    [
                        query_ref[:, column(first_head + index)]
                        for index in range(part * heads, (part + 1) * heads)
                    ],
                    axis=0,
                )
                scores = lax.dot_general(
                    query, keys, (((1,), (1,)), ((), ())), preferred_element_type=jnp.float32
                )
                if span:
                    first = scores[:, :span].reshape(heads, tok, span) + bias_ref[:, :span][None]
                    first = first.reshape(part_rows, span)
                    if span < scores.shape[1]:
                        first = jnp.concatenate([first, scores[:, span:]], axis=1)
                    scores = first
                peak = jnp.max(scores, axis=1, keepdims=True) * factor
                if kept:
                    before = kept_refs[1][head, here, :]
                    peak = jnp.maximum(jnp.broadcast_to(peak, before.shape), before)
                    shifted = jnp.concatenate(
                        [
                            scores[:, at : at + dim] * factor - peak[:, : scores.shape[1] - at]
                            for at in range(0, scores.shape[1], dim)
                        ],
                        axis=1,
                    )
                else:
                    shifted = scores * factor - peak
                weights = jnp.exp2(shifted).astype(jnp.bfloat16)
                sums = jnp.dot(weights, values, preferred_element_type=jnp.float32)
                if kept:
                    carry = jnp.exp2(before - peak)
                    carry = jnp.concatenate([carry, carry], axis=1)
                    sums = sums + carry * kept_refs[0][head, here, :]
                emit(head, part, sums, peak)

        all_heads(one)

    def hand_on():
        def one(head):
            for part in range(PARTS):
                here = slice(part * part_rows, (part + 1) * part_rows)
                emit(head, part, kept_refs[0][head, here, :], kept_refs[1][head, here, :])

        all_heads(one)

    def out_copy(head):
        span = GROUP * dim
        start = head * span if isinstance(head, int) else pl.multiple_of(head * span, span)
        here = pl.ds(start, span)
        return pltpu.make_async_copy(out_refs[0].at[:, here], result_ref.at[:, here], sems.at[head])

    def all_heads(one):
        if last:
            for head in range(KV_HEADS):
                one(head)
                out_copy(head).start()
            return

        @pl.loop(0, KV_HEADS // STEP_HEADS)
        def _(step):
            for index in range(STEP_HEADS):
                one(step * STEP_HEADS + index)

    near = tok * sum(piece[0] == 0 for piece in pieces)
    near = min(-(-near // dim) * dim, len(pieces) * tok)
    lowest, highest = pieces[0][0], pieces[-1][0]

    @pl.when(zz >= highest)
    def _():
        attend(pieces, near)

    if lowest < highest:

        @pl.when(jnp.logical_and(zz >= lowest, zz < highest))
        def _():
            attend(pieces, len(pieces) * tok)

    if lowest > 0:

        @pl.when(zz < lowest)
        def _():
            hand_on()

    if last:

        @pl.loop(0, KV_HEADS)
        def _(head):
            out_copy(head).wait()


def solution(mesh):
    grid = chip_grid(mesh.shape["tp"])
    depth, width, cores = grid
    groups = mesh.shape["groups"]
    assert cores == 2 and depth > 2

    def body(query_rows, key_rows, value_rows):
        tok, columns = query_rows.shape
        dim = key_rows.shape[1] // KV_HEADS
        rows = GROUP * tok
        query_rows, *own = (
            pltpu.with_memory_space_constraint(array, pltpu.HBM)
            for array in (query_rows, key_rows, value_rows)
        )
        whole = pl.BlockSpec(memory_space=pltpu.VMEM)
        state_shapes = [
            jax.ShapeDtypeStruct((KV_HEADS, rows, size), jnp.float32) for size in (2 * dim, dim)
        ]

        arrays, found = {}, {}

        def keep(name, array, places):
            arrays[name] = array
            found.update({place: (name, at) for at, place in enumerate(places)})

        def phase(places, state, last=False):
            names = list(dict.fromkeys(found[place][0] for place in places))
            sources = [
                [(place, found[place][1]) for place in places if found[place][0] == name]
                for name in names
            ]
            operands = [arrays[name] for name in names]
            keys = tok * len(places)
            levels = {dz for dz, _, _ in places}
            scratch = []
            if last:
                scratch += [pltpu.VMEM((tok, columns), query_rows.dtype)]
                scratch += [pltpu.SemaphoreType.DMA((KV_HEADS,))]
            if 0 in levels or len(levels) > 1:
                scratch += [pltpu.VMEM((tok, keys), jnp.float32)]
            return pl.pallas_call(
                functools.partial(attend_kernel, grid, sources, bool(state), last),
                out_shape=query_rows if last else state_shapes,
                in_specs=[whole] * (1 + len(operands) + len(state)),
                out_specs=pl.BlockSpec(memory_space=pltpu.HBM) if last else [whole] * 2,
                scratch_shapes=scratch,
                input_output_aliases={}
                if last or not state
                else {1 + len(operands) + at: at for at in range(2)},
                compiler_params=pltpu.CompilerParams(vmem_limit_bytes=16 * 2**20),
                cost_estimate=pl.CostEstimate(flops=1000, bytes_accessed=1000, transcendentals=0),
                name="attend_last" if last else "attend",
            )(queries, *operands, *state)

        batches = []
        for dz in range(1, depth):
            batches.append([(dz, 0, 0), (dz - 1, 0, 1)])
            if width == 2:
                batches[-1] += [(dz - 1, 1, 0)] + [(dz - 2, 1, 1)] * (dz > 1)
        batches[0].append((0, 0, 0))
        final = [(depth - 1, 0, 1)]
        if width == 2:
            final += [(depth - 1, 0, 0), (depth - 1, 1, 0), (depth - 1, 1, 1)]
            batches[-1].remove((depth - 1, 0, 0))
            batches[-1].append((depth - 2, 1, 1))
        while len(batches) > 8:
            batches = [sum(batches[at : at + 2], []) for at in range(0, len(batches), 2)]

        keep("z0", stack(own, "pack"), [(0, 0, 0)])
        queries = fetch(query_rows)
        state = []
        for dz in range(depth):
            block = arrays[f"z{dz}"]
            if dz == 0:
                parts = [z_forward(array, grid, 1, groups) for array in (key_rows, value_rows)]
            elif dz + 1 < depth:
                keep(f"z{dz + 1}", z_forward(block, grid, dz + 1, groups), [(dz + 1, 0, 0)])
            if width == 2:
                keep(f"y{dz}", y_swap(block, grid, dz), [(dz, 1, 0)])
            keep(f"c{dz}", core_swap(block, grid), [(dz, 0, 1)])
            if dz and width == 2:
                swapped = arrays[f"y{dz - 1}"]
                if dz + 1 == depth:
                    swapped, _ = lax.optimization_barrier((swapped, block))
                    swapped = stack([core_swap(swapped[half], grid) for half in range(2)], "pack")
                else:
                    swapped = core_swap(swapped, grid)
                keep(f"d{dz}", swapped, [(dz - 1, 1, 1)])
            if dz and batches and all(place in found for place in batches[0]):
                state = phase(batches.pop(0), state)
            if dz == 0:
                parts, state, queries = lax.optimization_barrier((parts, state, queries))
                keep("z1", stack(parts, "pack"), [(1, 0, 0)])
            elif dz + 1 < depth:
                tied = [f"z{dz + 1}"]
                values, state, queries = lax.optimization_barrier(
                    ([arrays[name] for name in tied], state, queries)
                )
                arrays.update(zip(tied, values))
        if width == 2:
            block, state = lax.optimization_barrier((arrays[f"y{depth - 1}"], state))
            arrays[f"y{depth - 1}"] = block
            keep("c", core_swap(block, grid), [(depth - 1, 1, 1)])
        assert not batches
        return phase(final, state, last=True)

    spec = P(("groups", "tp"), None)
    return jax.shard_map(
        body, mesh=mesh, in_specs=(spec, spec, spec), out_specs=spec, check_vma=False
    )
```
